128 devices in a mesh: section: 8 (over z_lo, x), uly: 4 (over y), blk: 4 (over z_hi, core).
Axes of the slice: x: 4, y: 4, z: 4 (z_hi: 2, z_lo: 2; z = z_hi * 2 + z_lo), core: 2. Of those that a mesh axis runs over, the one named last changes fastest.
Arguments:
- in_flight: bfloat16 [8, 1024, 3072], P('section', ('uly', 'blk')), may hold values from -6 to 6
- entering: bfloat16 [1, 1024, 3072], P(None, ('uly', 'blk')), may hold values from -6 to 6
- patch_ids: int32 [9], replicated, may hold values from 0 to 3
- timestep: int32 [1], replicated, may hold values from 0 to 49
- time_table: float32 [50, 3072], replicated, may hold values from -6 to 6
- mod_weight: bfloat16 [8, 3072, 3, 3072], P('section', None, None, ('uly', 'blk')), may hold values from -0.109375 to 0.109375
- qkv_weight: bfloat16 [8, 3072, 3, 1536], P('section', None, None, 'uly'), may hold values from -0.109375 to 0.109375
- out_weight: bfloat16 [8, 1536, 3072], P('section', ('uly', 'blk')), may hold values from -0.15625 to 0.15625
- stale_cache: bfloat16 [8, 4096, 2, 1536], P('section', 'blk', None, 'uly'), may hold values from -300 to 300
Outputs:
- outputs: bfloat16 [8, 2, 1024, 3072], P('section', None, ('uly', 'blk'))
The draws below stay inside these ranges and needn't reach their ends.
All inputs are finite; a program needn't handle non-finite values.
Results may differ from the reference program's by a relative error of at most 0.015.
Values may be sent and summed in bfloat16 or wider, within the bound.
No kernel may reach another device: no remote copies, remote signals or barrier semaphores. Data moves between devices by JAX's collectives and lax.ppermute only.
A program may use at most 128 MiB of HBM per device.

```python
import jax
import jax.numpy as jnp
from jax import lax

D = 3072
HEADS = 12
HD = 128
PATCHES = 4
MB = 2
STEPS = 50
PATCH_TOK = 1024
SEQ = 4096
N_SECTION = 8


def draw_stale_cache(key, part):
    key = jax.random.fold_in(key, 11)
    shape = (N_SECTION, SEQ, 2, HEADS * HD)
    return jax.random.truncated_normal(key, -6.0, 6.0, shape, jnp.float32).astype(jnp.bfloat16)


def plant(result, stream_key, least, high):
    dims = result.shape
    spot = [jax.random.randint(jax.random.fold_in(stream_key, axis), (), 0, dims[axis]) for axis in range(len(dims))]
    result = result.at[tuple(spot)].set(least)
    longest = dims.index(max(dims))
    spot[longest] = (spot[longest] + 1) % dims[longest]
    return result.at[tuple(spot)].set(high)


def block_scale(stream_key, shape, cuts, smallest, largest):
    loudness = 1.0
    for dim, parts in cuts:
        heights = jax.random.uniform(jax.random.fold_in(jax.random.fold_in(stream_key, 6), dim), (parts,), jnp.float32, smallest / len(cuts), largest / len(cuts))
        loudness = loudness * jnp.repeat(jnp.exp(heights), shape[dim] // parts).reshape((-1,) + (1,) * (len(shape) - 1 - dim))
    return loudness


def gaussian(stream_key, dims, scale, reach, cuts=(), kind=jnp.bfloat16):
    result = scale * jax.random.normal(stream_key, dims, jnp.float32)
    if cuts:
        result = result * block_scale(stream_key, dims, cuts, -0.22, 0.18)
    return jnp.clip(result, -reach, reach).astype(kind)


def setup_inputs(seed: int = 0) -> dict:
    key_of = jax.random.split(jax.random.key(seed), 10)
    return {
        "in_flight": gaussian(key_of[0], (N_SECTION, PATCH_TOK, D), 1.0, 6.0, ((0, 8), (1, 16))),
        "entering": gaussian(key_of[1], (MB - 1, PATCH_TOK, D), 1.0, 6.0, ((1, 16),)),
        "patch_ids": plant(jax.random.randint(key_of[2], (N_SECTION + MB - 1,), 0, PATCHES), jax.random.fold_in(key_of[2], 1), 0, PATCHES - 1).astype(jnp.int32),
        "timestep": jax.random.randint(key_of[3], (1,), 0, STEPS).astype(jnp.int32),
        "time_table": gaussian(key_of[4], (STEPS, D), 1.0, 6.0, (), jnp.float32),
        "mod_weight": gaussian(key_of[5], (N_SECTION, D, 3, D), D ** -0.5, 0.109375, ((0, 8), (3, 16))),
        "qkv_weight": gaussian(key_of[6], (N_SECTION, D, 3, HEADS * HD), D ** -0.5, 0.109375, ((0, 8), (3, 4))),
        "out_weight": gaussian(key_of[7], (N_SECTION, HEADS * HD, D), (HEADS * HD) ** -0.5, 0.15625, ((0, 8), (1, 16))),
        "stale_cache": draw_stale_cache(jax.random.fold_in(key_of[9], 71), 0),
    }


def normalize_heads(values):
    return values * lax.rsqrt(lax.optimization_barrier(jnp.mean(values * values, axis=-1, keepdims=True)) + 1e-06)

def run_block(hidden_in, section_index, patch_index, modulation, qkv_weight, out_weight, stale_cache):
    inputs_f = hidden_in.astype(jnp.float32)
    center = inputs_f - lax.optimization_barrier(jnp.mean(inputs_f, axis=-1, keepdims=True))
    normed = center * lax.rsqrt(lax.optimization_barrier(jnp.mean(center * center, axis=-1, keepdims=True)) + 1e-06)
    modulated = (normed * (1.0 + modulation[1]) + modulation[0]).astype(jnp.bfloat16)
    weight_flat = qkv_weight[section_index].reshape(D, 3 * HEADS * HD)
    projected = jnp.dot(modulated, weight_flat, preferred_element_type=jnp.float32)
    projected = projected.reshape(PATCH_TOK, 3, HEADS, HD)
    queries = normalize_heads(projected[:, 0]).astype(jnp.bfloat16)
    keys_new = normalize_heads(projected[:, 1]).astype(jnp.bfloat16)
    values_new = projected[:, 2].astype(jnp.bfloat16)
    stale = stale_cache[section_index].reshape(SEQ, 2, HEADS, HD)
    all_keys = jnp.concatenate([keys_new, stale[:, 0]], axis=0).astype(jnp.float32)
    all_values = jnp.concatenate([values_new, stale[:, 1]], axis=0).astype(jnp.float32)
    stale_patch = jnp.arange(SEQ, dtype=jnp.int32) // PATCH_TOK
    allowed = jnp.concatenate([jnp.ones((PATCH_TOK,), dtype=bool), stale_patch != patch_index])
    scores = jnp.einsum('qhd,khd->hqk', queries.astype(jnp.float32), all_keys) * HD ** (-0.5)
    scores = jnp.where(allowed[None, None, :], scores, jnp.float32(-1e+30))
    peak = lax.optimization_barrier(jnp.max(scores, axis=-1, keepdims=True))
    weights = jnp.exp(scores - peak)
    total = lax.optimization_barrier(jnp.sum(weights, axis=-1))
    rounded = weights.astype(jnp.bfloat16)
    numer = jnp.einsum('hqk,khd->qhd', rounded.astype(jnp.float32), all_values)
    mixed = numer / jnp.transpose(total)[:, :, None]
    attended = mixed.astype(jnp.bfloat16).reshape(PATCH_TOK, HEADS * HD)
    branch_out = jnp.dot(attended, out_weight[section_index], preferred_element_type=jnp.float32)
    return (inputs_f + modulation[2] * branch_out).astype(jnp.bfloat16)

def reference(in_flight, entering, patch_ids, timestep, time_table, mod_weight, qkv_weight, out_weight, stale_cache):
    steps_range = jnp.arange(STEPS, dtype=jnp.int32)
    time_vector = lax.optimization_barrier(jnp.sum(jnp.where((steps_range == timestep[0])[:, None], time_table, jnp.float32(0.0)), axis=0))
    activated = jax.nn.silu(time_vector).astype(jnp.bfloat16)
    results = []
    for section_index in range(N_SECTION):
        results.append([])
    for tick_index in range(MB):
        for section_index in range(N_SECTION):
            flat_mod = mod_weight[section_index].reshape(D, 3 * D)
            modulation = jnp.dot(activated, flat_mod, preferred_element_type=jnp.float32).reshape(3, D)
            if tick_index == 0:
                block_in = in_flight[section_index]
            elif section_index == 0:
                block_in = entering[tick_index - 1]
            else:
                block_in = results[section_index - 1][tick_index - 1]
            patch_index = patch_ids[tick_index - section_index + N_SECTION - 1]
            results[section_index].append(run_block(block_in, section_index, patch_index, modulation, qkv_weight, out_weight, stale_cache))
    return jnp.stack([jnp.stack(section_rows) for section_rows in results])
```

```python
import functools

import jax
import jax.numpy as jnp
from jax import lax
from jax.experimental import pallas as pl
from jax.experimental.pallas import tpu as pltpu
from jax.sharding import PartitionSpec as P

HD = 128
F32 = jnp.float32
BF16 = jnp.bfloat16
LOG2E = 1.4426950408889634
VMEM_BYTES = 48 * 1024 * 1024
SMEM_SPEC = pl.BlockSpec(memory_space=pltpu.SMEM)
VMEM_SPEC = pl.BlockSpec(memory_space=pltpu.VMEM)


def shift(x, section=0, uly=0, blk=0):
    names = ("section", "uly", "blk")
    moves = (section, uly, blk)
    used = tuple(n for n, m in zip(names, moves) if m)
    sizes = [lax.axis_size(n) for n in used]
    total = 1
    for size in sizes:
        total *= size
    pairs = []
    for source in range(total):
        rest, place = source, []
        for size in reversed(sizes):
            place.insert(0, rest % size)
            rest //= size
        target = 0
        for name, size, at in zip(used, sizes, place):
            move = moves[names.index(name)]
            target = target * size + ((at ^ move) if name == "blk" else (at + move) % size)
        pairs.append((source, target))
    return lax.ppermute(x, used if len(used) > 1 else used[0], pairs)


def params():
    return pltpu.CompilerParams(vmem_limit_bytes=VMEM_BYTES)


def norm_rows(x, mod_ref):
    center = x - jnp.mean(x, axis=-1, keepdims=True)
    normed = center * lax.rsqrt(jnp.mean(center * center, axis=-1, keepdims=True) + 1e-06)
    return (normed * (1.0 + mod_ref[1:2, :]) + mod_ref[0:1, :]).astype(BF16)


def norm_heads(part, heads):
    out = []
    for h in range(heads):
        v = part[:, h * HD : (h + 1) * HD]
        out.append(v * lax.rsqrt(jnp.mean(v * v, axis=-1, keepdims=True) + 1e-06))
    return jnp.concatenate(out, axis=1).astype(BF16)


def project_step(mod_s, w_ref, q_ref, k_ref, v_ref):
    g = pl.program_id(0)
    part = jnp.dot(mod_s[...], w_ref[0], preferred_element_type=F32)
    heads = part.shape[1] // HD

    @pl.when(g == 0)
    def _():
        q_ref[...] = norm_heads(part, heads)

    @pl.when(g == 1)
    def _():
        k_ref[...] = norm_heads(part, heads)

    @pl.when(g == 2)
    def _():
        v_ref[...] = part.astype(BF16)


def qkv_first_kernel(n, sc, x0, x1, x2, x3, mod_ref, w_ref, q_ref, k_ref, v_ref, cols_ref, mod_s):
    u = sc[1]
    rows = x0.shape[0]
    width = cols_ref.shape[1]

    @pl.when(pl.program_id(0) == 0)
    def _():
        for k, ref in enumerate((x0, x1, x2, x3)):
            at = pl.multiple_of(lax.rem(u - k + n, n) * rows, rows)
            mod_s[pl.ds(at, rows), :] = norm_rows(ref[...].astype(F32), mod_ref)
            cols_ref[pl.ds(at, rows), :] = ref[:, pl.ds(pl.multiple_of(u * width, 128), width)]

    project_step(mod_s, w_ref, q_ref, k_ref, v_ref)


def qkv_next_kernel(
    n, sc, y0, y1, y2, y3, enter, mod_ref, w_ref, q_ref, k_ref, v_ref, ret_ref, own_ref, mod_s, x_s
):
    u = sc[1]
    first = sc[0] == 0
    width = y0.shape[1]
    rows = own_ref.shape[0]

    @pl.when(pl.program_id(0) == 0)
    def _():
        for k, ref in enumerate((y0, y1, y2, y3)):
            at = pl.multiple_of(lax.rem(u - k + n, n) * width, 128)
            x_s[:, pl.ds(at, width)] = ref[...]
        mine = pl.ds(pl.multiple_of(u * rows, rows), rows)
        ret_ref[...] = x_s[mine, :]

        @pl.when(first)
        def _():
            x_s[...] = enter[...]

        own_ref[...] = x_s[mine, :]
        for r in range(n):
            mod_s[r * rows : (r + 1) * rows, :] = norm_rows(
                x_s[r * rows : (r + 1) * rows, :].astype(F32), mod_ref
            )

    project_step(mod_s, w_ref, q_ref, k_ref, v_ref)


def fixed(shape):
    return pl.BlockSpec(shape, lambda *g: (0,) * len(shape))


def qkv_first(n, scalars, pieces, modulation, weight):
    rows, width = pieces[0].shape
    cols = weight.shape[2]
    tokens = n * rows
    out = jax.ShapeDtypeStruct((tokens, cols), BF16)
    return pl.pallas_call(
        functools.partial(qkv_first_kernel, n),
        grid=(3,),
        in_specs=[SMEM_SPEC]
        + [fixed((rows, width))] * 4
        + [fixed(modulation.shape), pl.BlockSpec((1, width, cols), lambda g: (g, 0, 0))],
        out_specs=[fixed((tokens, cols))] * 3 + [fixed((tokens, width // n))],
        out_shape=[out] * 3 + [jax.ShapeDtypeStruct((tokens, width // n), BF16)],
        scratch_shapes=[pltpu.VMEM((tokens, width), BF16)],
        compiler_params=params(),
        name="qkv_first",
    )(scalars, *pieces, modulation, weight)


def qkv_next(n, scalars, pieces, enter, modulation, weight):
    tokens, part = pieces[0].shape
    width = part * n
    cols = weight.shape[2]
    rows = tokens // n
    out = jax.ShapeDtypeStruct((tokens, cols), BF16)
    return pl.pallas_call(
        functools.partial(qkv_next_kernel, n),
        grid=(3,),
        in_specs=[SMEM_SPEC]
        + [fixed((tokens, part))] * 4
        + [fixed(enter.shape), fixed(modulation.shape)]
        + [pl.BlockSpec((1, width, cols), lambda g: (g, 0, 0))],
        out_specs=[fixed((tokens, cols))] * 3 + [fixed((rows, width))] * 2,
        out_shape=[out] * 3 + [jax.ShapeDtypeStruct((rows, width), BF16)] * 2,
        scratch_shapes=[pltpu.VMEM((tokens, width), BF16)] * 2,
        compiler_params=params(),
        name="qkv_next",
    )(scalars, *pieces, enter, modulation, weight)


def attend_kernel(packed, sc, patch, q_ref, ko, vo, km, vm, so, sm, *outs):
    b = sc[2]
    p = patch[0]
    heads = q_ref.shape[1] // HD
    rows = q_ref.shape[0]
    rate = HD ** (-0.5) * LOG2E
    lane = lax.broadcasted_iota(jnp.int32, (rows, HD), 1)
    stats = jnp.zeros((rows, HD), F32)
    nt = (((1,), (1,)), ((), ()))
    for h in range(heads):
        at = slice(h * HD, (h + 1) * HD)
        q = q_ref[:, at]
        scores = []
        for keys in (ko[:, at], km[:, at], so[0, :, at], sm[0, :, at]):
            scores.append(lax.dot_general(q, keys, nt, preferred_element_type=F32))
        scores[2] = jnp.where(p == b, -1e30, scores[2])
        scores[3] = jnp.where(p == jnp.bitwise_xor(b, 1), -1e30, scores[3])
        peak = functools.reduce(
            jnp.maximum, [jnp.max(s, axis=-1, keepdims=True) for s in scores]
        )
        total = jnp.zeros((rows, 1), F32)
        numer = jnp.zeros((rows, HD), F32)
        for s, values in zip(scores, (vo[:, at], vm[:, at], so[1, :, at], sm[1, :, at])):
            weights = jnp.exp2((s - peak) * rate)
            total = total + jnp.sum(weights, axis=-1, keepdims=True)
            numer = numer + jnp.dot(weights.astype(BF16), values, preferred_element_type=F32)
        mixed = numer / total
        level = peak * rate + jnp.log2(total)
        if packed:
            outs[0][:, at] = mixed.astype(BF16)
            high = level.astype(BF16).astype(F32)
            middle = (level - high).astype(BF16).astype(F32)
            low = level - high - middle
            for j, part in enumerate((high, middle, low)):
                stats = jnp.where(lane == 3 * h + j, part, stats)
        else:
            outs[0][:, at] = mixed
            stats = jnp.where(lane == h, level, stats)
    if packed:
        outs[0][:, heads * HD :] = stats.astype(BF16)
    else:
        outs[1][...] = stats


def attend(packed, scalars, patch, q, ko, vo, km, vm, so, sm):
    rows, cols = q.shape
    if packed:
        out_shape = [jax.ShapeDtypeStruct((rows, cols + HD), BF16)]
    else:
        out_shape = [jax.ShapeDtypeStruct((rows, cols), F32), jax.ShapeDtypeStruct((rows, HD), F32)]
    return pl.pallas_call(
        functools.partial(attend_kernel, packed),
        in_specs=[SMEM_SPEC] * 2 + [VMEM_SPEC] * 7,
        out_specs=[VMEM_SPEC] * len(out_shape),
        out_shape=out_shape,
        compiler_params=params(),
        name="attend_other" if packed else "attend_own",
    )(scalars, patch, q, ko, vo, km, vm, so, sm)


def merge_kernel(o_ref, level_ref, other_ref, out_ref):
    cols = o_ref.shape[1]
    for h in range(cols // HD):
        at = slice(h * HD, (h + 1) * HD)
        mine = level_ref[:, h : h + 1]
        parts = [
            other_ref[:, cols + 3 * h + j : cols + 3 * h + j + 1].astype(F32) for j in range(3)
        ]
        theirs = parts[0] + parts[1] + parts[2]
        peak = jnp.maximum(mine, theirs)
        a, b = jnp.exp2(mine - peak), jnp.exp2(theirs - peak)
        mixed = (a * o_ref[:, at] + b * other_ref[:, at].astype(F32)) / (a + b)
        out_ref[:, at] = mixed.astype(BF16)


def merge(o, level, other):
    return pl.pallas_call(
        merge_kernel,
        in_specs=[VMEM_SPEC] * 3,
        out_specs=VMEM_SPEC,
        out_shape=jax.ShapeDtypeStruct(o.shape, BF16),
        compiler_params=params(),
        name="merge",
    )(o, level, other)


def place_kernel(n, sc, w_ref, out_ref):
    u, b = sc[1], sc[2]
    rows = w_ref.shape[1]
    for j, flip in enumerate((0, 2, 1, 3)):
        for k in range(n):
            at = lax.rem(u - k + n, n) * 4 + jnp.bitwise_xor(b, flip)
            out_ref[pl.ds(pl.multiple_of(at * rows, rows), rows), :] = w_ref[j * n + k]


def place(n, scalars, pieces):
    count, rows, cols = pieces.shape
    return pl.pallas_call(
        functools.partial(place_kernel, n),
        in_specs=[SMEM_SPEC, VMEM_SPEC],
        out_specs=VMEM_SPEC,
        out_shape=jax.ShapeDtypeStruct((count * rows, cols), BF16),
        compiler_params=params(),
        name="place",
    )(scalars, pieces)


def out_cols_kernel(n, sc, a0, a1, a2, a3, w_ref, x_ref, gate_ref, y_ref):
    u = sc[1]
    depth = a0.shape[1]
    total = None
    for k, ref in enumerate((a0, a1, a2, a3)):
        at = pl.multiple_of(lax.rem(u - k + n, n) * depth, 128)
        part = jnp.dot(ref[...], w_ref[pl.ds(at, depth), :], preferred_element_type=F32)
        total = part if total is None else total + part
    y_ref[...] = (x_ref[...].astype(F32) + gate_ref[...] * total).astype(BF16)


def out_cols(n, scalars, pieces, weight, x, gate):
    return pl.pallas_call(
        functools.partial(out_cols_kernel, n),
        in_specs=[SMEM_SPEC] + [VMEM_SPEC] * 7,
        out_specs=VMEM_SPEC,
        out_shape=jax.ShapeDtypeStruct(x.shape, BF16),
        compiler_params=params(),
        name="out_cols",
    )(scalars, *pieces, weight, x, gate)


def out_last_kernel(n, sc, a0, a1, a2, a3, w_ref, x_ref, mod_ref, before_ref, y_ref):
    u = sc[1]
    depth = a0.shape[1]
    total = None
    for k, ref in enumerate((a0, a1, a2, a3)):
        at = pl.multiple_of(lax.rem(u + k, n) * depth, 128)
        part = jnp.dot(ref[...], w_ref[pl.ds(at, depth), :], preferred_element_type=F32)
        total = part if total is None else total + part
    y_ref[0, 0] = before_ref[...]
    y_ref[0, 1] = (x_ref[...].astype(F32) + mod_ref[2:3, :] * total).astype(BF16)


def out_last(n, scalars, pieces, weight, x, modulation, before):
    rows, width = x.shape
    chunk = width // 4
    return pl.pallas_call(
        functools.partial(out_last_kernel, n),
        grid=(width // chunk,),
        in_specs=[SMEM_SPEC]
        + [fixed(pieces[0].shape)] * 4
        + [pl.BlockSpec((weight.shape[0], chunk), lambda g: (0, g))]
        + [pl.BlockSpec((rows, chunk), lambda g: (0, g))]
        + [pl.BlockSpec((3, chunk), lambda g: (0, g))]
        + [pl.BlockSpec((rows, chunk), lambda g: (0, g))],
        out_specs=pl.BlockSpec((1, 2, rows, chunk), lambda g: (0, 0, 0, g)),
        out_shape=jax.ShapeDtypeStruct((1, 2, rows, width), BF16),
        compiler_params=params(),
        name="out_last",
    )(scalars, *pieces, weight, x, modulation, before)


def per_device(
    in_flight,
    entering,
    patch_ids,
    timestep,
    time_table,
    mod_weight,
    qkv_weight,
    out_weight,
    stale_cache,
):
    s = lax.axis_index("section")
    u = lax.axis_index("uly")
    b = lax.axis_index("blk")
    n = lax.axis_size("uly")
    section_count = lax.axis_size("section")
    rows, width = in_flight.shape[1:]
    part = width // n
    scalars = jnp.stack([s, u, b]).astype(jnp.int32)
    patches = [lax.dynamic_slice(patch_ids, (t + section_count - 1 - s,), (1,)) for t in range(2)]

    x_pieces = [in_flight[0]] + [shift(in_flight[0], uly=k) for k in range(1, n)]
    time_vector = lax.dynamic_index_in_dim(time_table, timestep[0], 0, keepdims=False)
    activated = jax.nn.silu(time_vector).astype(BF16)
    mod_cols = mod_weight.shape[3]
    mod_part = jnp.dot(
        activated, mod_weight[0].reshape(width, 3 * mod_cols), preferred_element_type=F32
    ).reshape(3, mod_cols)
    group = n * lax.axis_size("blk")
    spread = lax.all_to_all(
        jnp.broadcast_to(mod_part[None], (group, 3, mod_cols)), ("uly", "blk"), 0, 0
    )
    modulation = jnp.transpose(spread, (1, 0, 2)).reshape(3, width)

    weight = jnp.transpose(qkv_weight[0], (1, 0, 2))
    stale_own = jnp.transpose(stale_cache[0], (1, 0, 2))
    stale_mate = shift(stale_own, blk=1)

    w_cut = [
        lax.dynamic_slice(out_weight[0], (0, lax.rem(u + k, n) * part), (out_weight.shape[1], part))
        for k in range(n)
    ]
    w_pieces = jnp.stack([shift(w_cut[k], section=1, uly=k) for k in range(n)])
    w_two = jnp.concatenate([w_pieces, shift(w_pieces, blk=2)], axis=0)
    w_four = jnp.concatenate([w_two, shift(w_two, blk=1)], axis=0)
    w_before = place(n, scalars, w_four)

    q, k_new, v_new, cols = qkv_first(n, scalars, x_pieces, modulation, weight)
    cols_before = shift(cols, section=1)
    gate_before = shift(modulation[2:3], section=1)
    gate_part = lax.dynamic_slice(gate_before, (0, u * part), (1, part))
    enter_all = lax.all_gather(entering[0], "uly", axis=0, tiled=True)
    out_rows = lax.all_gather(out_weight[0], ("uly", "blk"), axis=0, tiled=True)

    def attention(q, k_new, v_new, patch):
        q_other = shift(q, blk=2)
        k_mate, v_mate = shift(k_new, blk=1), shift(v_new, blk=1)
        rest = (k_new, v_new, k_mate, v_mate, stale_own, stale_mate)
        o, level = attend(False, scalars, patch, q, *rest)
        (for_other,) = attend(True, scalars, patch, q_other, *rest)
        return merge(o, level, shift(for_other, blk=2))

    attended = attention(q, k_new, v_new, patches[0])
    a_pieces = [shift(attended, section=1, uly=k) for k in range(n)]
    y = out_cols(n, scalars, a_pieces, w_before, cols_before, gate_part)
    y_pieces = [y] + [shift(y, uly=k) for k in range(1, n)]
    q, k_new, v_new, back, x_own = qkv_next(n, scalars, y_pieces, enter_all, modulation, weight)
    before = shift(back, section=-1)
    attended = attention(q, k_new, v_new, patches[1])

    def tokens_of(k):
        return lax.dynamic_slice(attended, (lax.rem(u - k + n, n) * rows, 0), (rows, attended.shape[1]))

    last = [tokens_of(0)] + [shift(tokens_of(k), uly=-k) for k in range(1, n)]
    return out_last(n, scalars, last, out_rows, x_own, modulation, before)


def solution(mesh):
    return jax.shard_map(
        per_device,
        mesh=mesh,
        in_specs=(
            P("section", ("uly", "blk"), None),
            P(None, ("uly", "blk"), None),
            P(),
            P(),
            P(),
            P("section", None, None, ("uly", "blk")),
            P("section", None, None, "uly"),
            P("section", ("uly", "blk"), None),
            P("section", "blk", None, "uly"),
        ),
        out_specs=P("section", None, ("uly", "blk"), None),
        check_vma=False,
    )
```

```python
import functools

import jax
import jax.numpy as jnp
from jax import lax
from jax.experimental import pallas as pl
from jax.experimental.pallas import tpu as pltpu
from jax.sharding import PartitionSpec as P

HD = 128
F32 = jnp.float32
BF16 = jnp.bfloat16
QKV_MIB = 32
LOG2E = 1.4426950408889634
SMEM_SPEC = pl.BlockSpec(memory_space=pltpu.SMEM)
VMEM_SPEC = pl.BlockSpec(memory_space=pltpu.VMEM)
ANY_SPEC = pl.BlockSpec(memory_space=pl.ANY)
HBM_SPEC = pl.BlockSpec(memory_space=pltpu.HBM)


def shift(x, section=0, uly=0, blk=0):
    names = ("section", "uly", "blk")
    moves = (section, uly, blk)
    used = tuple(n for n, m in zip(names, moves) if m)
    sizes = [lax.axis_size(n) for n in used]
    total = 1
    for size in sizes:
        total *= size
    pairs = []
    for source in range(total):
        rest, place = source, []
        for size in reversed(sizes):
            place.insert(0, rest % size)
            rest //= size
        target = 0
        for name, size, at in zip(used, sizes, place):
            move = moves[names.index(name)]
            target = target * size + ((at ^ move) if name == "blk" else (at + move) % size)
        pairs.append((source, target))
    return lax.ppermute(x, used if len(used) > 1 else used[0], pairs)


def params(mib=24):
    return pltpu.CompilerParams(vmem_limit_bytes=mib * 1024 * 1024)


def cost(us):
    return pl.CostEstimate(flops=int(us * 1.1e9), transcendentals=0, bytes_accessed=1024)


def start_all(pairs, sem, first=0):
    copies = [pltpu.make_async_copy(s, d, sem.at[first + i]) for i, (s, d) in enumerate(pairs)]
    for copy in copies:
        copy.start()
    return copies


def wait_all(copies):
    for copy in copies:
        copy.wait()


def modulate_kernel(step, table_ref, w_ref, out_ref, table, w, sem):
    copies = start_all([(table_ref, table), (w_ref, w)], sem)
    copies[0].wait()
    at = lax.broadcasted_iota(jnp.int32, table.shape, 0)
    v = jnp.sum(jnp.where(at == step[0], table[...], 0.0), axis=0, keepdims=True)
    activated = (v / (1.0 + jnp.exp(-v))).astype(BF16)
    wide = jnp.broadcast_to(activated, (8, v.shape[1]))
    count, cols = w.shape[:2]
    parts = []
    copies[1].wait()
    for i in range(count):
        part = lax.dot_general(
            wide, w[i], (((1,), (1,)), ((), ())), preferred_element_type=F32
        )[0:1]
        parts += [part[:, :HD], jnp.concatenate([part[:, HD:], part[:, : 2 * HD - cols]], axis=1)]
    parts += [jnp.zeros((8 - len(parts), HD), F32)]
    out_ref[...] = jnp.concatenate(parts, axis=0)


def modulate(timestep, time_table, mod_weight):
    return pl.pallas_call(
        modulate_kernel,
        in_specs=[SMEM_SPEC, HBM_SPEC, HBM_SPEC],
        out_specs=VMEM_SPEC,
        out_shape=shaped((8, HD), F32),
        scratch_shapes=[
            pltpu.VMEM(time_table.shape, F32),
            pltpu.VMEM(mod_weight.shape, BF16),
            pltpu.SemaphoreType.DMA((2,)),
        ],
        compiler_params=params(),
        cost_estimate=cost(3),
        name="modulate",
    )(timestep, time_table, mod_weight)


def norm_rows(x, shift_vec, scale_vec):
    center = x - jnp.mean(x, axis=-1, keepdims=True)
    normed = center * lax.rsqrt(jnp.mean(center * center, axis=-1, keepdims=True) + 1e-06)
    return (normed * (1.0 + scale_vec) + shift_vec).astype(BF16)


def norm_heads(part, heads):
    out = []
    for h in range(heads):
        v = part[:, h * HD : (h + 1) * HD]
        out.append(v * lax.rsqrt(jnp.mean(v * v, axis=-1, keepdims=True) + 1e-06))
    return jnp.concatenate(out, axis=1).astype(BF16)


def project(mod_s, w_s, w_copies, q_ref, kv_ref):
    for g in range(3):
        w_copies[g].wait()
        part = jnp.dot(mod_s[...], w_s[g], preferred_element_type=F32)
        heads = part.shape[1] // HD
        if g == 0:
            q_ref[...] = norm_heads(part, heads)
        elif g == 1:
            kv_ref[0] = norm_heads(part, heads)
        else:
            kv_ref[1] = part.astype(BF16)


def qkv_first_kernel(
    n, held, sc, x0, x1, x2, x3, m0, m1, m2, m3, w_ref, enter_ref, *refs
):
    q_ref, kv_ref, cols_ref, vectors_ref, gate_ref, out_ref, *scratch = refs[held:]
    x_s, mod_s, w_s, tiles, sem = scratch
    u, b = sc[1], sc[2]
    rows = x0.shape[0]
    width = cols_ref.shape[1]
    blocks = m0.shape[0]
    inner = x0.shape[1] // (n * blocks) - HD
    at = [lax.rem(u - k + n, n) for k in range(n)]
    spots = [pl.ds(pl.multiple_of(i * rows, rows), rows) for i in at]
    x_copies = start_all([(r, x_s.at[i]) for r, i in zip((x0, x1, x2, x3), spots)], sem)
    w_copies = start_all([(w_ref.at[g], w_s.at[g]) for g in range(3)], sem, n)
    e_copy = start_all([(enter_ref, out_ref)], sem, n + 3)
    for i, ref in zip(at, (m0, m1, m2, m3)):
        for j in range(blocks):
            tiles[i * blocks + jnp.bitwise_xor(b, j)] = ref[j]
    for i, ref in enumerate((vectors_ref.at[0:1], vectors_ref.at[1:2], gate_ref)):
        pieces = []
        for j in range(n * blocks):
            pieces += [tiles[j, 2 * i : 2 * i + 1, :], tiles[j, 2 * i + 1 : 2 * i + 2, :inner]]
        ref[...] = jnp.concatenate(pieces, axis=1)
    for copy, i in zip(x_copies, spots):
        copy.wait()
        mod_s[i, :] = norm_rows(x_s[i, :].astype(F32), vectors_ref[0:1, :], vectors_ref[1:2, :])
    cols_ref[...] = x_s[:, pl.ds(pl.multiple_of(u * width, 128), width)]
    project(mod_s, w_s, w_copies, q_ref, kv_ref)
    wait_all(e_copy)


def qkv_next_kernel(
    n, sc, y0, y1, y2, y3, enter, vectors, w_ref,
    q_ref, kv_ref, cols_ref,
    x_s, mod_s, w_s, sem,
):
    u = sc[1]
    first = sc[0] == 0
    width = y0.shape[1]
    rows = x_s.shape[0] // n
    spots = [pl.ds(pl.multiple_of(lax.rem(u - k + n, n) * width, 128), width) for k in range(n)]
    x_copies = [
        pltpu.make_async_copy(r, x_s.at[:, at], sem.at[k])
        for k, (r, at) in enumerate(zip((y0, y1, y2, y3), spots))
    ]
    e_copy = pltpu.make_async_copy(enter, x_s, sem.at[n])

    @pl.when(first)
    def _():
        e_copy.start()

    @pl.when(jnp.logical_not(first))
    def _():
        for copy in x_copies:
            copy.start()

    w_copies = start_all([(w_ref.at[g], w_s.at[g]) for g in range(3)], sem, n + 1)

    @pl.when(first)
    def _():
        e_copy.wait()

    @pl.when(jnp.logical_not(first))
    def _():
        for copy in x_copies:
            copy.wait()

    for r in range(n):
        at = slice(r * rows, (r + 1) * rows)
        mod_s[at, :] = norm_rows(x_s[at, :].astype(F32), vectors[0:1, :], vectors[1:2, :])
    cols_ref[...] = x_s[:, pl.ds(pl.multiple_of(u * width, 128), width)]
    project(mod_s, w_s, w_copies, q_ref, kv_ref)


def shaped(shape, dtype=BF16):
    return jax.ShapeDtypeStruct(shape, dtype)


def qkv_scratch(tokens, weight, sems):
    width = weight.shape[1]
    return [
        pltpu.VMEM((tokens, width), BF16),
        pltpu.VMEM((tokens, width), BF16),
        pltpu.VMEM(weight.shape, BF16),
        pltpu.SemaphoreType.DMA((sems,)),
    ]


def qkv_first(n, scalars, pieces, tiles, weight, entering, hold):
    rows, width = pieces[0].shape
    cols = weight.shape[2]
    tokens = n * rows
    blocks = tiles[0].shape[0]
    scratch = qkv_scratch(tokens, weight, n + 4)
    return pl.pallas_call(
        functools.partial(qkv_first_kernel, n, len(hold)),
        in_specs=[SMEM_SPEC] + [ANY_SPEC] * n + [VMEM_SPEC] * n + [ANY_SPEC] * (2 + len(hold)),
        out_specs=[VMEM_SPEC] * 6,
        out_shape=[
            shaped((tokens, cols)),
            shaped((2, tokens, cols)),
            shaped((tokens, width // n)),
            shaped((2, width), F32),
            shaped((1, width), F32),
            shaped(entering.shape),
        ],
        scratch_shapes=scratch[:3] + [pltpu.VMEM((n * blocks, 8, HD), F32)] + scratch[3:],
        compiler_params=params(QKV_MIB),
        cost_estimate=cost(6),
        name="qkv_first",
    )(scalars, *pieces, *tiles, weight, entering, *hold)


def qkv_next(n, scalars, pieces, enter, vectors, weight):
    tokens, part = pieces[0].shape
    cols = weight.shape[2]
    return pl.pallas_call(
        functools.partial(qkv_next_kernel, n),
        in_specs=[SMEM_SPEC] + [ANY_SPEC] * (n + 1) + [VMEM_SPEC, ANY_SPEC],
        out_specs=[VMEM_SPEC] * 3,
        out_shape=[shaped((tokens, cols)), shaped((2, tokens, cols)), shaped((tokens, part))],
        scratch_shapes=qkv_scratch(tokens, weight, n + 4),
        compiler_params=params(QKV_MIB),
        cost_estimate=cost(6),
        name="qkv_next",
    )(scalars, *pieces, enter, vectors, weight)


def attend_kernel(packed, held, by_rows, n, sc, patch, q_ref, fo, fm, so, sm, *refs):
    refs = refs[held:]
    cut_refs = ()
    if n:
        whole, outs, cut_refs = refs[0], refs[1:-n], refs[-n:]
    else:
        outs = refs
    for k, ref in enumerate(cut_refs):
        rows, part = ref.shape
        if by_rows:
            at = pl.ds(pl.multiple_of(lax.rem(sc[1] - k + n, n) * rows, rows), rows)
            ref[...] = whole[at, :]
        else:
            at = pl.ds(pl.multiple_of(lax.rem(sc[1] + k, n) * part, 128), part)
            ref[...] = whole[:, at]
    b = sc[2]
    p = patch[0]
    heads = q_ref.shape[1] // HD
    rows = q_ref.shape[0]
    rate = HD ** (-0.5) * LOG2E
    lane = lax.broadcasted_iota(jnp.int32, (rows, HD), 1)
    stats = jnp.zeros((rows, HD), F32)
    nt = (((1,), (1,)), ((), ()))
    for h in range(heads):
        at = slice(h * HD, (h + 1) * HD)
        q = q_ref[:, at]
        scores = [
            lax.dot_general(q, keys[0, :, at], nt, preferred_element_type=F32)
            for keys in (fo, fm, so, sm)
        ]
        for j in range(2):
            scores[2 + j] = jnp.where(p == jnp.bitwise_xor(b, j), -1e30, scores[2 + j])
        peak = functools.reduce(
            jnp.maximum, [jnp.max(s, axis=-1, keepdims=True) for s in scores]
        )
        total = jnp.zeros((rows, 1), F32)
        numer = jnp.zeros((rows, HD), F32)
        for s, values in zip(scores, (fo[1, :, at], fm[1, :, at], so[1, :, at], sm[1, :, at])):
            weights = jnp.exp2((s - peak) * rate)
            total = total + jnp.sum(weights, axis=-1, keepdims=True)
            numer = numer + jnp.dot(weights.astype(BF16), values, preferred_element_type=F32)
        mixed = numer / total
        level = peak * rate + jnp.log2(total)
        if packed:
            outs[0][:, at] = mixed.astype(BF16)
            high = level.astype(BF16).astype(F32)
            middle = (level - high).astype(BF16).astype(F32)
            low = level - high - middle
            for j, piece in enumerate((high, middle, low)):
                stats = jnp.where(lane == 3 * h + j, piece, stats)
        else:
            outs[0][:, at] = mixed
            stats = jnp.where(lane == h, level, stats)
    if packed:
        outs[0][:, heads * HD :] = stats.astype(BF16)
    else:
        outs[1][...] = stats


def attend(packed, scalars, patch, q, fo, fm, so, sm, hold=(), whole=None, by_rows=False, n=0):
    rows, cols = q.shape
    if packed:
        out_shape = [shaped((rows, cols + HD))]
    else:
        out_shape = [shaped((rows, cols), F32), shaped((rows, HD), F32)]
    extra = list(hold)
    if n:
        extra.append(whole)
        height, width = whole.shape
        out_shape += [shaped((height // n, width) if by_rows else (height, width // n))] * n
    return pl.pallas_call(
        functools.partial(attend_kernel, packed, len(hold), by_rows, n),
        in_specs=[SMEM_SPEC] * 2
        + [VMEM_SPEC] * 5
        + [ANY_SPEC] * len(hold)
        + [VMEM_SPEC] * (1 if n else 0),
        out_specs=[VMEM_SPEC] * len(out_shape),
        out_shape=out_shape,
        compiler_params=params(),
        cost_estimate=cost(5),
        name="attend_other" if packed else "attend_own",
    )(scalars, patch, q, fo, fm, so, sm, *extra)


def merge_kernel(o_ref, level_ref, other_ref, *refs):
    out_ref = refs[-1]
    cols = o_ref.shape[1]
    for h in range(cols // HD):
        at = slice(h * HD, (h + 1) * HD)
        mine = level_ref[:, h : h + 1]
        parts = [
            other_ref[:, cols + 3 * h + j : cols + 3 * h + j + 1].astype(F32) for j in range(3)
        ]
        theirs = parts[0] + parts[1] + parts[2]
        peak = jnp.maximum(mine, theirs)
        a, b = jnp.exp2(mine - peak), jnp.exp2(theirs - peak)
        mixed = (a * o_ref[:, at] + b * other_ref[:, at].astype(F32)) / (a + b)
        out_ref[:, at] = mixed.astype(BF16)


def merge(o, level, other, hold=()):
    return pl.pallas_call(
        merge_kernel,
        in_specs=[VMEM_SPEC] * 3 + [ANY_SPEC] * len(hold),
        out_specs=VMEM_SPEC,
        out_shape=jax.ShapeDtypeStruct(o.shape, BF16),
        compiler_params=params(),
        name="merge",
    )(o, level, other, *hold)


def place_kernel(n, sc, *refs):
    u, core = sc[1], lax.rem(sc[2], 2)
    mine, mate, out_ref = refs[:n], refs[n : 2 * n], refs[2 * n]
    rows = mine[0].shape[0] // 2
    for k in range(n):
        for ref, flip in ((mine[k], 0), (mate[k], 1)):
            for z in range(2):
                at = lax.rem(u - k + n, n) * 4 + 2 * z + jnp.bitwise_xor(core, flip)
                at = pl.multiple_of(at * rows, rows)
                out_ref[pl.ds(at, rows), :] = ref[z * rows : (z + 1) * rows, :]


def place(n, scalars, mine, mate):
    rows, cols = mine[0].shape
    return pl.pallas_call(
        functools.partial(place_kernel, n),
        in_specs=[SMEM_SPEC] + [VMEM_SPEC] * (2 * n),
        out_specs=VMEM_SPEC,
        out_shape=shaped((2 * n * rows, cols)),
        compiler_params=params(),
        cost_estimate=cost(1.5),
        name="place",
    )(scalars, *mine, *mate)


def out_cols_kernel(n, sc, a0, a1, a2, a3, w_ref, x_ref, gate_ref, y_ref, *part_refs):
    u = sc[1]
    depth = a0.shape[1]
    tokens, width = x_ref.shape
    total = None
    for k, ref in enumerate((a0, a1, a2, a3)):
        at = pl.multiple_of(lax.rem(u - k + n, n) * depth, 128)
        part = jnp.dot(ref[...], w_ref[pl.ds(at, depth), :], preferred_element_type=F32)
        total = part if total is None else total + part
    gate = gate_ref[:, pl.ds(pl.multiple_of(u * width, 128), width)]
    y_ref[...] = (x_ref[...].astype(F32) + gate * total).astype(BF16)
    rows = tokens // n
    for k, ref in enumerate(part_refs):
        at = pl.multiple_of(lax.rem(u - k + n, n) * rows, rows)
        ref[...] = y_ref[pl.ds(at, rows), :]


def out_cols(n, scalars, pieces, weight, x, gate, split):
    tokens, width = x.shape
    outs = [shaped(x.shape)] + [shaped((tokens // n, width))] * (n if split else 0)
    return pl.pallas_call(
        functools.partial(out_cols_kernel, n),
        in_specs=[SMEM_SPEC] + [VMEM_SPEC] * (n + 3),
        out_specs=[VMEM_SPEC] * len(outs),
        out_shape=outs,
        compiler_params=params(),
        cost_estimate=cost(2),
        name="out_cols",
    )(scalars, *pieces, weight, x, gate)


def finish_kernel(n, sc, *refs):
    u = sc[1]
    out_ref = refs[-1]
    width = refs[0].shape[1]
    for t in range(2):
        for k in range(n):
            at = pl.multiple_of(lax.rem(u + k, n) * width, 128)
            out_ref[0, t, :, pl.ds(at, width)] = refs[t * n + k][...]


def finish(n, scalars, parts):
    rows, width = parts[0].shape
    return pl.pallas_call(
        functools.partial(finish_kernel, n),
        in_specs=[SMEM_SPEC] + [VMEM_SPEC] * len(parts),
        out_specs=VMEM_SPEC,
        out_shape=shaped((1, 2, rows, n * width)),
        compiler_params=params(),
        cost_estimate=cost(1.5),
        name="finish",
    )(scalars, *parts)


def per_device(
    in_flight,
    entering,
    patch_ids,
    timestep,
    time_table,
    mod_weight,
    qkv_weight,
    out_weight,
    stale_cache,
):
    s = lax.axis_index("section")
    u = lax.axis_index("uly")
    b = lax.axis_index("blk")
    n = lax.axis_size("uly")
    section_count = lax.axis_size("section")
    rows, width = in_flight.shape[1:]
    part = width // n
    scalars = jnp.stack([s, u, b]).astype(jnp.int32)
    patches = [lax.dynamic_slice(patch_ids, (t + section_count - 1 - s,), (1,)) for t in range(2)]

    x_pieces = [in_flight[0]] + [shift(in_flight[0], uly=k) for k in range(1, n)]
    tile = modulate(timestep, time_table, jnp.transpose(mod_weight[0], (1, 2, 0)))
    tiles = jnp.stack([tile, shift(tile, blk=1)])
    tiles = jnp.concatenate([tiles, shift(tiles, blk=2)])
    tiles = [tiles] + [shift(tiles, uly=k) for k in range(1, n)]

    weight = jnp.transpose(qkv_weight[0], (1, 0, 2))
    stale_own = jnp.transpose(stale_cache[0], (1, 0, 2))
    stale_mate = shift(stale_own, blk=1)
    pair = lax.all_gather(
        out_weight[0], "blk", axis=0, tiled=True, axis_index_groups=[[0, 2], [1, 3]]
    )

    q, fresh, cols, vectors, gate, enter = qkv_first(
        n, scalars, x_pieces, tiles, weight, entering[0], []
    )
    enter_all = lax.all_gather(enter, "uly", axis=0, tiled=True)

    def attention(q, fresh, patch, whole, by_rows):
        q_other = shift(q, blk=2)
        rest = (fresh, shift(fresh, blk=1), stale_own, stale_mate)
        o, level, *cut = attend(
            False, scalars, patch, q, *rest, whole=whole, by_rows=by_rows, n=n
        )
        (for_other,) = attend(True, scalars, patch, q_other, *rest, hold=[level])
        return merge(o, level, shift(for_other, blk=2)), cut

    attended, cut = attention(q, fresh, patches[0], pair, False)
    mine = [cut[0]] + [shift(cut[k], uly=k) for k in range(1, n)]
    w_cols = place(n, scalars, mine, [shift(x, blk=1) for x in mine])
    a_pieces = [attended] + [shift(attended, uly=k) for k in range(1, n)]
    (y_first,) = out_cols(n, scalars, a_pieces, w_cols, cols, gate, False)
    y = shift(y_first, section=1)
    y_pieces = [y] + [shift(y, uly=k) for k in range(1, n)]
    q, fresh, cols = qkv_next(n, scalars, y_pieces, enter_all, vectors, weight)
    attended, parts = attention(q, fresh, patches[1], y_first, True)
    parts = [parts[0]] + [shift(parts[k], uly=-k) for k in range(1, n)]
    a_pieces = [attended] + [shift(attended, uly=k) for k in range(1, n)]
    _, *last = out_cols(n, scalars, a_pieces, w_cols, cols, gate, True)
    last = [last[0]] + [shift(last[k], uly=-k) for k in range(1, n)]
    return finish(n, scalars, parts + last)


def solution(mesh):
    return jax.shard_map(
        per_device,
        mesh=mesh,
        in_specs=(
            P("section", ("uly", "blk"), None),
            P(None, ("uly", "blk"), None),
            P(),
            P(),
            P(),
            P("section", None, None, ("uly", "blk")),
            P("section", None, None, "uly"),
            P("section", ("uly", "blk"), None),
            P("section", "blk", None, "uly"),
        ),
        out_specs=P("section", None, ("uly", "blk"), None),
        check_vma=False,
    )
```

```python
import functools

import jax
import jax.numpy as jnp
from jax import lax
from jax.experimental import pallas as pl
from jax.experimental.pallas import tpu as pltpu
from jax.sharding import PartitionSpec as P

HD = 128
F32 = jnp.float32
BF16 = jnp.bfloat16
QKV_MIB = 58
ATTEND_MIB = 24
LOG2E = 1.4426950408889634
SMEM_SPEC = pl.BlockSpec(memory_space=pltpu.SMEM)
VMEM_SPEC = pl.BlockSpec(memory_space=pltpu.VMEM)
ANY_SPEC = pl.BlockSpec(memory_space=pl.ANY)


def shift(x, section=0, uly=0, blk=0):
    names = ("section", "uly", "blk")
    moves = (section, uly, blk)
    used = tuple(n for n, m in zip(names, moves) if m)
    sizes = [lax.axis_size(n) for n in used]
    total = 1
    for size in sizes:
        total *= size
    pairs = []
    for source in range(total):
        rest, place = source, []
        for size in reversed(sizes):
            place.insert(0, rest % size)
            rest //= size
        target = 0
        for name, size, at in zip(used, sizes, place):
            move = moves[names.index(name)]
            target = target * size + ((at ^ move) if name == "blk" else (at + move) % size)
        pairs.append((source, target))
    return lax.ppermute(x, used if len(used) > 1 else used[0], pairs)


def params(mib=24):
    return pltpu.CompilerParams(vmem_limit_bytes=mib * 1024 * 1024)


def cost(us):
    return pl.CostEstimate(flops=int(us * 1.1e9), transcendentals=0, bytes_accessed=1024)


def start_all(pairs, sem, first=0):
    copies = [pltpu.make_async_copy(s, d, sem.at[first + i]) for i, (s, d) in enumerate(pairs)]
    for copy in copies:
        copy.start()
    return copies


def wait_all(copies):
    for copy in copies:
        copy.wait()


def modulate_kernel(held, step, table_ref, w_ref, *refs):
    out_ref, table, w, sem = refs[held:]
    copies = start_all([(table_ref, table), (w_ref, w)], sem)
    copies[0].wait()
    at = lax.broadcasted_iota(jnp.int32, table.shape, 0)
    v = jnp.sum(jnp.where(at == step[0], table[...], 0.0), axis=0, keepdims=True)
    activated = (v / (1.0 + jnp.exp(-v))).astype(BF16)
    wide = jnp.broadcast_to(activated, (8, v.shape[1]))
    count, cols = w.shape[:2]
    parts = []
    copies[1].wait()
    for i in range(count):
        part = lax.dot_general(
            wide, w[i], (((1,), (1,)), ((), ())), preferred_element_type=F32
        )[0:1]
        parts += [part[:, :HD], jnp.concatenate([part[:, HD:], part[:, : 2 * HD - cols]], axis=1)]
    parts += [jnp.zeros((8 - len(parts), HD), F32)]
    out_ref[...] = jnp.concatenate(parts, axis=0)


def modulate(timestep, time_table, mod_weight, hold):
    return pl.pallas_call(
        functools.partial(modulate_kernel, len(hold)),
        in_specs=[SMEM_SPEC] + [ANY_SPEC] * (2 + len(hold)),
        out_specs=VMEM_SPEC,
        out_shape=shaped((8, HD), F32),
        scratch_shapes=[
            pltpu.VMEM(time_table.shape, F32),
            pltpu.VMEM(mod_weight.shape, BF16),
            pltpu.SemaphoreType.DMA((2,)),
        ],
        compiler_params=params(QKV_MIB),
        cost_estimate=cost(3),
        name="modulate",
    )(timestep, time_table, mod_weight, *hold)


def norm_rows(x, shift_vec, scale_vec):
    center = x - jnp.mean(x, axis=-1, keepdims=True)
    normed = center * lax.rsqrt(jnp.mean(center * center, axis=-1, keepdims=True) + 1e-06)
    return (normed * (1.0 + scale_vec) + shift_vec).astype(BF16)


def norm_heads(part, heads):
    out = []
    for h in range(heads):
        v = part[:, h * HD : (h + 1) * HD]
        out.append(v * lax.rsqrt(jnp.mean(v * v, axis=-1, keepdims=True) + 1e-06))
    return jnp.concatenate(out, axis=1).astype(BF16)


def project(mod_s, w_s, w_copies, q_ref, kv_ref):
    for g in range(3):
        w_copies[g].wait()
        part = jnp.dot(mod_s[...], w_s[g], preferred_element_type=F32)
        heads = part.shape[1] // HD
        if g == 0:
            q_ref[...] = norm_heads(part, heads)
        elif g == 1:
            kv_ref[0] = norm_heads(part, heads)
        else:
            kv_ref[1] = part.astype(BF16)


def qkv_first_kernel(
    n, sc, x0, x1, x2, x3, m0, m1, m2, m3, w_ref,
    q_ref, kv_ref, cols_ref, vectors_ref, gate_ref,
    x_s, mod_s, w_s, tiles, sem,
):
    u, b = sc[1], sc[2]
    rows = x0.shape[0]
    width = cols_ref.shape[1]
    blocks = m0.shape[0]
    inner = x0.shape[1] // (n * blocks) - HD
    at = [lax.rem(u - k + n, n) for k in range(n)]
    spots = [pl.ds(pl.multiple_of(i * rows, rows), rows) for i in at]
    x_copies = start_all([(r, x_s.at[i]) for r, i in zip((x0, x1, x2, x3), spots)], sem)
    w_copies = start_all([(w_ref.at[g], w_s.at[g]) for g in range(3)], sem, n)
    for i, ref in zip(at, (m0, m1, m2, m3)):
        for j in range(blocks):
            tiles[i * blocks + jnp.bitwise_xor(b, j)] = ref[j]
    for i, ref in enumerate((vectors_ref.at[0:1], vectors_ref.at[1:2], gate_ref)):
        pieces = []
        for j in range(n * blocks):
            pieces += [tiles[j, 2 * i : 2 * i + 1, :], tiles[j, 2 * i + 1 : 2 * i + 2, :inner]]
        ref[...] = jnp.concatenate(pieces, axis=1)
    for copy, i in zip(x_copies, spots):
        copy.wait()
        mod_s[i, :] = norm_rows(x_s[i, :].astype(F32), vectors_ref[0:1, :], vectors_ref[1:2, :])
    cols_ref[...] = x_s[:, pl.ds(pl.multiple_of(u * width, 128), width)]
    project(mod_s, w_s, w_copies, q_ref, kv_ref)


def qkv_next_kernel(
    n, sc, y0, y1, y2, y3, vectors, w_ref, q_ref, kv_ref, x_s, mod_s, w_s, sem
):
    u = sc[1]
    width = y0.shape[1]
    rows = x_s.shape[0] // n
    spots = [pl.ds(pl.multiple_of(lax.rem(u - k + n, n) * width, 128), width) for k in range(n)]
    x_copies = start_all([(r, x_s.at[:, at]) for r, at in zip((y0, y1, y2, y3), spots)], sem)
    w_copies = start_all([(w_ref.at[g], w_s.at[g]) for g in range(3)], sem, n)
    wait_all(x_copies)
    for r in range(n):
        at = slice(r * rows, (r + 1) * rows)
        mod_s[at, :] = norm_rows(x_s[at, :].astype(F32), vectors[0:1, :], vectors[1:2, :])
    project(mod_s, w_s, w_copies, q_ref, kv_ref)


def shaped(shape, dtype=BF16):
    return jax.ShapeDtypeStruct(shape, dtype)


def qkv_scratch(tokens, weight, sems):
    width = weight.shape[1]
    return [
        pltpu.VMEM((tokens, width), BF16),
        pltpu.VMEM((tokens, width), BF16),
        pltpu.VMEM(weight.shape, BF16),
        pltpu.SemaphoreType.DMA((sems,)),
    ]


def qkv_first(n, scalars, pieces, tiles, weight):
    rows, width = pieces[0].shape
    cols = weight.shape[2]
    tokens = n * rows
    blocks = tiles[0].shape[0]
    scratch = qkv_scratch(tokens, weight, n + 3)
    return pl.pallas_call(
        functools.partial(qkv_first_kernel, n),
        in_specs=[SMEM_SPEC] + [ANY_SPEC] * n + [VMEM_SPEC] * n + [ANY_SPEC],
        out_specs=[VMEM_SPEC] * 5,
        out_shape=[
            shaped((tokens, cols)),
            shaped((2, tokens, cols)),
            shaped((tokens, width // n)),
            shaped((2, width), F32),
            shaped((1, width), F32),
        ],
        scratch_shapes=scratch[:3] + [pltpu.VMEM((n * blocks, 8, HD), F32)] + scratch[3:],
        compiler_params=params(QKV_MIB),
        cost_estimate=cost(6),
        name="qkv_first",
    )(scalars, *pieces, *tiles, weight)


def qkv_next(n, scalars, pieces, vectors, weight):
    tokens = pieces[0].shape[0]
    cols = weight.shape[2]
    return pl.pallas_call(
        functools.partial(qkv_next_kernel, n),
        in_specs=[SMEM_SPEC] + [ANY_SPEC] * n + [VMEM_SPEC, ANY_SPEC],
        out_specs=[VMEM_SPEC] * 2,
        out_shape=[shaped((tokens, cols)), shaped((2, tokens, cols))],
        scratch_shapes=qkv_scratch(tokens, weight, n + 3),
        compiler_params=params(QKV_MIB),
        cost_estimate=cost(6),
        name="qkv_next",
    )(scalars, *pieces, vectors, weight)


def attend_kernel(packed, held, cuts, n, sc, patch, q_ref, fo, fm, so, sm, *refs):
    refs = refs[held:]
    wholes, refs = refs[: len(cuts)], refs[len(cuts) :]
    outs = refs[: len(refs) - n * len(cuts)]
    for c, by_rows in enumerate(cuts):
        for k in range(n):
            ref = refs[len(outs) + c * n + k]
            rows, part = ref.shape
            if by_rows:
                at = pl.ds(pl.multiple_of(lax.rem(sc[1] - k + n, n) * rows, rows), rows)
                ref[...] = wholes[c][at, :]
            else:
                at = pl.ds(pl.multiple_of(lax.rem(sc[1] + k, n) * part, 128), part)
                ref[...] = wholes[c][:, at]
    b = sc[2]
    p = patch[0]
    heads = q_ref.shape[1] // HD
    rows = q_ref.shape[0]
    rate = HD ** (-0.5) * LOG2E
    lane = lax.broadcasted_iota(jnp.int32, (rows, HD), 1)
    stats = jnp.zeros((rows, HD), F32)
    nt = (((1,), (1,)), ((), ()))
    for h in range(heads):
        at = slice(h * HD, (h + 1) * HD)
        q = q_ref[:, at]
        scores = [
            lax.dot_general(q, keys[0, :, at], nt, preferred_element_type=F32)
            for keys in (fo, fm, so, sm)
        ]
        for j in range(2):
            scores[2 + j] = jnp.where(p == jnp.bitwise_xor(b, j), -1e30, scores[2 + j])
        peak = functools.reduce(
            jnp.maximum, [jnp.max(s, axis=-1, keepdims=True) for s in scores]
        )
        total = jnp.zeros((rows, 1), F32)
        numer = jnp.zeros((rows, HD), F32)
        for s, values in zip(scores, (fo[1, :, at], fm[1, :, at], so[1, :, at], sm[1, :, at])):
            weights = jnp.exp2((s - peak) * rate)
            total = total + jnp.sum(weights, axis=-1, keepdims=True)
            numer = numer + jnp.dot(weights.astype(BF16), values, preferred_element_type=F32)
        mixed = numer / total
        level = peak * rate + jnp.log2(total)
        if packed:
            outs[0][:, at] = mixed.astype(BF16)
            high = level.astype(BF16).astype(F32)
            middle = (level - high).astype(BF16).astype(F32)
            low = level - high - middle
            for j, piece in enumerate((high, middle, low)):
                stats = jnp.where(lane == 3 * h + j, piece, stats)
        else:
            outs[0][:, at] = mixed
            stats = jnp.where(lane == h, level, stats)
    if packed:
        outs[0][:, heads * HD :] = stats.astype(BF16)
    else:
        outs[1][...] = stats


def attend(n, packed, scalars, patch, q, fo, fm, so, sm, hold=(), by_rows=(), by_cols=()):
    rows, cols = q.shape
    if packed:
        out_shape = [shaped((rows, cols + HD))]
    else:
        out_shape = [shaped((rows, cols), F32), shaped((rows, HD), F32)]
    for x in by_rows:
        out_shape += [shaped((x.shape[0] // n, x.shape[1]))] * n
    for x in by_cols:
        out_shape += [shaped((x.shape[0], x.shape[1] // n))] * n
    cuts = [True] * len(by_rows) + [False] * len(by_cols)
    return pl.pallas_call(
        functools.partial(attend_kernel, packed, len(hold), cuts, n),
        in_specs=[SMEM_SPEC] * 2
        + [VMEM_SPEC] * 5
        + [ANY_SPEC] * len(hold)
        + [VMEM_SPEC] * len(cuts),
        out_specs=[VMEM_SPEC] * len(out_shape),
        out_shape=out_shape,
        compiler_params=params(ATTEND_MIB),
        cost_estimate=cost(5),
        name="attend_other" if packed else "attend_own",
    )(scalars, patch, q, fo, fm, so, sm, *hold, *by_rows, *by_cols)


def merge_kernel(o_ref, level_ref, other_ref, *refs):
    out_ref = refs[-1]
    cols = o_ref.shape[1]
    for h in range(cols // HD):
        at = slice(h * HD, (h + 1) * HD)
        mine = level_ref[:, h : h + 1]
        parts = [
            other_ref[:, cols + 3 * h + j : cols + 3 * h + j + 1].astype(F32) for j in range(3)
        ]
        theirs = parts[0] + parts[1] + parts[2]
        peak = jnp.maximum(mine, theirs)
        a, b = jnp.exp2(mine - peak), jnp.exp2(theirs - peak)
        mixed = (a * o_ref[:, at] + b * other_ref[:, at].astype(F32)) / (a + b)
        out_ref[:, at] = mixed.astype(BF16)


def merge(o, level, other, hold=()):
    return pl.pallas_call(
        merge_kernel,
        in_specs=[VMEM_SPEC] * 3 + [ANY_SPEC] * len(hold),
        out_specs=VMEM_SPEC,
        out_shape=jax.ShapeDtypeStruct(o.shape, BF16),
        compiler_params=params(),
        cost_estimate=cost(12),
        name="merge",
    )(o, level, other, *hold)


def place_kernel(n, sc, *refs):
    u, core = sc[1], lax.rem(sc[2], 2)
    mine, mate, out_ref = refs[:n], refs[n : 2 * n], refs[2 * n]
    rows = mine[0].shape[0] // 2
    for k in range(n):
        for ref, flip in ((mine[k], 0), (mate[k], 1)):
            for z in range(2):
                at = lax.rem(u - k + n, n) * 4 + 2 * z + jnp.bitwise_xor(core, flip)
                at = pl.multiple_of(at * rows, rows)
                out_ref[pl.ds(at, rows), :] = ref[z * rows : (z + 1) * rows, :]


def place(n, scalars, mine, mate):
    rows, cols = mine[0].shape
    return pl.pallas_call(
        functools.partial(place_kernel, n),
        in_specs=[SMEM_SPEC] + [VMEM_SPEC] * (2 * n),
        out_specs=VMEM_SPEC,
        out_shape=shaped((2 * n * rows, cols)),
        compiler_params=params(),
        cost_estimate=cost(0.1),
        name="place",
    )(scalars, *mine, *mate)


def out_cols_kernel(n, last, sc, a0, a1, a2, a3, w_ref, x_ref, gate_ref, *refs):
    u = sc[1]
    depth = a0.shape[1]
    tokens, width = x_ref.shape
    rows = tokens // n
    total = None
    for k, ref in enumerate((a0, a1, a2, a3)):
        at = pl.multiple_of(lax.rem(u - k + n, n) * depth, 128)
        part = jnp.dot(ref[...], w_ref[pl.ds(at, depth), :], preferred_element_type=F32)
        total = part if total is None else total + part
    gate = gate_ref[:, pl.ds(pl.multiple_of(u * width, 128), width)]
    y_ref = refs[-1]
    y_ref[...] = (x_ref[...].astype(F32) + gate * total).astype(BF16)
    spots = [pl.ds(pl.multiple_of(lax.rem(u - k + n, n) * rows, rows), rows) for k in range(n)]
    if last:
        for ref, at in zip(refs[:n], spots):
            ref[...] = y_ref[at, :]
    else:
        enter, (next_ref,) = refs[:n], refs[n : n + 1]
        end = sc[0] == sc[3] - 1

        @pl.when(end)
        def _():
            for ref, at in zip(enter, spots):
                next_ref[at, :] = ref[...]

        @pl.when(jnp.logical_not(end))
        def _():
            next_ref[...] = y_ref[...]


def out_cols(n, scalars, pieces, weight, x, gate, enter=()):
    tokens, width = x.shape
    last = not enter
    if last:
        outs, scratch = [shaped((tokens // n, width))] * n, [pltpu.VMEM(x.shape, BF16)]
    else:
        outs, scratch = [shaped(x.shape)] * 2, []
    return pl.pallas_call(
        functools.partial(out_cols_kernel, n, last),
        in_specs=[SMEM_SPEC] + [VMEM_SPEC] * (n + 3 + len(enter)),
        out_specs=[VMEM_SPEC] * len(outs),
        out_shape=outs,
        scratch_shapes=scratch,
        compiler_params=params(),
        cost_estimate=cost(2),
        name="out_cols",
    )(scalars, *pieces, weight, x, gate, *enter)


def finish_kernel(n, sc, *refs):
    u = sc[1]
    out_ref = refs[-1]
    width = refs[0].shape[1]
    for t in range(2):
        for k in range(n):
            at = pl.multiple_of(lax.rem(u + k, n) * width, 128)
            out_ref[0, t, :, pl.ds(at, width)] = refs[t * n + k][...]


def finish(n, scalars, parts):
    rows, width = parts[0].shape
    return pl.pallas_call(
        functools.partial(finish_kernel, n),
        in_specs=[SMEM_SPEC] + [VMEM_SPEC] * len(parts),
        out_specs=VMEM_SPEC,
        out_shape=shaped((1, 2, rows, n * width)),
        compiler_params=params(),
        cost_estimate=cost(1.5),
        name="finish",
    )(scalars, *parts)


def per_device(
    in_flight,
    entering,
    patch_ids,
    timestep,
    time_table,
    mod_weight,
    qkv_weight,
    out_weight,
    stale_cache,
):
    s = lax.axis_index("section")
    u = lax.axis_index("uly")
    b = lax.axis_index("blk")
    n = lax.axis_size("uly")
    section_count = lax.axis_size("section")
    rows, width = in_flight.shape[1:]
    part = width // n
    scalars = jnp.stack([s, u, b, section_count]).astype(jnp.int32)
    patches = [lax.dynamic_slice(patch_ids, (t + section_count - 1 - s,), (1,)) for t in range(2)]

    x_pieces = [in_flight[0]] + [shift(in_flight[0], uly=k) for k in range(1, n)]
    stale_own = jnp.transpose(stale_cache[0], (1, 0, 2))
    stale_mate = shift(stale_own, blk=1)
    tile = modulate(timestep, time_table, jnp.transpose(mod_weight[0], (1, 2, 0)), [stale_mate])
    tiles = jnp.stack([tile, shift(tile, blk=1)])
    tiles = jnp.concatenate([tiles, shift(tiles, blk=2)])
    tiles = [tiles] + [shift(tiles, uly=k) for k in range(1, n)]

    weight = jnp.transpose(qkv_weight[0], (1, 0, 2))
    pair = lax.all_gather(
        out_weight[0], "blk", axis=0, tiled=True, axis_index_groups=[[0, 2], [1, 3]]
    )

    q, fresh, cols, vectors, gate = qkv_first(n, scalars, x_pieces, tiles, weight)

    def attention(q, fresh, patch, cut_own, cut_other):
        q_other = shift(q, blk=2)
        rest = (fresh, shift(fresh, blk=1), stale_own, stale_mate)
        o, level, *own = attend(n, False, scalars, patch, q, *rest, **cut_own)
        for_other, *cut = attend(n, True, scalars, patch, q_other, *rest, hold=[level], **cut_other)
        return o, level, shift(for_other, blk=2), own, cut

    o, level, other, cut, _ = attention(
        q, fresh, patches[0], dict(by_cols=[pair, entering[0]]), {}
    )
    cut, enter = cut[:n], cut[n:]
    enter = [enter[0]] + [shift(enter[k], uly=k) for k in range(1, n)]
    mine = [cut[0]] + [shift(cut[k], uly=k) for k in range(1, n)]
    w_cols = place(n, scalars, mine, [shift(x, blk=1) for x in mine])
    attended = merge(o, level, other)
    a_pieces = [attended] + [shift(attended, uly=k) for k in range(1, n)]
    y, y_first = out_cols(n, scalars, a_pieces, w_cols, cols, gate, enter)
    y = shift(y, section=1)
    y_pieces = [y] + [shift(y, uly=k) for k in range(1, n)]
    q, fresh = qkv_next(n, scalars, y_pieces, vectors, weight)
    o, level, other, parts, _ = attention(
        q, fresh, patches[1], dict(by_rows=[y_first]), {}
    )
    parts = [parts[0]] + [shift(parts[k], uly=-k) for k in range(1, n)]
    attended = merge(o, level, other, hold=parts[1:])
    a_pieces = [attended] + [shift(attended, uly=k) for k in range(1, n)]
    last = out_cols(n, scalars, a_pieces, w_cols, y, gate)
    last = [last[0]] + [shift(last[k], uly=-k) for k in range(1, n)]
    return finish(n, scalars, parts + last)


def solution(mesh):
    return jax.shard_map(
        per_device,
        mesh=mesh,
        in_specs=(
            P("section", ("uly", "blk"), None),
            P(None, ("uly", "blk"), None),
            P(),
            P(),
            P(),
            P("section", None, None, ("uly", "blk")),
            P("section", None, None, "uly"),
            P("section", ("uly", "blk"), None),
            P("section", "blk", None, "uly"),
        ),
        out_specs=P("section", None, ("uly", "blk"), None),
        check_vma=False,
    )
```

```python
import functools

import jax
import jax.numpy as jnp
from jax import lax
from jax.experimental import pallas as pl
from jax.experimental.pallas import tpu as pltpu
from jax.sharding import PartitionSpec as P

HD = 128
F32 = jnp.float32
BF16 = jnp.bfloat16
QKV_MIB = 58
ATTEND_MIB = 24
LOG2E = 1.4426950408889634
SMEM_SPEC = pl.BlockSpec(memory_space=pltpu.SMEM)
VMEM_SPEC = pl.BlockSpec(memory_space=pltpu.VMEM)
ANY_SPEC = pl.BlockSpec(memory_space=pl.ANY)


def shift(x, section=0, uly=0, blk=0):
    names = ("section", "uly", "blk")
    moves = (section, uly, blk)
    used = tuple(n for n, m in zip(names, moves) if m)
    sizes = [lax.axis_size(n) for n in used]
    total = 1
    for size in sizes:
        total *= size
    pairs = []
    for source in range(total):
        rest, place = source, []
        for size in reversed(sizes):
            place.insert(0, rest % size)
            rest //= size
        target = 0
        for name, size, at in zip(used, sizes, place):
            move = moves[names.index(name)]
            target = target * size + ((at ^ move) if name == "blk" else (at + move) % size)
        pairs.append((source, target))
    return lax.ppermute(x, used if len(used) > 1 else used[0], pairs)


def params(mib=24):
    return pltpu.CompilerParams(vmem_limit_bytes=mib * 1024 * 1024)


def cost(us):
    return pl.CostEstimate(flops=int(us * 1.1e9), transcendentals=0, bytes_accessed=1024)


def start_all(pairs, sem, first=0):
    copies = [pltpu.make_async_copy(s, d, sem.at[first + i]) for i, (s, d) in enumerate(pairs)]
    for copy in copies:
        copy.start()
    return copies


def wait_all(copies):
    for copy in copies:
        copy.wait()


def modulate_kernel(held, step, table_ref, w_ref, *refs):
    out_ref, table, w, sem = refs[held:]
    copies = start_all([(table_ref, table), (w_ref, w)], sem)
    copies[0].wait()
    at = lax.broadcasted_iota(jnp.int32, table.shape, 0)
    v = jnp.sum(jnp.where(at == step[0], table[...], 0.0), axis=0, keepdims=True)
    activated = (v / (1.0 + jnp.exp(-v))).astype(BF16)
    wide = jnp.broadcast_to(activated, (8, v.shape[1]))
    count, cols = w.shape[:2]
    parts = []
    copies[1].wait()
    for i in range(count):
        part = lax.dot_general(
            wide, w[i], (((1,), (1,)), ((), ())), preferred_element_type=F32
        )[0:1]
        parts += [part[:, :HD], jnp.concatenate([part[:, HD:], part[:, : 2 * HD - cols]], axis=1)]
    parts += [jnp.zeros((8 - len(parts), HD), F32)]
    out_ref[...] = jnp.concatenate(parts, axis=0)


def modulate(timestep, time_table, mod_weight, hold):
    return pl.pallas_call(
        functools.partial(modulate_kernel, len(hold)),
        in_specs=[SMEM_SPEC] + [ANY_SPEC] * (2 + len(hold)),
        out_specs=VMEM_SPEC,
        out_shape=shaped((8, HD), F32),
        scratch_shapes=[
            pltpu.VMEM(time_table.shape, F32),
            pltpu.VMEM(mod_weight.shape, BF16),
            pltpu.SemaphoreType.DMA((2,)),
        ],
        compiler_params=params(QKV_MIB),
        cost_estimate=cost(0.1),
        name="modulate",
    )(timestep, time_table, mod_weight, *hold)


def join_kernel(x_ref, y_ref, *refs):
    count = x_ref.shape[0]
    refs[-1][:count] = x_ref[...]
    refs[-1][count:] = y_ref[...]


def join(x, y, hold):
    return pl.pallas_call(
        join_kernel,
        in_specs=[VMEM_SPEC] * 2 + [ANY_SPEC] * len(hold),
        out_specs=VMEM_SPEC,
        out_shape=shaped((2 * x.shape[0],) + x.shape[1:], x.dtype),
        compiler_params=params(),
        cost_estimate=cost(0.1),
        name="join",
    )(x, y, *hold)


def norm_rows(x, shift_vec, scale_vec):
    center = x - jnp.mean(x, axis=-1, keepdims=True)
    normed = center * lax.rsqrt(jnp.mean(center * center, axis=-1, keepdims=True) + 1e-06)
    return (normed * (1.0 + scale_vec) + shift_vec).astype(BF16)


def norm_heads(part, heads):
    out = []
    for h in range(heads):
        v = part[:, h * HD : (h + 1) * HD]
        out.append(v * lax.rsqrt(jnp.mean(v * v, axis=-1, keepdims=True) + 1e-06))
    return jnp.concatenate(out, axis=1).astype(BF16)


def project(mod_s, w_s, w_copies, q_ref, kv_ref):
    for g in range(3):
        w_copies[g].wait()
        part = jnp.dot(mod_s[...], w_s[g], preferred_element_type=F32)
        heads = part.shape[1] // HD
        if g == 0:
            q_ref[...] = norm_heads(part, heads)
        elif g == 1:
            kv_ref[0] = norm_heads(part, heads)
        else:
            kv_ref[1] = part.astype(BF16)


def qkv_first_kernel(
    n, held, sc, x0, x1, x2, x3, m0, m1, m2, m3, w_ref, *refs
):
    q_ref, kv_ref, cols_ref, vectors_ref, gate_ref, *scratch = refs[held:]
    x_s, mod_s, w_s, tiles, sem = scratch
    u, b = sc[1], sc[2]
    rows = x0.shape[0]
    width = cols_ref.shape[1]
    blocks = m0.shape[0]
    inner = x0.shape[1] // (n * blocks) - HD
    at = [lax.rem(u - k + n, n) for k in range(n)]
    spots = [pl.ds(pl.multiple_of(i * rows, rows), rows) for i in at]
    x_copies = start_all([(r, x_s.at[i]) for r, i in zip((x0, x1, x2, x3), spots)], sem)
    w_copies = start_all([(w_ref.at[g], w_s.at[g]) for g in range(3)], sem, n)
    for i, ref in zip(at, (m0, m1, m2, m3)):
        for j in range(blocks):
            tiles[i * blocks + jnp.bitwise_xor(b, j)] = ref[j]
    for i, ref in enumerate((vectors_ref.at[0:1], vectors_ref.at[1:2], gate_ref)):
        pieces = []
        for j in range(n * blocks):
            pieces += [tiles[j, 2 * i : 2 * i + 1, :], tiles[j, 2 * i + 1 : 2 * i + 2, :inner]]
        ref[...] = jnp.concatenate(pieces, axis=1)
    for copy, i in zip(x_copies, spots):
        copy.wait()
        mod_s[i, :] = norm_rows(x_s[i, :].astype(F32), vectors_ref[0:1, :], vectors_ref[1:2, :])
    cols_ref[...] = x_s[:, pl.ds(pl.multiple_of(u * width, 128), width)]
    project(mod_s, w_s, w_copies, q_ref, kv_ref)


def qkv_next_kernel(
    n, sc, y0, y1, y2, y3, vectors, w_ref, q_ref, kv_ref, cols_ref, x_s, mod_s, w_s, sem
):
    u = sc[1]
    first = sc[0] == 0
    width = y0.shape[1]
    rows = x_s.shape[0] // n
    by_cols, by_rows = [], []
    for k, ref in enumerate((y0, y1, y2, y3)):
        i = lax.rem(u - k + n, n)
        at = pl.ds(pl.multiple_of(i * width, 128), width)
        by_cols.append(pltpu.make_async_copy(ref, x_s.at[:, at], sem.at[k]))
        at = pl.ds(pl.multiple_of(i * rows, rows), rows)
        for j in range(n):
            by_rows.append(
                pltpu.make_async_copy(
                    ref.at[j * rows : (j + 1) * rows, :],
                    x_s.at[at, j * width : (j + 1) * width],
                    sem.at[n + n * k + j],
                )
            )

    @pl.when(first)
    def _():
        for copy in by_rows:
            copy.start()

    @pl.when(jnp.logical_not(first))
    def _():
        for copy in by_cols:
            copy.start()

    w_copies = start_all([(w_ref.at[g], w_s.at[g]) for g in range(3)], sem, n + n * n)

    @pl.when(first)
    def _():
        wait_all(by_rows)

    @pl.when(jnp.logical_not(first))
    def _():
        wait_all(by_cols)

    for r in range(n):
        at = slice(r * rows, (r + 1) * rows)
        mod_s[at, :] = norm_rows(x_s[at, :].astype(F32), vectors[0:1, :], vectors[1:2, :])
    cols_ref[...] = x_s[:, pl.ds(pl.multiple_of(u * width, 128), width)]
    project(mod_s, w_s, w_copies, q_ref, kv_ref)


def shaped(shape, dtype=BF16):
    return jax.ShapeDtypeStruct(shape, dtype)


def qkv_scratch(tokens, weight, sems):
    width = weight.shape[1]
    return [
        pltpu.VMEM((tokens, width), BF16),
        pltpu.VMEM((tokens, width), BF16),
        pltpu.VMEM(weight.shape, BF16),
        pltpu.SemaphoreType.DMA((sems,)),
    ]


def qkv_first(n, scalars, pieces, tiles, weight, hold):
    rows, width = pieces[0].shape
    cols = weight.shape[2]
    tokens = n * rows
    blocks = tiles[0].shape[0]
    scratch = qkv_scratch(tokens, weight, n + 3)
    return pl.pallas_call(
        functools.partial(qkv_first_kernel, n, len(hold)),
        in_specs=[SMEM_SPEC] + [ANY_SPEC] * n + [VMEM_SPEC] * n + [ANY_SPEC] * (1 + len(hold)),
        out_specs=[VMEM_SPEC] * 5,
        out_shape=[
            shaped((tokens, cols)),
            shaped((2, tokens, cols)),
            shaped((tokens, width // n)),
            shaped((2, width), F32),
            shaped((1, width), F32),
        ],
        scratch_shapes=scratch[:3] + [pltpu.VMEM((n * blocks, 8, HD), F32)] + scratch[3:],
        compiler_params=params(QKV_MIB),
        cost_estimate=cost(0.1),
        name="qkv_first",
    )(scalars, *pieces, *tiles, weight, *hold)


def qkv_next(n, scalars, pieces, vectors, weight):
    tokens, part = pieces[0].shape
    cols = weight.shape[2]
    return pl.pallas_call(
        functools.partial(qkv_next_kernel, n),
        in_specs=[SMEM_SPEC] + [ANY_SPEC] * n + [VMEM_SPEC, ANY_SPEC],
        out_specs=[VMEM_SPEC] * 3,
        out_shape=[shaped((tokens, cols)), shaped((2, tokens, cols)), shaped((tokens, part))],
        scratch_shapes=qkv_scratch(tokens, weight, n + n * n + 3),
        compiler_params=params(QKV_MIB),
        cost_estimate=cost(6),
        name="qkv_next",
    )(scalars, *pieces, vectors, weight)


def cut_into(refs, whole, u, n, by_rows):
    for k, ref in enumerate(refs):
        rows, part = ref.shape
        if by_rows:
            at = pl.ds(pl.multiple_of(lax.rem(u - k + n, n) * rows, rows), rows)
            ref[...] = whole[at, :]
        else:
            at = pl.ds(pl.multiple_of(lax.rem(u + k, n) * part, 128), part)
            ref[...] = whole[:, at]


def cut_kernel(n, count, sc, *refs):
    wholes, outs = refs[:count], refs[-n * count :]
    for c in range(count):
        cut_into(outs[c * n : (c + 1) * n], wholes[c], sc[1], n, False)


def cut_columns(n, scalars, wholes, hold):
    outs = []
    for x in wholes:
        outs += [shaped((x.shape[0], x.shape[1] // n))] * n
    return pl.pallas_call(
        functools.partial(cut_kernel, n, len(wholes)),
        in_specs=[SMEM_SPEC] + [VMEM_SPEC] * len(wholes) + [ANY_SPEC] * len(hold),
        out_specs=[VMEM_SPEC] * len(outs),
        out_shape=outs,
        compiler_params=params(),
        cost_estimate=cost(1),
        name="cut_columns",
    )(scalars, *wholes, *hold)


NT = (((1,), (1,)), ((), ()))
RATE = HD ** (-0.5) * LOG2E


def weigh(q, pieces):
    scores = []
    for keys, _, masked in pieces:
        score = lax.dot_general(q, keys, NT, preferred_element_type=F32)
        scores.append(score if masked is None else jnp.where(masked, -1e30, score))
    peak = functools.reduce(jnp.maximum, [jnp.max(s, axis=-1, keepdims=True) for s in scores])
    total = jnp.zeros(peak.shape, F32)
    numer = jnp.zeros(q.shape, F32)
    for s, (_, values, _) in zip(scores, pieces):
        weights = jnp.exp2((s - peak) * RATE)
        total = total + jnp.sum(weights, axis=-1, keepdims=True)
        numer = numer + jnp.dot(weights.astype(BF16), values, preferred_element_type=F32)
    return peak, total, numer


def store_part(refs, h, peak, total, numer, stats):
    at = slice(h * HD, (h + 1) * HD)
    lane = lax.broadcasted_iota(jnp.int32, stats.shape, 1)
    level = peak * RATE + jnp.log2(total)
    if len(refs) == 2:
        refs[0][:, at] = numer / total
        return jnp.where(lane == h, level, stats)
    refs[0][:, at] = (numer / total).astype(BF16)
    high = level.astype(BF16).astype(F32)
    middle = (level - high).astype(BF16).astype(F32)
    for j, piece in enumerate((high, middle, level - high - middle)):
        stats = jnp.where(lane == 3 * h + j, piece, stats)
    return stats


def attend_kernel(packed, held, sc, patch, q_ref, fo, fm, so, sm, *refs):
    outs = refs[held:]
    b, p = sc[2], patch[0]
    heads = q_ref.shape[1] // HD
    stats = jnp.zeros((q_ref.shape[0], HD), F32)
    for h in range(heads):
        at = slice(h * HD, (h + 1) * HD)
        pieces = [(ref[0, :, at], ref[1, :, at], None) for ref in (fo, fm)]
        pieces += [
            (ref[0, :, at], ref[1, :, at], p == jnp.bitwise_xor(b, j))
            for j, ref in enumerate((so, sm))
        ]
        stats = store_part(outs, h, *weigh(q_ref[:, at], pieces), stats)
    if packed:
        outs[0][:, heads * HD :] = stats.astype(BF16)
    else:
        outs[1][...] = stats


def attend(packed, scalars, patch, q, fo, fm, so, sm, hold=()):
    rows, cols = q.shape
    if packed:
        out_shape = [shaped((rows, cols + HD))]
    else:
        out_shape = [shaped((rows, cols), F32), shaped((rows, HD), F32)]
    return pl.pallas_call(
        functools.partial(attend_kernel, packed, len(hold)),
        in_specs=[SMEM_SPEC] * 2 + [VMEM_SPEC] * 5 + [ANY_SPEC] * len(hold),
        out_specs=[VMEM_SPEC] * len(out_shape),
        out_shape=out_shape,
        compiler_params=params(ATTEND_MIB),
        cost_estimate=cost(5),
        name="attend_other" if packed else "attend_own",
    )(scalars, patch, q, fo, fm, so, sm, *hold)


def attend_stale_kernel(sc, patch, q_ref, fo, fm, stale, o_ref, level_ref, stale_s, sem):
    count = stale.shape[0]
    live = [lax.rem(patch[0] + 1 + i, count) for i in range(count - 1)]
    copies = start_all([(stale.at[j], stale_s.at[i]) for i, j in enumerate(live)], sem)
    wait_all(copies)
    stats = jnp.zeros(level_ref.shape, F32)
    for h in range(q_ref.shape[1] // HD):
        at = slice(h * HD, (h + 1) * HD)
        pieces = [(ref[0, :, at], ref[1, :, at], None) for ref in (fo, fm)]
        pieces += [(stale_s[i, 0, :, at], stale_s[i, 1, :, at], None) for i in range(count - 1)]
        stats = store_part((o_ref, level_ref), h, *weigh(q_ref[:, at], pieces), stats)
    level_ref[...] = stats


def attend_stale(scalars, patch, q, fo, fm, stale):
    rows, cols = q.shape
    return pl.pallas_call(
        attend_stale_kernel,
        in_specs=[SMEM_SPEC] * 2 + [VMEM_SPEC] * 3 + [ANY_SPEC],
        out_specs=[VMEM_SPEC] * 2,
        out_shape=[shaped((rows, cols), F32), shaped((rows, HD), F32)],
        scratch_shapes=[
            pltpu.VMEM((stale.shape[0] - 1,) + stale.shape[1:], BF16),
            pltpu.SemaphoreType.DMA((stale.shape[0] - 1,)),
        ],
        compiler_params=params(QKV_MIB),
        cost_estimate=cost(8),
        name="attend_stale",
    )(scalars, patch, q, fo, fm, stale)


def attend_rest_kernel(q_ref, fo, fm, o_ref, level_ref, out_ref):
    for h in range(q_ref.shape[1] // HD):
        at = slice(h * HD, (h + 1) * HD)
        pieces = [(ref[0, :, at], ref[1, :, at], None) for ref in (fo, fm)]
        peak, total, numer = weigh(q_ref[:, at], pieces)
        peak = peak * RATE
        level = level_ref[:, h : h + 1]
        top = jnp.maximum(level, peak)
        a, b = jnp.exp2(level - top), jnp.exp2(peak - top)
        out_ref[:, at] = ((a * o_ref[:, at] + b * numer) / (a + b * total)).astype(BF16)


def attend_rest(q, fo, fm, o, level):
    return pl.pallas_call(
        attend_rest_kernel,
        in_specs=[VMEM_SPEC] * 5,
        out_specs=VMEM_SPEC,
        out_shape=shaped(q.shape),
        compiler_params=params(ATTEND_MIB),
        cost_estimate=cost(3),
        name="attend_rest",
    )(q, fo, fm, o, level)


def merge_kernel(o_ref, level_ref, other_ref, *refs):
    out_ref = refs[-1]
    cols = o_ref.shape[1]
    for h in range(cols // HD):
        at = slice(h * HD, (h + 1) * HD)
        mine = level_ref[:, h : h + 1]
        parts = [
            other_ref[:, cols + 3 * h + j : cols + 3 * h + j + 1].astype(F32) for j in range(3)
        ]
        theirs = parts[0] + parts[1] + parts[2]
        peak = jnp.maximum(mine, theirs)
        a, b = jnp.exp2(mine - peak), jnp.exp2(theirs - peak)
        mixed = (a * o_ref[:, at] + b * other_ref[:, at].astype(F32)) / (a + b)
        out_ref[:, at] = mixed.astype(BF16)


def merge(o, level, other, hold=()):
    return pl.pallas_call(
        merge_kernel,
        in_specs=[VMEM_SPEC] * 3 + [ANY_SPEC] * len(hold),
        out_specs=VMEM_SPEC,
        out_shape=jax.ShapeDtypeStruct(o.shape, BF16),
        compiler_params=params(),
        cost_estimate=cost(12),
        name="merge",
    )(o, level, other, *hold)


def place_kernel(n, sc, *refs):
    u, core = sc[1], lax.rem(sc[2], 2)
    mine, mate, out_ref = refs[:n], refs[n : 2 * n], refs[2 * n]
    rows = mine[0].shape[0] // 2
    for k in range(n):
        for ref, flip in ((mine[k], 0), (mate[k], 1)):
            for z in range(2):
                at = lax.rem(u - k + n, n) * 4 + 2 * z + jnp.bitwise_xor(core, flip)
                at = pl.multiple_of(at * rows, rows)
                out_ref[pl.ds(at, rows), :] = ref[z * rows : (z + 1) * rows, :]


def place(n, scalars, mine, mate):
    rows, cols = mine[0].shape
    return pl.pallas_call(
        functools.partial(place_kernel, n),
        in_specs=[SMEM_SPEC] + [VMEM_SPEC] * (2 * n),
        out_specs=VMEM_SPEC,
        out_shape=shaped((2 * n * rows, cols)),
        compiler_params=params(),
        cost_estimate=cost(0.1),
        name="place",
    )(scalars, *mine, *mate)


def pass_on(x, hold):
    return pl.pallas_call(
        lambda *refs: None,
        in_specs=[ANY_SPEC] * (1 + len(hold)),
        out_specs=ANY_SPEC,
        out_shape=shaped(x.shape, x.dtype),
        input_output_aliases={0: 0},
        compiler_params=params(),
        cost_estimate=cost(0.1),
        name="pass_on",
    )(x, *hold)


def out_cols_kernel(n, last, sc, a0, a1, a2, a3, w_ref, x_ref, gate_ref, *refs):
    u = sc[1]
    depth = a0.shape[1]
    tokens, width = x_ref.shape
    rows = tokens // n
    total = None
    for k, ref in enumerate((a0, a1, a2, a3)):
        at = pl.multiple_of(lax.rem(u - k + n, n) * depth, 128)
        part = jnp.dot(ref[...], w_ref[pl.ds(at, depth), :], preferred_element_type=F32)
        total = part if total is None else total + part
    gate = gate_ref[:, pl.ds(pl.multiple_of(u * width, 128), width)]
    y = (x_ref[...].astype(F32) + gate * total).astype(BF16)
    y_s = refs[-1]
    y_s[...] = y
    cut_into(refs[-n - 1 : -1], y_s, u, n, True)
    if not last:
        enter, next_ref = refs[:2]
        end = sc[0] == sc[3] - 1

        @pl.when(end)
        def _():
            for j in range(n):
                next_ref[j * rows : (j + 1) * rows, :] = enter[:, j * width : (j + 1) * width]

        @pl.when(jnp.logical_not(end))
        def _():
            next_ref[...] = y


def out_cols(n, scalars, pieces, weight, x, gate, enter=None):
    tokens, width = x.shape
    last = enter is None
    outs = [shaped((tokens // n, width))] * n
    return pl.pallas_call(
        functools.partial(out_cols_kernel, n, last),
        in_specs=[SMEM_SPEC] + [VMEM_SPEC] * (n + 3 + (not last)),
        out_specs=[VMEM_SPEC] * (n + (not last)),
        out_shape=outs if last else [shaped(x.shape)] + outs,
        scratch_shapes=[pltpu.VMEM(x.shape, BF16)],
        compiler_params=params(),
        cost_estimate=cost(2),
        name="out_cols",
    )(scalars, *pieces, weight, x, gate, *([] if last else [enter]))


def finish_kernel(n, sc, *refs):
    out_ref = refs[-1]
    width = refs[0].shape[1]
    for t in range(2):
        for k in range(n):
            at = pl.multiple_of(lax.rem(sc[1] + k, n) * width, 128)
            out_ref[0, t, :, pl.ds(at, width)] = refs[t * n + k][...]


def finish(n, scalars, parts):
    rows, width = parts[0].shape
    return pl.pallas_call(
        functools.partial(finish_kernel, n),
        in_specs=[SMEM_SPEC] + [VMEM_SPEC] * len(parts),
        out_specs=VMEM_SPEC,
        out_shape=shaped((1, 2, rows, n * width)),
        compiler_params=params(),
        cost_estimate=cost(1.5),
        name="finish",
    )(scalars, *parts)


def per_device(
    in_flight,
    entering,
    patch_ids,
    timestep,
    time_table,
    mod_weight,
    qkv_weight,
    out_weight,
    stale_cache,
):
    s = lax.axis_index("section")
    u = lax.axis_index("uly")
    b = lax.axis_index("blk")
    n = lax.axis_size("uly")
    section_count = lax.axis_size("section")
    rows, width = in_flight.shape[1:]
    part = width // n
    scalars = jnp.stack([s, u, b, section_count]).astype(jnp.int32)
    patches = [lax.dynamic_slice(patch_ids, (t + section_count - 1 - s,), (1,)) for t in range(2)]

    x_pieces = [in_flight[0]] + [shift(in_flight[0], uly=k) for k in range(1, n)]
    stale_own = jnp.transpose(stale_cache[0], (1, 0, 2))
    stale_mate = shift(stale_own, blk=1)
    tile = modulate(timestep, time_table, jnp.transpose(mod_weight[0], (1, 2, 0)), [])
    tiles = jnp.stack([tile, shift(tile, blk=1)])
    tiles = join(tiles, shift(tiles, blk=2), [stale_mate])
    tiles = [tiles] + [shift(tiles, uly=k) for k in range(1, n)]

    weight = jnp.transpose(qkv_weight[0], (1, 0, 2))
    pair = lax.all_gather(
        out_weight[0], "blk", axis=0, tiled=True, axis_index_groups=[[0, 2], [1, 3]]
    )

    q, fresh, cols, vectors, gate = qkv_first(n, scalars, x_pieces, tiles, weight, [])

    q_other = shift(q, blk=2)
    rest = (fresh, shift(fresh, blk=1), stale_own, stale_mate)
    cut = cut_columns(n, scalars, [pair], [rest[1]])
    mine = [cut[0]] + [shift(cut[k], uly=k) for k in range(1, n)]
    mates = [shift(x, blk=1) for x in mine]
    (for_other,) = attend(True, scalars, patches[0], q_other, *rest)
    o, level = attend(False, scalars, patches[0], q, *rest, hold=[for_other])
    other = shift(for_other, blk=2)
    w_cols = place(n, scalars, mine, mates)
    attended = merge(o, level, other, hold=mates)
    a_pieces = [attended] + [shift(attended, uly=k) for k in range(1, n)]
    y, *parts = out_cols(n, scalars, a_pieces, w_cols, cols, gate, entering[0])
    parts = [parts[0]] + [shift(parts[k], uly=-k) for k in range(1, n)]
    y = pass_on(shift(y, section=1), parts[1:])
    y_pieces = [y] + [shift(y, uly=k) for k in range(1, n)]
    stale_all = lax.all_gather(pass_on(stale_own, [attended]), "blk", axis=0)
    q, fresh, cols = qkv_next(n, scalars, y_pieces, vectors, weight)

    mate, far = shift(fresh, blk=1), shift(fresh, blk=2)
    o, level = attend_stale(scalars, patches[1], q, fresh, mate, stale_all)
    far = pass_on(far, [level])
    far_mate = shift(far, blk=1)
    attended = attend_rest(q, far, far_mate, o, level)
    a_pieces = [attended] + [shift(attended, uly=k) for k in range(1, n)]
    last = out_cols(n, scalars, a_pieces, w_cols, cols, gate)
    last = [last[0]] + [shift(last[k], uly=-k) for k in range(1, n)]
    return finish(n, scalars, parts + last)


def solution(mesh):
    return jax.shard_map(
        per_device,
        mesh=mesh,
        in_specs=(
            P("section", ("uly", "blk"), None),
            P(None, ("uly", "blk"), None),
            P(),
            P(),
            P(),
            P("section", None, None, ("uly", "blk")),
            P("section", None, None, "uly"),
            P("section", ("uly", "blk"), None),
            P("section", "blk", None, "uly"),
        ),
        out_specs=P("section", None, ("uly", "blk"), None),
        check_vma=False,
    )
```

```python
import functools

import jax
import jax.numpy as jnp
from jax import lax
from jax.experimental import pallas as pl
from jax.experimental.pallas import tpu as pltpu
from jax.sharding import PartitionSpec as P

HD = 128
F32 = jnp.float32
BF16 = jnp.bfloat16
QKV_MIB = 48
ATTEND_MIB = 24
LOG2E = 1.4426950408889634
SMEM_SPEC = pl.BlockSpec(memory_space=pltpu.SMEM)
VMEM_SPEC = pl.BlockSpec(memory_space=pltpu.VMEM)
ANY_SPEC = pl.BlockSpec(memory_space=pl.ANY)


def shift(x, section=0, uly=0, blk=0):
    names = ("section", "uly", "blk")
    moves = (section, uly, blk)
    used = tuple(n for n, m in zip(names, moves) if m)
    sizes = [lax.axis_size(n) for n in used]
    total = 1
    for size in sizes:
        total *= size
    pairs = []
    for source in range(total):
        rest, place = source, []
        for size in reversed(sizes):
            place.insert(0, rest % size)
            rest //= size
        target = 0
        for name, size, at in zip(used, sizes, place):
            move = moves[names.index(name)]
            target = target * size + ((at ^ move) if name == "blk" else (at + move) % size)
        pairs.append((source, target))
    return lax.ppermute(x, used if len(used) > 1 else used[0], pairs)


def params(mib=24):
    return pltpu.CompilerParams(vmem_limit_bytes=mib * 1024 * 1024)


def cost(us):
    return pl.CostEstimate(flops=int(us * 1.1e9), transcendentals=0, bytes_accessed=1024)


def start_all(pairs, sem, first=0):
    copies = [pltpu.make_async_copy(s, d, sem.at[first + i]) for i, (s, d) in enumerate(pairs)]
    for copy in copies:
        copy.start()
    return copies


def wait_all(copies):
    for copy in copies:
        copy.wait()


def modulate_kernel(held, step, table_ref, w_ref, *refs):
    out_ref, table, w, sem = refs[held:]
    copies = start_all([(table_ref, table), (w_ref, w)], sem)
    copies[0].wait()
    at = lax.broadcasted_iota(jnp.int32, table.shape, 0)
    v = jnp.sum(jnp.where(at == step[0], table[...], 0.0), axis=0, keepdims=True)
    activated = (v / (1.0 + jnp.exp(-v))).astype(BF16)
    wide = jnp.broadcast_to(activated, (8, v.shape[1]))
    count, cols = w.shape[:2]
    parts = []
    copies[1].wait()
    for i in range(count):
        part = lax.dot_general(
            wide, w[i], (((1,), (1,)), ((), ())), preferred_element_type=F32
        )[0:1]
        parts += [part[:, :HD], jnp.concatenate([part[:, HD:], part[:, : 2 * HD - cols]], axis=1)]
    parts += [jnp.zeros((8 - len(parts), HD), F32)]
    out_ref[...] = jnp.concatenate(parts, axis=0)


def modulate(timestep, time_table, mod_weight, hold):
    return pl.pallas_call(
        functools.partial(modulate_kernel, len(hold)),
        in_specs=[SMEM_SPEC] + [ANY_SPEC] * (2 + len(hold)),
        out_specs=VMEM_SPEC,
        out_shape=shaped((8, HD), F32),
        scratch_shapes=[
            pltpu.VMEM(time_table.shape, F32),
            pltpu.VMEM(mod_weight.shape, BF16),
            pltpu.SemaphoreType.DMA((2,)),
        ],
        compiler_params=params(QKV_MIB),
        cost_estimate=cost(0.1),
        name="modulate",
    )(timestep, time_table, mod_weight, *hold)


def join_kernel(x_ref, y_ref, *refs):
    count = x_ref.shape[0]
    refs[-1][:count] = x_ref[...]
    refs[-1][count:] = y_ref[...]


def join(x, y, hold):
    return pl.pallas_call(
        join_kernel,
        in_specs=[VMEM_SPEC] * 2 + [ANY_SPEC] * len(hold),
        out_specs=VMEM_SPEC,
        out_shape=shaped((2 * x.shape[0],) + x.shape[1:], x.dtype),
        compiler_params=params(),
        cost_estimate=cost(0.1),
        name="join",
    )(x, y, *hold)


def norm_rows(x, shift_vec, scale_vec):
    center = x - jnp.mean(x, axis=-1, keepdims=True)
    normed = center * lax.rsqrt(jnp.mean(center * center, axis=-1, keepdims=True) + 1e-06)
    return (normed * (1.0 + scale_vec) + shift_vec).astype(BF16)


def norm_heads(part, heads):
    out = []
    for h in range(heads):
        v = part[:, h * HD : (h + 1) * HD]
        out.append(v * lax.rsqrt(jnp.mean(v * v, axis=-1, keepdims=True) + 1e-06))
    return jnp.concatenate(out, axis=1).astype(BF16)


def project(mod_s, w_s, w_copies, q_ref, kv_ref):
    for g in range(3):
        w_copies[g].wait()
        part = jnp.dot(mod_s[...], w_s[g], preferred_element_type=F32)
        heads = part.shape[1] // HD
        if g == 0:
            q_ref[...] = norm_heads(part, heads)
        elif g == 1:
            kv_ref[0] = norm_heads(part, heads)
        else:
            kv_ref[1] = part.astype(BF16)


def qkv_first_kernel(
    n, held, sc, x0, x1, x2, x3, m0, m1, m2, m3, w_ref, *refs
):
    q_ref, kv_ref, cols_ref, vectors_ref, gate_ref, *scratch = refs[held:]
    x_s, mod_s, w_s, tiles, sem = scratch
    u, b = sc[1], sc[2]
    rows = x0.shape[0]
    width = cols_ref.shape[1]
    blocks = m0.shape[0]
    inner = x0.shape[1] // (n * blocks) - HD
    at = [lax.rem(u - k + n, n) for k in range(n)]
    spots = [pl.ds(pl.multiple_of(i * rows, rows), rows) for i in at]
    x_copies = start_all([(r, x_s.at[i]) for r, i in zip((x0, x1, x2, x3), spots)], sem)
    w_copies = start_all([(w_ref.at[g], w_s.at[g]) for g in range(3)], sem, n)
    for i, ref in zip(at, (m0, m1, m2, m3)):
        for j in range(blocks):
            tiles[i * blocks + jnp.bitwise_xor(b, j)] = ref[j]
    for i, ref in enumerate((vectors_ref.at[0:1], vectors_ref.at[1:2], gate_ref)):
        pieces = []
        for j in range(n * blocks):
            pieces += [tiles[j, 2 * i : 2 * i + 1, :], tiles[j, 2 * i + 1 : 2 * i + 2, :inner]]
        ref[...] = jnp.concatenate(pieces, axis=1)
    for copy, i in zip(x_copies, spots):
        copy.wait()
        mod_s[i, :] = norm_rows(x_s[i, :].astype(F32), vectors_ref[0:1, :], vectors_ref[1:2, :])
    cols_ref[...] = x_s[:, pl.ds(pl.multiple_of(u * width, 128), width)]
    project(mod_s, w_s, w_copies, q_ref, kv_ref)


def qkv_next_kernel(
    n, sc, y0, y1, y2, y3, vectors, w_ref, q_ref, kv_ref, cols_ref, x_s, mod_s, w_s, sem
):
    u = sc[1]
    first = sc[0] == 0
    width = y0.shape[1]
    rows = x_s.shape[0] // n
    by_cols, by_rows = [], []
    for k, ref in enumerate((y0, y1, y2, y3)):
        i = lax.rem(u - k + n, n)
        at = pl.ds(pl.multiple_of(i * width, 128), width)
        by_cols.append(pltpu.make_async_copy(ref, x_s.at[:, at], sem.at[k]))
        at = pl.ds(pl.multiple_of(i * rows, rows), rows)
        for j in range(n):
            by_rows.append(
                pltpu.make_async_copy(
                    ref.at[j * rows : (j + 1) * rows, :],
                    x_s.at[at, j * width : (j + 1) * width],
                    sem.at[n + n * k + j],
                )
            )

    @pl.when(first)
    def _():
        for copy in by_rows:
            copy.start()

    @pl.when(jnp.logical_not(first))
    def _():
        for copy in by_cols:
            copy.start()

    w_copies = start_all([(w_ref.at[g], w_s.at[g]) for g in range(3)], sem, n + n * n)

    @pl.when(first)
    def _():
        wait_all(by_rows)

    @pl.when(jnp.logical_not(first))
    def _():
        wait_all(by_cols)

    for r in range(n):
        at = slice(r * rows, (r + 1) * rows)
        mod_s[at, :] = norm_rows(x_s[at, :].astype(F32), vectors[0:1, :], vectors[1:2, :])
    cols_ref[...] = x_s[:, pl.ds(pl.multiple_of(u * width, 128), width)]
    project(mod_s, w_s, w_copies, q_ref, kv_ref)


def shaped(shape, dtype=BF16):
    return jax.ShapeDtypeStruct(shape, dtype)


def qkv_scratch(tokens, weight, sems):
    width = weight.shape[1]
    return [
        pltpu.VMEM((tokens, width), BF16),
        pltpu.VMEM((tokens, width), BF16),
        pltpu.VMEM(weight.shape, BF16),
        pltpu.SemaphoreType.DMA((sems,)),
    ]


def qkv_first(n, scalars, pieces, tiles, weight, hold):
    rows, width = pieces[0].shape
    cols = weight.shape[2]
    tokens = n * rows
    blocks = tiles[0].shape[0]
    scratch = qkv_scratch(tokens, weight, n + 3)
    return pl.pallas_call(
        functools.partial(qkv_first_kernel, n, len(hold)),
        in_specs=[SMEM_SPEC] + [ANY_SPEC] * n + [VMEM_SPEC] * n + [ANY_SPEC] * (1 + len(hold)),
        out_specs=[VMEM_SPEC] * 5,
        out_shape=[
            shaped((tokens, cols)),
            shaped((2, tokens, cols)),
            shaped((tokens, width // n)),
            shaped((2, width), F32),
            shaped((1, width), F32),
        ],
        scratch_shapes=scratch[:3] + [pltpu.VMEM((n * blocks, 8, HD), F32)] + scratch[3:],
        compiler_params=params(QKV_MIB),
        cost_estimate=cost(0.1),
        name="qkv_first",
    )(scalars, *pieces, *tiles, weight, *hold)


def qkv_next(n, scalars, pieces, vectors, weight):
    tokens, part = pieces[0].shape
    cols = weight.shape[2]
    return pl.pallas_call(
        functools.partial(qkv_next_kernel, n),
        in_specs=[SMEM_SPEC] + [ANY_SPEC] * n + [VMEM_SPEC, ANY_SPEC],
        out_specs=[VMEM_SPEC] * 3,
        out_shape=[shaped((tokens, cols)), shaped((2, tokens, cols)), shaped((tokens, part))],
        scratch_shapes=qkv_scratch(tokens, weight, n + n * n + 3),
        compiler_params=params(QKV_MIB),
        cost_estimate=cost(6),
        name="qkv_next",
    )(scalars, *pieces, vectors, weight)


def cut_into(refs, whole, u, n, by_rows):
    for k, ref in enumerate(refs):
        rows, part = ref.shape
        if by_rows:
            at = pl.ds(pl.multiple_of(lax.rem(u - k + n, n) * rows, rows), rows)
            ref[...] = whole[at, :]
        else:
            at = pl.ds(pl.multiple_of(lax.rem(u + k, n) * part, 128), part)
            ref[...] = whole[:, at]


def cut_kernel(n, count, sc, *refs):
    wholes, outs = refs[:count], refs[-n * count :]
    for c in range(count):
        cut_into(outs[c * n : (c + 1) * n], wholes[c], sc[1], n, False)


def cut_columns(n, scalars, wholes, hold):
    outs = []
    for x in wholes:
        outs += [shaped((x.shape[0], x.shape[1] // n))] * n
    return pl.pallas_call(
        functools.partial(cut_kernel, n, len(wholes)),
        in_specs=[SMEM_SPEC] + [VMEM_SPEC] * len(wholes) + [ANY_SPEC] * len(hold),
        out_specs=[VMEM_SPEC] * len(outs),
        out_shape=outs,
        compiler_params=params(),
        cost_estimate=cost(1),
        name="cut_columns",
    )(scalars, *wholes, *hold)


NT = (((1,), (1,)), ((), ()))
RATE = HD ** (-0.5) * LOG2E


def weigh(q, pieces):
    scores = []
    for keys, _, masked in pieces:
        score = lax.dot_general(q, keys, NT, preferred_element_type=F32)
        scores.append(score if masked is None else jnp.where(masked, -1e30, score))
    peak = functools.reduce(jnp.maximum, [jnp.max(s, axis=-1, keepdims=True) for s in scores])
    total = jnp.zeros(peak.shape, F32)
    numer = jnp.zeros(q.shape, F32)
    for s, (_, values, _) in zip(scores, pieces):
        weights = jnp.exp2((s - peak) * RATE)
        total = total + jnp.sum(weights, axis=-1, keepdims=True)
        numer = numer + jnp.dot(weights.astype(BF16), values, preferred_element_type=F32)
    return peak, total, numer


def store_part(refs, h, peak, total, numer, stats):
    at = slice(h * HD, (h + 1) * HD)
    lane = lax.broadcasted_iota(jnp.int32, stats.shape, 1)
    level = peak * RATE + jnp.log2(total)
    if len(refs) == 2:
        refs[0][:, at] = numer / total
        return jnp.where(lane == h, level, stats)
    refs[0][:, at] = (numer / total).astype(BF16)
    high = level.astype(BF16).astype(F32)
    middle = (level - high).astype(BF16).astype(F32)
    for j, piece in enumerate((high, middle, level - high - middle)):
        stats = jnp.where(lane == 3 * h + j, piece, stats)
    return stats


def attend_kernel(packed, held, sc, patch, q_ref, fo, fm, so, sm, *refs):
    outs = refs[held:]
    b, p = sc[2], patch[0]
    heads = q_ref.shape[1] // HD
    stats = jnp.zeros((q_ref.shape[0], HD), F32)
    for h in range(heads):
        at = slice(h * HD, (h + 1) * HD)
        pieces = [(ref[0, :, at], ref[1, :, at], None) for ref in (fo, fm)]
        pieces += [
            (ref[0, :, at], ref[1, :, at], p == jnp.bitwise_xor(b, j))
            for j, ref in enumerate((so, sm))
        ]
        stats = store_part(outs, h, *weigh(q_ref[:, at], pieces), stats)
    if packed:
        outs[0][:, heads * HD :] = stats.astype(BF16)
    else:
        outs[1][...] = stats


def attend(packed, scalars, patch, q, fo, fm, so, sm, hold=()):
    rows, cols = q.shape
    if packed:
        out_shape = [shaped((rows, cols + HD))]
    else:
        out_shape = [shaped((rows, cols), F32), shaped((rows, HD), F32)]
    return pl.pallas_call(
        functools.partial(attend_kernel, packed, len(hold)),
        in_specs=[SMEM_SPEC] * 2 + [VMEM_SPEC] * 5 + [ANY_SPEC] * len(hold),
        out_specs=[VMEM_SPEC] * len(out_shape),
        out_shape=out_shape,
        compiler_params=params(ATTEND_MIB),
        cost_estimate=cost(5),
        name="attend_other" if packed else "attend_own",
    )(scalars, patch, q, fo, fm, so, sm, *hold)


def attend_stale_kernel(sc, patch, q_ref, fo, fm, stale, o_ref, level_ref, stale_s, sem):
    count = stale.shape[0]
    live = [lax.rem(patch[0] + 1 + i, count) for i in range(count - 1)]
    copies = start_all([(stale.at[j], stale_s.at[i]) for i, j in enumerate(live)], sem)
    wait_all(copies)
    stats = jnp.zeros(level_ref.shape, F32)
    for h in range(q_ref.shape[1] // HD):
        at = slice(h * HD, (h + 1) * HD)
        pieces = [(ref[0, :, at], ref[1, :, at], None) for ref in (fo, fm)]
        pieces += [(stale_s[i, 0, :, at], stale_s[i, 1, :, at], None) for i in range(count - 1)]
        stats = store_part((o_ref, level_ref), h, *weigh(q_ref[:, at], pieces), stats)
    level_ref[...] = stats


def attend_stale(scalars, patch, q, fo, fm, stale):
    rows, cols = q.shape
    return pl.pallas_call(
        attend_stale_kernel,
        in_specs=[SMEM_SPEC] * 2 + [VMEM_SPEC] * 3 + [ANY_SPEC],
        out_specs=[VMEM_SPEC] * 2,
        out_shape=[shaped((rows, cols), F32), shaped((rows, HD), F32)],
        scratch_shapes=[
            pltpu.VMEM((stale.shape[0] - 1,) + stale.shape[1:], BF16),
            pltpu.SemaphoreType.DMA((stale.shape[0] - 1,)),
        ],
        compiler_params=params(ATTEND_MIB),
        cost_estimate=cost(8),
        name="attend_stale",
    )(scalars, patch, q, fo, fm, stale)


def attend_rest_kernel(q_ref, fo, fm, o_ref, level_ref, out_ref):
    for h in range(q_ref.shape[1] // HD):
        at = slice(h * HD, (h + 1) * HD)
        pieces = [(ref[0, :, at], ref[1, :, at], None) for ref in (fo, fm)]
        peak, total, numer = weigh(q_ref[:, at], pieces)
        peak = peak * RATE
        level = level_ref[:, h : h + 1]
        top = jnp.maximum(level, peak)
        a, b = jnp.exp2(level - top), jnp.exp2(peak - top)
        out_ref[:, at] = ((a * o_ref[:, at] + b * numer) / (a + b * total)).astype(BF16)


def attend_rest(q, fo, fm, o, level):
    return pl.pallas_call(
        attend_rest_kernel,
        in_specs=[VMEM_SPEC] * 5,
        out_specs=VMEM_SPEC,
        out_shape=shaped(q.shape),
        compiler_params=params(ATTEND_MIB),
        cost_estimate=cost(3),
        name="attend_rest",
    )(q, fo, fm, o, level)


def merge_kernel(o_ref, level_ref, other_ref, *refs):
    out_ref = refs[-1]
    cols = o_ref.shape[1]
    for h in range(cols // HD):
        at = slice(h * HD, (h + 1) * HD)
        mine = level_ref[:, h : h + 1]
        parts = [
            other_ref[:, cols + 3 * h + j : cols + 3 * h + j + 1].astype(F32) for j in range(3)
        ]
        theirs = parts[0] + parts[1] + parts[2]
        peak = jnp.maximum(mine, theirs)
        a, b = jnp.exp2(mine - peak), jnp.exp2(theirs - peak)
        mixed = (a * o_ref[:, at] + b * other_ref[:, at].astype(F32)) / (a + b)
        out_ref[:, at] = mixed.astype(BF16)


def merge(o, level, other, hold=()):
    return pl.pallas_call(
        merge_kernel,
        in_specs=[VMEM_SPEC] * 3 + [ANY_SPEC] * len(hold),
        out_specs=VMEM_SPEC,
        out_shape=jax.ShapeDtypeStruct(o.shape, BF16),
        compiler_params=params(),
        cost_estimate=cost(12),
        name="merge",
    )(o, level, other, *hold)


def place_kernel(n, sc, *refs):
    u, core = sc[1], lax.rem(sc[2], 2)
    mine, mate, out_ref = refs[:n], refs[n : 2 * n], refs[2 * n]
    rows = mine[0].shape[0] // 2
    for k in range(n):
        for ref, flip in ((mine[k], 0), (mate[k], 1)):
            for z in range(2):
                at = lax.rem(u - k + n, n) * 4 + 2 * z + jnp.bitwise_xor(core, flip)
                at = pl.multiple_of(at * rows, rows)
                out_ref[pl.ds(at, rows), :] = ref[z * rows : (z + 1) * rows, :]


def place(n, scalars, mine, mate):
    rows, cols = mine[0].shape
    return pl.pallas_call(
        functools.partial(place_kernel, n),
        in_specs=[SMEM_SPEC] + [VMEM_SPEC] * (2 * n),
        out_specs=VMEM_SPEC,
        out_shape=shaped((2 * n * rows, cols)),
        compiler_params=params(),
        cost_estimate=cost(0.1),
        name="place",
    )(scalars, *mine, *mate)


def pass_on(x, hold):
    return pl.pallas_call(
        lambda *refs: None,
        in_specs=[ANY_SPEC] * (1 + len(hold)),
        out_specs=ANY_SPEC,
        out_shape=shaped(x.shape, x.dtype),
        input_output_aliases={0: 0},
        compiler_params=params(),
        cost_estimate=cost(0.1),
        name="pass_on",
    )(x, *hold)


def out_cols_kernel(n, last, sc, a0, a1, a2, a3, w_ref, x_ref, gate_ref, *refs):
    u = sc[1]
    depth = a0.shape[1]
    tokens, width = x_ref.shape
    rows = tokens // n
    total = None
    for k, ref in enumerate((a0, a1, a2, a3)):
        at = pl.multiple_of(lax.rem(u - k + n, n) * depth, 128)
        part = jnp.dot(ref[...], w_ref[pl.ds(at, depth), :], preferred_element_type=F32)
        total = part if total is None else total + part
    gate = gate_ref[:, pl.ds(pl.multiple_of(u * width, 128), width)]
    y = (x_ref[...].astype(F32) + gate * total).astype(BF16)
    y_s = refs[-1]
    y_s[...] = y
    cut_into(refs[-n - 1 : -1], y_s, u, n, True)
    if not last:
        enter, next_ref = refs[:2]
        end = sc[0] == sc[3] - 1

        @pl.when(end)
        def _():
            for j in range(n):
                next_ref[j * rows : (j + 1) * rows, :] = enter[:, j * width : (j + 1) * width]

        @pl.when(jnp.logical_not(end))
        def _():
            next_ref[...] = y


def out_cols(n, scalars, pieces, weight, x, gate, enter=None):
    tokens, width = x.shape
    last = enter is None
    outs = [shaped((tokens // n, width))] * n
    return pl.pallas_call(
        functools.partial(out_cols_kernel, n, last),
        in_specs=[SMEM_SPEC] + [VMEM_SPEC] * (n + 3 + (not last)),
        out_specs=[VMEM_SPEC] * (n + (not last)),
        out_shape=outs if last else [shaped(x.shape)] + outs,
        scratch_shapes=[pltpu.VMEM(x.shape, BF16)],
        compiler_params=params(),
        cost_estimate=cost(2),
        name="out_cols",
    )(scalars, *pieces, weight, x, gate, *([] if last else [enter]))


def finish_kernel(n, sc, *refs):
    out_ref = refs[-1]
    width = refs[0].shape[1]
    for t in range(2):
        for k in range(n):
            at = pl.multiple_of(lax.rem(sc[1] + k, n) * width, 128)
            out_ref[0, t, :, pl.ds(at, width)] = refs[t * n + k][...]


def finish(n, scalars, parts):
    rows, width = parts[0].shape
    return pl.pallas_call(
        functools.partial(finish_kernel, n),
        in_specs=[SMEM_SPEC] + [VMEM_SPEC] * len(parts),
        out_specs=VMEM_SPEC,
        out_shape=shaped((1, 2, rows, n * width)),
        compiler_params=params(),
        cost_estimate=cost(1.5),
        name="finish",
    )(scalars, *parts)


def per_device(
    in_flight,
    entering,
    patch_ids,
    timestep,
    time_table,
    mod_weight,
    qkv_weight,
    out_weight,
    stale_cache,
):
    s = lax.axis_index("section")
    u = lax.axis_index("uly")
    b = lax.axis_index("blk")
    n = lax.axis_size("uly")
    section_count = lax.axis_size("section")
    rows, width = in_flight.shape[1:]
    part = width // n
    scalars = jnp.stack([s, u, b, section_count]).astype(jnp.int32)
    patches = [lax.dynamic_slice(patch_ids, (t + section_count - 1 - s,), (1,)) for t in range(2)]

    x_pieces = [in_flight[0]] + [shift(in_flight[0], uly=k) for k in range(1, n)]
    stale_own = jnp.transpose(stale_cache[0], (1, 0, 2))
    stale_mate = shift(stale_own, blk=1)
    tile = modulate(timestep, time_table, jnp.transpose(mod_weight[0], (1, 2, 0)), [])
    tiles = jnp.stack([tile, shift(tile, blk=1)])
    tiles = join(tiles, shift(tiles, blk=2), [stale_mate])
    tiles = [tiles] + [shift(tiles, uly=k) for k in range(1, n)]

    weight = jnp.transpose(qkv_weight[0], (1, 0, 2))
    pair = lax.all_gather(
        out_weight[0], "blk", axis=0, tiled=True, axis_index_groups=[[0, 2], [1, 3]]
    )

    q, fresh, cols, vectors, gate = qkv_first(n, scalars, x_pieces, tiles, weight, [])

    q_other = shift(q, blk=2)
    rest = (fresh, shift(fresh, blk=1), stale_own, stale_mate)
    cut = cut_columns(n, scalars, [pair], [rest[1]])
    mine = [cut[0]] + [shift(cut[k], uly=k) for k in range(1, n)]
    mates = [shift(x, blk=1) for x in mine]
    (for_other,) = attend(True, scalars, patches[0], q_other, *rest)
    o, level = attend(False, scalars, patches[0], q, *rest, hold=[for_other] + mine[1:])
    other = shift(for_other, blk=2)
    w_cols = place(n, scalars, mine, mates)
    attended = merge(o, level, other)
    a_pieces = [attended] + [shift(attended, uly=k) for k in range(1, n)]
    y, *parts = out_cols(n, scalars, a_pieces, w_cols, cols, gate, entering[0])
    parts = [parts[0]] + [shift(parts[k], uly=-k) for k in range(1, n)]
    y = pass_on(shift(y, section=1), parts[1:])
    y_pieces = [y] + [shift(y, uly=k) for k in range(1, n)]
    stale_all = lax.all_gather(pass_on(stale_own, [attended]), "blk", axis=0)
    q, fresh, cols = qkv_next(n, scalars, y_pieces, vectors, weight)

    mate, far = shift(fresh, blk=1), shift(fresh, blk=2)
    o, level = attend_stale(scalars, patches[1], q, fresh, mate, stale_all)
    far = pass_on(far, [level])
    far_mate = shift(far, blk=1)
    attended = attend_rest(q, far, far_mate, o, level)
    a_pieces = [attended] + [shift(attended, uly=k) for k in range(1, n)]
    last = out_cols(n, scalars, a_pieces, w_cols, cols, gate)
    last = [last[0]] + [shift(last[k], uly=-k) for k in range(1, n)]
    return finish(n, scalars, parts + last)


def solution(mesh):
    return jax.shard_map(
        per_device,
        mesh=mesh,
        in_specs=(
            P("section", ("uly", "blk"), None),
            P(None, ("uly", "blk"), None),
            P(),
            P(),
            P(),
            P("section", None, None, ("uly", "blk")),
            P("section", None, None, "uly"),
            P("section", ("uly", "blk"), None),
            P("section", "blk", None, "uly"),
        ),
        out_specs=P("section", None, ("uly", "blk"), None),
        check_vma=False,
    )
```

```python
import functools

import jax
import jax.numpy as jnp
from jax import lax
from jax.experimental import pallas as pl
from jax.experimental.pallas import tpu as pltpu
from jax.sharding import PartitionSpec as P

HD = 128
F32 = jnp.float32
BF16 = jnp.bfloat16
QKV_MIB = 48
ATTEND_MIB = 24
LOG2E = 1.4426950408889634
SMEM_SPEC = pl.BlockSpec(memory_space=pltpu.SMEM)
VMEM_SPEC = pl.BlockSpec(memory_space=pltpu.VMEM)
ANY_SPEC = pl.BlockSpec(memory_space=pl.ANY)


def shift(x, section=0, uly=0, blk=0):
    names = ("section", "uly", "blk")
    moves = (section, uly, blk)
    used = tuple(n for n, m in zip(names, moves) if m)
    sizes = [lax.axis_size(n) for n in used]
    total = 1
    for size in sizes:
        total *= size
    pairs = []
    for source in range(total):
        rest, place = source, []
        for size in reversed(sizes):
            place.insert(0, rest % size)
            rest //= size
        target = 0
        for name, size, at in zip(used, sizes, place):
            move = moves[names.index(name)]
            target = target * size + ((at ^ move) if name == "blk" else (at + move) % size)
        pairs.append((source, target))
    return lax.ppermute(x, used if len(used) > 1 else used[0], pairs)


def params(mib=24):
    return pltpu.CompilerParams(vmem_limit_bytes=mib * 1024 * 1024)


def cost(us):
    return pl.CostEstimate(flops=int(us * 1.1e9), transcendentals=0, bytes_accessed=1024)


def start_all(pairs, sem, first=0):
    copies = [pltpu.make_async_copy(s, d, sem.at[first + i]) for i, (s, d) in enumerate(pairs)]
    for copy in copies:
        copy.start()
    return copies


def wait_all(copies):
    for copy in copies:
        copy.wait()


def modulate_kernel(held, step, table_ref, w_ref, *refs):
    out_ref, table, w, sem = refs[held:]
    copies = start_all([(table_ref, table), (w_ref, w)], sem)
    copies[0].wait()
    at = lax.broadcasted_iota(jnp.int32, table.shape, 0)
    v = jnp.sum(jnp.where(at == step[0], table[...], 0.0), axis=0, keepdims=True)
    activated = (v / (1.0 + jnp.exp(-v))).astype(BF16)
    wide = jnp.broadcast_to(activated, (8, v.shape[1]))
    count, cols = w.shape[:2]
    parts = []
    copies[1].wait()
    for i in range(count):
        part = lax.dot_general(
            wide, w[i], (((1,), (1,)), ((), ())), preferred_element_type=F32
        )[0:1]
        parts += [part[:, :HD], jnp.concatenate([part[:, HD:], part[:, : 2 * HD - cols]], axis=1)]
    parts += [jnp.zeros((8 - len(parts), HD), F32)]
    out_ref[...] = jnp.concatenate(parts, axis=0)


def modulate(timestep, time_table, mod_weight, hold):
    return pl.pallas_call(
        functools.partial(modulate_kernel, len(hold)),
        in_specs=[SMEM_SPEC] + [ANY_SPEC] * (2 + len(hold)),
        out_specs=VMEM_SPEC,
        out_shape=shaped((8, HD), F32),
        scratch_shapes=[
            pltpu.VMEM(time_table.shape, F32),
            pltpu.VMEM(mod_weight.shape, BF16),
            pltpu.SemaphoreType.DMA((2,)),
        ],
        compiler_params=params(QKV_MIB),
        cost_estimate=cost(0.1),
        name="modulate",
    )(timestep, time_table, mod_weight, *hold)


def join_kernel(x_ref, y_ref, *refs):
    count = x_ref.shape[0]
    refs[-1][:count] = x_ref[...]
    refs[-1][count:] = y_ref[...]


def join(x, y, hold):
    return pl.pallas_call(
        join_kernel,
        in_specs=[VMEM_SPEC] * 2 + [ANY_SPEC] * len(hold),
        out_specs=VMEM_SPEC,
        out_shape=shaped((2 * x.shape[0],) + x.shape[1:], x.dtype),
        compiler_params=params(),
        cost_estimate=cost(0.1),
        name="join",
    )(x, y, *hold)


def norm_rows(x, shift_vec, scale_vec):
    center = x - jnp.mean(x, axis=-1, keepdims=True)
    normed = center * lax.rsqrt(jnp.mean(center * center, axis=-1, keepdims=True) + 1e-06)
    return (normed * (1.0 + scale_vec) + shift_vec).astype(BF16)


def norm_heads(part, heads):
    out = []
    for h in range(heads):
        v = part[:, h * HD : (h + 1) * HD]
        out.append(v * lax.rsqrt(jnp.mean(v * v, axis=-1, keepdims=True) + 1e-06))
    return jnp.concatenate(out, axis=1).astype(BF16)


def project(mod_s, w_s, w_copies, q_ref, kv_ref):
    for g in range(3):
        w_copies[g].wait()
        part = jnp.dot(mod_s[...], w_s[g], preferred_element_type=F32)
        heads = part.shape[1] // HD
        if g == 0:
            q_ref[...] = norm_heads(part, heads)
        elif g == 1:
            kv_ref[0] = norm_heads(part, heads)
        else:
            kv_ref[1] = part.astype(BF16)


def qkv_first_kernel(
    n, held, sc, x0, x1, x2, x3, m0, m1, m2, m3, w_ref, *refs
):
    q_ref, kv_ref, cols_ref, vectors_ref, gate_ref, *scratch = refs[held:]
    x_s, mod_s, w_s, tiles, sem = scratch
    u, b = sc[1], sc[2]
    rows = x0.shape[0]
    width = cols_ref.shape[1]
    blocks = m0.shape[0]
    inner = x0.shape[1] // (n * blocks) - HD
    at = [lax.rem(u - k + n, n) for k in range(n)]
    spots = [pl.ds(pl.multiple_of(i * rows, rows), rows) for i in at]
    x_copies = start_all([(r, x_s.at[i]) for r, i in zip((x0, x1, x2, x3), spots)], sem)
    w_copies = start_all([(w_ref.at[g], w_s.at[g]) for g in range(3)], sem, n)
    for i, ref in zip(at, (m0, m1, m2, m3)):
        for j in range(blocks):
            tiles[i * blocks + jnp.bitwise_xor(b, j)] = ref[j]
    for i, ref in enumerate((vectors_ref.at[0:1], vectors_ref.at[1:2], gate_ref)):
        pieces = []
        for j in range(n * blocks):
            pieces += [tiles[j, 2 * i : 2 * i + 1, :], tiles[j, 2 * i + 1 : 2 * i + 2, :inner]]
        ref[...] = jnp.concatenate(pieces, axis=1)
    for copy, i in zip(x_copies, spots):
        copy.wait()
        mod_s[i, :] = norm_rows(x_s[i, :].astype(F32), vectors_ref[0:1, :], vectors_ref[1:2, :])
    cols_ref[...] = x_s[:, pl.ds(pl.multiple_of(u * width, 128), width)]
    project(mod_s, w_s, w_copies, q_ref, kv_ref)


def qkv_next_kernel(n, sc, *refs):
    pieces, refs = refs[: 2 * n], refs[2 * n :]
    vectors, w_ref, q_ref, kv_ref, cols_ref, x_s, mod_s, w_s, sem = refs
    u = sc[1]
    first = sc[0] == 0
    half, width = pieces[0].shape
    rows = x_s.shape[0] // n
    per = half // rows
    by_cols, by_rows = [], []
    for h in range(2):
        for k in range(n):
            ref = pieces[h * n + k]
            i = lax.rem(u - k + n, n)
            at = pl.ds(pl.multiple_of(i * width, 128), width)
            by_cols.append((ref, x_s.at[h * half : (h + 1) * half, at]))
            at = pl.ds(pl.multiple_of(i * rows, rows), rows)
            for j in range(per):
                to = slice((h * per + j) * width, (h * per + j + 1) * width)
                by_rows.append((ref.at[j * rows : (j + 1) * rows, :], x_s.at[at, to]))
    by_cols = [pltpu.make_async_copy(s, d, sem.at[i]) for i, (s, d) in enumerate(by_cols)]
    by_rows = [pltpu.make_async_copy(s, d, sem.at[2 * n + i]) for i, (s, d) in enumerate(by_rows)]

    @pl.when(first)
    def _():
        for copy in by_rows:
            copy.start()

    @pl.when(jnp.logical_not(first))
    def _():
        for copy in by_cols:
            copy.start()

    w_copies = start_all([(w_ref.at[g], w_s.at[g]) for g in range(3)], sem, 2 * n + n * n)

    @pl.when(first)
    def _():
        wait_all(by_rows)

    @pl.when(jnp.logical_not(first))
    def _():
        wait_all(by_cols)

    for r in range(n):
        at = slice(r * rows, (r + 1) * rows)
        mod_s[at, :] = norm_rows(x_s[at, :].astype(F32), vectors[0:1, :], vectors[1:2, :])
    cols_ref[...] = x_s[:, pl.ds(pl.multiple_of(u * width, 128), width)]
    project(mod_s, w_s, w_copies, q_ref, kv_ref)


def shaped(shape, dtype=BF16):
    return jax.ShapeDtypeStruct(shape, dtype)


def qkv_scratch(tokens, weight, sems):
    width = weight.shape[1]
    return [
        pltpu.VMEM((tokens, width), BF16),
        pltpu.VMEM((tokens, width), BF16),
        pltpu.VMEM(weight.shape, BF16),
        pltpu.SemaphoreType.DMA((sems,)),
    ]


def qkv_first(n, scalars, pieces, tiles, weight, hold):
    rows, width = pieces[0].shape
    cols = weight.shape[2]
    tokens = n * rows
    blocks = tiles[0].shape[0]
    scratch = qkv_scratch(tokens, weight, n + 3)
    return pl.pallas_call(
        functools.partial(qkv_first_kernel, n, len(hold)),
        in_specs=[SMEM_SPEC] + [ANY_SPEC] * n + [VMEM_SPEC] * n + [ANY_SPEC] * (1 + len(hold)),
        out_specs=[VMEM_SPEC] * 5,
        out_shape=[
            shaped((tokens, cols)),
            shaped((2, tokens, cols)),
            shaped((tokens, width // n)),
            shaped((2, width), F32),
            shaped((1, width), F32),
        ],
        scratch_shapes=scratch[:3] + [pltpu.VMEM((n * blocks, 8, HD), F32)] + scratch[3:],
        compiler_params=params(QKV_MIB),
        cost_estimate=cost(0.1),
        name="qkv_first",
    )(scalars, *pieces, *tiles, weight, *hold)


def qkv_next(n, scalars, pieces, vectors, weight):
    half, part = pieces[0].shape
    tokens = 2 * half
    cols = weight.shape[2]
    return pl.pallas_call(
        functools.partial(qkv_next_kernel, n),
        in_specs=[SMEM_SPEC] + [ANY_SPEC] * (2 * n) + [VMEM_SPEC, ANY_SPEC],
        out_specs=[VMEM_SPEC] * 3,
        out_shape=[shaped((tokens, cols)), shaped((2, tokens, cols)), shaped((tokens, part))],
        scratch_shapes=qkv_scratch(tokens, weight, 2 * n + n * n + 3),
        compiler_params=params(QKV_MIB),
        cost_estimate=cost(6),
        name="qkv_next",
    )(scalars, *pieces, vectors, weight)


def cut_into(refs, whole, u, n, by_rows):
    for k, ref in enumerate(refs):
        rows, part = ref.shape
        if by_rows:
            at = pl.ds(pl.multiple_of(lax.rem(u - k + n, n) * rows, rows), rows)
            ref[...] = whole[at, :]
        else:
            at = pl.ds(pl.multiple_of(lax.rem(u + k, n) * part, 128), part)
            ref[...] = whole[:, at]


def cut_kernel(n, count, sc, *refs):
    wholes, outs = refs[:count], refs[-n * count :]
    for c in range(count):
        cut_into(outs[c * n : (c + 1) * n], wholes[c], sc[1], n, False)


def cut_columns(n, scalars, wholes, hold):
    outs = []
    for x in wholes:
        outs += [shaped((x.shape[0], x.shape[1] // n))] * n
    return pl.pallas_call(
        functools.partial(cut_kernel, n, len(wholes)),
        in_specs=[SMEM_SPEC] + [VMEM_SPEC] * len(wholes) + [ANY_SPEC] * len(hold),
        out_specs=[VMEM_SPEC] * len(outs),
        out_shape=outs,
        compiler_params=params(),
        cost_estimate=cost(1),
        name="cut_columns",
    )(scalars, *wholes, *hold)


NT = (((1,), (1,)), ((), ()))
RATE = HD ** (-0.5) * LOG2E


def weigh(q, pieces):
    scores = []
    for keys, _, masked in pieces:
        score = lax.dot_general(q, keys, NT, preferred_element_type=F32)
        scores.append(score if masked is None else jnp.where(masked, -1e30, score))
    peak = functools.reduce(jnp.maximum, [jnp.max(s, axis=-1, keepdims=True) for s in scores])
    total = jnp.zeros(peak.shape, F32)
    numer = jnp.zeros(q.shape, F32)
    for s, (_, values, _) in zip(scores, pieces):
        weights = jnp.exp2((s - peak) * RATE)
        total = total + jnp.sum(weights, axis=-1, keepdims=True)
        numer = numer + jnp.dot(weights.astype(BF16), values, preferred_element_type=F32)
    return peak, total, numer


def store_part(refs, h, peak, total, numer, stats):
    at = slice(h * HD, (h + 1) * HD)
    lane = lax.broadcasted_iota(jnp.int32, stats.shape, 1)
    level = peak * RATE + jnp.log2(total)
    if len(refs) == 2:
        refs[0][:, at] = numer / total
        return jnp.where(lane == h, level, stats)
    refs[0][:, at] = (numer / total).astype(BF16)
    high = level.astype(BF16).astype(F32)
    middle = (level - high).astype(BF16).astype(F32)
    for j, piece in enumerate((high, middle, level - high - middle)):
        stats = jnp.where(lane == 3 * h + j, piece, stats)
    return stats


def attend_kernel(packed, held, sc, patch, q_ref, fo, fm, so, sm, *refs):
    outs = refs[held:]
    b, p = sc[2], patch[0]
    heads = q_ref.shape[1] // HD
    stats = jnp.zeros((q_ref.shape[0], HD), F32)
    for h in range(heads):
        at = slice(h * HD, (h + 1) * HD)
        pieces = [(ref[0, :, at], ref[1, :, at], None) for ref in (fo, fm)]
        pieces += [
            (ref[0, :, at], ref[1, :, at], p == jnp.bitwise_xor(b, j))
            for j, ref in enumerate((so, sm))
        ]
        stats = store_part(outs, h, *weigh(q_ref[:, at], pieces), stats)
    if packed:
        outs[0][:, heads * HD :] = stats.astype(BF16)
    else:
        outs[1][...] = stats


def attend(packed, scalars, patch, q, fo, fm, so, sm, hold=()):
    rows, cols = q.shape
    if packed:
        out_shape = [shaped((rows, cols + HD))]
    else:
        out_shape = [shaped((rows, cols), F32), shaped((rows, HD), F32)]
    return pl.pallas_call(
        functools.partial(attend_kernel, packed, len(hold)),
        in_specs=[SMEM_SPEC] * 2 + [VMEM_SPEC] * 5 + [ANY_SPEC] * len(hold),
        out_specs=[VMEM_SPEC] * len(out_shape),
        out_shape=out_shape,
        compiler_params=params(ATTEND_MIB),
        cost_estimate=cost(5),
        name="attend_other" if packed else "attend_own",
    )(scalars, patch, q, fo, fm, so, sm, *hold)


def attend_stale_kernel(sc, patch, q_ref, fo, fm, stale, o_ref, level_ref, stale_s, sem):
    count = stale.shape[0]
    live = [lax.rem(patch[0] + 1 + i, count) for i in range(count - 1)]
    copies = start_all([(stale.at[j], stale_s.at[i]) for i, j in enumerate(live)], sem)
    wait_all(copies)
    stats = jnp.zeros(level_ref.shape, F32)
    for h in range(q_ref.shape[1] // HD):
        at = slice(h * HD, (h + 1) * HD)
        pieces = [(ref[0, :, at], ref[1, :, at], None) for ref in (fo, fm)]
        pieces += [(stale_s[i, 0, :, at], stale_s[i, 1, :, at], None) for i in range(count - 1)]
        stats = store_part((o_ref, level_ref), h, *weigh(q_ref[:, at], pieces), stats)
    level_ref[...] = stats


def attend_stale(scalars, patch, q, fo, fm, stale):
    rows, cols = q.shape
    return pl.pallas_call(
        attend_stale_kernel,
        in_specs=[SMEM_SPEC] * 2 + [VMEM_SPEC] * 3 + [ANY_SPEC],
        out_specs=[VMEM_SPEC] * 2,
        out_shape=[shaped((rows, cols), F32), shaped((rows, HD), F32)],
        scratch_shapes=[
            pltpu.VMEM((stale.shape[0] - 1,) + stale.shape[1:], BF16),
            pltpu.SemaphoreType.DMA((stale.shape[0] - 1,)),
        ],
        compiler_params=params(ATTEND_MIB),
        cost_estimate=cost(8),
        name="attend_stale",
    )(scalars, patch, q, fo, fm, stale)


def attend_rest_kernel(q_ref, fo, fm, o_ref, level_ref, out_ref):
    for h in range(q_ref.shape[1] // HD):
        at = slice(h * HD, (h + 1) * HD)
        pieces = [(ref[0, :, at], ref[1, :, at], None) for ref in (fo, fm)]
        peak, total, numer = weigh(q_ref[:, at], pieces)
        peak = peak * RATE
        level = level_ref[:, h : h + 1]
        top = jnp.maximum(level, peak)
        a, b = jnp.exp2(level - top), jnp.exp2(peak - top)
        out_ref[:, at] = ((a * o_ref[:, at] + b * numer) / (a + b * total)).astype(BF16)


def attend_rest(q, fo, fm, o, level):
    return pl.pallas_call(
        attend_rest_kernel,
        in_specs=[VMEM_SPEC] * 5,
        out_specs=VMEM_SPEC,
        out_shape=shaped(q.shape),
        compiler_params=params(ATTEND_MIB),
        cost_estimate=cost(3),
        name="attend_rest",
    )(q, fo, fm, o, level)


def merge_kernel(o_ref, level_ref, other_ref, *refs):
    out_ref = refs[-1]
    cols = o_ref.shape[1]
    for h in range(cols // HD):
        at = slice(h * HD, (h + 1) * HD)
        mine = level_ref[:, h : h + 1]
        parts = [
            other_ref[:, cols + 3 * h + j : cols + 3 * h + j + 1].astype(F32) for j in range(3)
        ]
        theirs = parts[0] + parts[1] + parts[2]
        peak = jnp.maximum(mine, theirs)
        a, b = jnp.exp2(mine - peak), jnp.exp2(theirs - peak)
        mixed = (a * o_ref[:, at] + b * other_ref[:, at].astype(F32)) / (a + b)
        out_ref[:, at] = mixed.astype(BF16)


def merge(o, level, other, hold=()):
    return pl.pallas_call(
        merge_kernel,
        in_specs=[VMEM_SPEC] * 3 + [ANY_SPEC] * len(hold),
        out_specs=VMEM_SPEC,
        out_shape=jax.ShapeDtypeStruct(o.shape, BF16),
        compiler_params=params(),
        cost_estimate=cost(12),
        name="merge",
    )(o, level, other, *hold)


def place_kernel(n, sc, *refs):
    u, core = sc[1], lax.rem(sc[2], 2)
    mine, mate, out_ref = refs[:n], refs[n : 2 * n], refs[2 * n]
    rows = mine[0].shape[0] // 2
    for k in range(n):
        for ref, flip in ((mine[k], 0), (mate[k], 1)):
            for z in range(2):
                at = lax.rem(u - k + n, n) * 4 + 2 * z + jnp.bitwise_xor(core, flip)
                at = pl.multiple_of(at * rows, rows)
                out_ref[pl.ds(at, rows), :] = ref[z * rows : (z + 1) * rows, :]


def place(n, scalars, mine, mate):
    rows, cols = mine[0].shape
    return pl.pallas_call(
        functools.partial(place_kernel, n),
        in_specs=[SMEM_SPEC] + [VMEM_SPEC] * (2 * n),
        out_specs=VMEM_SPEC,
        out_shape=shaped((2 * n * rows, cols)),
        compiler_params=params(),
        cost_estimate=cost(0.1),
        name="place",
    )(scalars, *mine, *mate)


def pass_on(x, hold):
    return pl.pallas_call(
        lambda *refs: None,
        in_specs=[ANY_SPEC] * (1 + len(hold)),
        out_specs=ANY_SPEC,
        out_shape=shaped(x.shape, x.dtype),
        input_output_aliases={0: 0},
        compiler_params=params(),
        cost_estimate=cost(0.1),
        name="pass_on",
    )(x, *hold)


def out_cols_kernel(n, last, sc, a0, a1, a2, a3, w_ref, x_ref, gate_ref, *refs):
    u = sc[1]
    depth = a0.shape[1]
    tokens, width = x_ref.shape
    rows = tokens // n
    total = None
    for k, ref in enumerate((a0, a1, a2, a3)):
        at = pl.multiple_of(lax.rem(u - k + n, n) * depth, 128)
        part = jnp.dot(ref[...], w_ref[pl.ds(at, depth), :], preferred_element_type=F32)
        total = part if total is None else total + part
    gate = gate_ref[:, pl.ds(pl.multiple_of(u * width, 128), width)]
    y = (x_ref[...].astype(F32) + gate * total).astype(BF16)
    y_s = refs[-1]
    y_s[...] = y
    cut_into(refs[-n - 1 : -1], y_s, u, n, True)
    if not last:
        enter, next_refs = refs[0], refs[1:3]
        half = tokens // 2
        end = sc[0] == sc[3] - 1

        @pl.when(end)
        def _():
            for j in range(n):
                to = next_refs[j * rows // half]
                at = j * rows % half
                to[at : at + rows, :] = enter[:, j * width : (j + 1) * width]

        @pl.when(jnp.logical_not(end))
        def _():
            for h in range(2):
                next_refs[h][...] = y[h * half : (h + 1) * half]


def out_cols(n, scalars, pieces, weight, x, gate, enter=None):
    tokens, width = x.shape
    last = enter is None
    outs = [shaped((tokens // n, width))] * n
    return pl.pallas_call(
        functools.partial(out_cols_kernel, n, last),
        in_specs=[SMEM_SPEC] + [VMEM_SPEC] * (n + 3 + (not last)),
        out_specs=[VMEM_SPEC] * (n + 2 * (not last)),
        out_shape=outs if last else [shaped((tokens // 2, width))] * 2 + outs,
        scratch_shapes=[pltpu.VMEM(x.shape, BF16)],
        compiler_params=params(),
        cost_estimate=cost(2),
        name="out_cols",
    )(scalars, *pieces, weight, x, gate, *([] if last else [enter]))


def finish_kernel(n, sc, *refs):
    out_ref = refs[-1]
    width = refs[0].shape[1]
    for t in range(2):
        for k in range(n):
            at = pl.multiple_of(lax.rem(sc[1] + k, n) * width, 128)
            out_ref[0, t, :, pl.ds(at, width)] = refs[t * n + k][...]


def finish(n, scalars, parts):
    rows, width = parts[0].shape
    return pl.pallas_call(
        functools.partial(finish_kernel, n),
        in_specs=[SMEM_SPEC] + [VMEM_SPEC] * len(parts),
        out_specs=VMEM_SPEC,
        out_shape=shaped((1, 2, rows, n * width)),
        compiler_params=params(),
        cost_estimate=cost(1.5),
        name="finish",
    )(scalars, *parts)


def per_device(
    in_flight,
    entering,
    patch_ids,
    timestep,
    time_table,
    mod_weight,
    qkv_weight,
    out_weight,
    stale_cache,
):
    s = lax.axis_index("section")
    u = lax.axis_index("uly")
    b = lax.axis_index("blk")
    n = lax.axis_size("uly")
    section_count = lax.axis_size("section")
    rows, width = in_flight.shape[1:]
    part = width // n
    scalars = jnp.stack([s, u, b, section_count]).astype(jnp.int32)
    patches = [lax.dynamic_slice(patch_ids, (t + section_count - 1 - s,), (1,)) for t in range(2)]

    x_pieces = [in_flight[0]] + [shift(in_flight[0], uly=k) for k in range(1, n)]
    stale_own = jnp.transpose(stale_cache[0], (1, 0, 2))
    stale_mate = shift(stale_own, blk=1)
    tile = modulate(timestep, time_table, jnp.transpose(mod_weight[0], (1, 2, 0)), [])
    tiles = jnp.stack([tile, shift(tile, blk=1)])
    tiles = join(tiles, shift(tiles, blk=2), [stale_mate])
    tiles = [tiles] + [shift(tiles, uly=k) for k in range(1, n)]

    weight = jnp.transpose(qkv_weight[0], (1, 0, 2))
    pair = lax.all_gather(
        out_weight[0], "blk", axis=0, tiled=True, axis_index_groups=[[0, 2], [1, 3]]
    )

    q, fresh, cols, vectors, gate = qkv_first(n, scalars, x_pieces, tiles, weight, [])

    q_other = shift(q, blk=2)
    rest = (fresh, shift(fresh, blk=1), stale_own, stale_mate)
    cut = cut_columns(n, scalars, [pair], [rest[1]])
    mine = [cut[0]] + [shift(cut[k], uly=k) for k in range(1, n)]
    mates = [shift(x, blk=1) for x in mine]
    (for_other,) = attend(True, scalars, patches[0], q_other, *rest)
    stale_own = pass_on(stale_own, [for_other] + mine[1:])
    stale_all = lax.all_gather(stale_own, "blk", axis=0)
    o, level = attend(False, scalars, patches[0], q, *rest[:2], stale_own, stale_mate)
    other = shift(for_other, blk=2)
    w_cols = place(n, scalars, mine, mates)
    attended = merge(o, level, other)
    a_pieces = [attended] + [shift(attended, uly=k) for k in range(1, n)]
    half_a, half_b, *parts = out_cols(n, scalars, a_pieces, w_cols, cols, gate, entering[0])
    half_a, half_b = shift(half_a, section=1), shift(half_b, section=1)
    parts = [parts[0]] + [shift(parts[k], uly=-k) for k in range(1, n)]
    half_b = pass_on(half_b, parts[1:])
    left_a, right_a = shift(half_a, uly=1), shift(half_a, uly=-1)
    left_b, right_b = shift(half_b, uly=1), shift(half_b, uly=-1)
    across_a, across_b = shift(left_a, uly=1), shift(right_b, uly=-1)
    y_pieces = [half_a, left_a, across_a, right_a, half_b, left_b, across_b, right_b]
    q, fresh, cols = qkv_next(n, scalars, y_pieces, vectors, weight)

    mate, far = shift(fresh, blk=1), shift(fresh, blk=2)
    o, level = attend_stale(scalars, patches[1], q, fresh, mate, stale_all)
    far = pass_on(far, [level])
    far_mate = shift(far, blk=1)
    attended = attend_rest(q, far, far_mate, o, level)
    a_pieces = [attended] + [shift(attended, uly=k) for k in range(1, n)]
    last = out_cols(n, scalars, a_pieces, w_cols, cols, gate)
    last = [last[0]] + [shift(last[k], uly=-k) for k in range(1, n)]
    return finish(n, scalars, parts + last)


def solution(mesh):
    return jax.shard_map(
        per_device,
        mesh=mesh,
        in_specs=(
            P("section", ("uly", "blk"), None),
            P(None, ("uly", "blk"), None),
            P(),
            P(),
            P(),
            P("section", None, None, ("uly", "blk")),
            P("section", None, None, "uly"),
            P("section", ("uly", "blk"), None),
            P("section", "blk", None, "uly"),
        ),
        out_specs=P("section", None, ("uly", "blk"), None),
        check_vma=False,
    )
```

```python
import functools

import jax
import jax.numpy as jnp
from jax import lax
from jax.experimental import pallas as pl
from jax.experimental.pallas import tpu as pltpu
from jax.sharding import PartitionSpec as P

HD = 128
F32 = jnp.float32
BF16 = jnp.bfloat16
QKV_MIB = 48
ATTEND_MIB = 24
LOG2E = 1.4426950408889634
SMEM_SPEC = pl.BlockSpec(memory_space=pltpu.SMEM)
VMEM_SPEC = pl.BlockSpec(memory_space=pltpu.VMEM)
ANY_SPEC = pl.BlockSpec(memory_space=pl.ANY)


def shift(x, section=0, uly=0, blk=0):
    names = ("section", "uly", "blk")
    moves = (section, uly, blk)
    used = tuple(n for n, m in zip(names, moves) if m)
    sizes = [lax.axis_size(n) for n in used]
    total = 1
    for size in sizes:
        total *= size
    pairs = []
    for source in range(total):
        rest, place = source, []
        for size in reversed(sizes):
            place.insert(0, rest % size)
            rest //= size
        target = 0
        for name, size, at in zip(used, sizes, place):
            move = moves[names.index(name)]
            target = target * size + ((at ^ move) if name == "blk" else (at + move) % size)
        pairs.append((source, target))
    return lax.ppermute(x, used if len(used) > 1 else used[0], pairs)


def params(mib=24):
    return pltpu.CompilerParams(vmem_limit_bytes=mib * 1024 * 1024)


def cost(us):
    return pl.CostEstimate(flops=int(us * 1.1e9), transcendentals=0, bytes_accessed=1024)


def located(kernel, *static):
    def body(*refs):
        place = [lax.axis_index(name) for name in ("section", "uly", "blk")]
        return kernel(*static, place + [lax.axis_size("section")], *refs)

    return body


def start_all(pairs, sem, first=0):
    copies = [pltpu.make_async_copy(s, d, sem.at[first + i]) for i, (s, d) in enumerate(pairs)]
    for copy in copies:
        copy.start()
    return copies


def wait_all(copies):
    for copy in copies:
        copy.wait()


def modulate_kernel(held, step, table_ref, w_ref, *refs):
    out_ref, table, w, sem = refs[held:]
    copies = start_all([(table_ref, table), (w_ref, w)], sem)
    copies[0].wait()
    at = lax.broadcasted_iota(jnp.int32, table.shape, 0)
    v = jnp.sum(jnp.where(at == step[0], table[...], 0.0), axis=0, keepdims=True)
    activated = (v / (1.0 + jnp.exp(-v))).astype(BF16)
    wide = jnp.broadcast_to(activated, (8, v.shape[1]))
    count, cols = w.shape[:2]
    parts = []
    copies[1].wait()
    for i in range(count):
        part = lax.dot_general(
            wide, w[i], (((1,), (1,)), ((), ())), preferred_element_type=F32
        )[0:1]
        parts += [part[:, :HD], jnp.concatenate([part[:, HD:], part[:, : 2 * HD - cols]], axis=1)]
    parts += [jnp.zeros((8 - len(parts), HD), F32)]
    out_ref[...] = jnp.concatenate(parts, axis=0)


def modulate(timestep, time_table, mod_weight, hold):
    return pl.pallas_call(
        functools.partial(modulate_kernel, len(hold)),
        in_specs=[SMEM_SPEC] + [ANY_SPEC] * (2 + len(hold)),
        out_specs=VMEM_SPEC,
        out_shape=shaped((8, HD), F32),
        scratch_shapes=[
            pltpu.VMEM(time_table.shape, F32),
            pltpu.VMEM(mod_weight.shape, BF16),
            pltpu.SemaphoreType.DMA((2,)),
        ],
        compiler_params=params(QKV_MIB),
        cost_estimate=cost(0.1),
        name="modulate",
    )(timestep, time_table, mod_weight, *hold)


def join_kernel(x_ref, y_ref, *refs):
    count = x_ref.shape[0]
    refs[-1][:count] = x_ref[...]
    refs[-1][count:] = y_ref[...]


def join(x, y, hold):
    return pl.pallas_call(
        join_kernel,
        in_specs=[VMEM_SPEC] * 2 + [ANY_SPEC] * len(hold),
        out_specs=VMEM_SPEC,
        out_shape=shaped((2 * x.shape[0],) + x.shape[1:], x.dtype),
        compiler_params=params(),
        cost_estimate=cost(0.1),
        name="join",
    )(x, y, *hold)


def norm_rows(x, shift_vec, scale_vec):
    center = x - jnp.mean(x, axis=-1, keepdims=True)
    normed = center * lax.rsqrt(jnp.mean(center * center, axis=-1, keepdims=True) + 1e-06)
    return (normed * (1.0 + scale_vec) + shift_vec).astype(BF16)


def norm_heads(part, heads):
    out = []
    for h in range(heads):
        v = part[:, h * HD : (h + 1) * HD]
        out.append(v * lax.rsqrt(jnp.mean(v * v, axis=-1, keepdims=True) + 1e-06))
    return jnp.concatenate(out, axis=1).astype(BF16)


def project(mod_s, w_s, w_copies, q_ref, kv_ref):
    for g in range(3):
        w_copies[g].wait()
        part = jnp.dot(mod_s[...], w_s[g], preferred_element_type=F32)
        heads = part.shape[1] // HD
        if g == 0:
            q_ref[...] = norm_heads(part, heads)
        elif g == 1:
            kv_ref[0] = norm_heads(part, heads)
        else:
            kv_ref[1] = part.astype(BF16)


def qkv_first_kernel(
    n, held, sc, x0, x1, x2, x3, m0, m1, m2, m3, w_ref, *refs
):
    q_ref, kv_ref, cols_ref, vectors_ref, gate_ref, *scratch = refs[held:]
    x_s, mod_s, w_s, tiles, sem = scratch
    u, b = sc[1], sc[2]
    rows = x0.shape[0]
    width = cols_ref.shape[1]
    blocks = m0.shape[0]
    inner = x0.shape[1] // (n * blocks) - HD
    at = [lax.rem(u - k + n, n) for k in range(n)]
    spots = [pl.ds(pl.multiple_of(i * rows, rows), rows) for i in at]
    x_copies = start_all([(r, x_s.at[i]) for r, i in zip((x0, x1, x2, x3), spots)], sem)
    w_copies = start_all([(w_ref.at[g], w_s.at[g]) for g in range(3)], sem, n)
    for i, ref in zip(at, (m0, m1, m2, m3)):
        for j in range(blocks):
            tiles[i * blocks + jnp.bitwise_xor(b, j)] = ref[j]
    for i, ref in enumerate((vectors_ref.at[0:1], vectors_ref.at[1:2], gate_ref)):
        pieces = []
        for j in range(n * blocks):
            pieces += [tiles[j, 2 * i : 2 * i + 1, :], tiles[j, 2 * i + 1 : 2 * i + 2, :inner]]
        ref[...] = jnp.concatenate(pieces, axis=1)
    for copy, i in zip(x_copies, spots):
        copy.wait()
        mod_s[i, :] = norm_rows(x_s[i, :].astype(F32), vectors_ref[0:1, :], vectors_ref[1:2, :])
    cols_ref[...] = x_s[:, pl.ds(pl.multiple_of(u * width, 128), width)]
    project(mod_s, w_s, w_copies, q_ref, kv_ref)


def qkv_next_kernel(n, sc, *refs):
    pieces, refs = refs[: 2 * n], refs[2 * n :]
    vectors, w_ref, q_ref, kv_ref, cols_ref, x_s, mod_s, w_s, sem = refs
    u = sc[1]
    first = sc[0] == 0
    half, width = pieces[0].shape
    rows = x_s.shape[0] // n
    per = half // rows
    by_cols, by_rows = [], []
    for h in range(2):
        for k in range(n):
            ref = pieces[h * n + k]
            i = lax.rem(u - k + n, n)
            at = pl.ds(pl.multiple_of(i * width, 128), width)
            by_cols.append((ref, x_s.at[h * half : (h + 1) * half, at]))
            at = pl.ds(pl.multiple_of(i * rows, rows), rows)
            for j in range(per):
                to = slice((h * per + j) * width, (h * per + j + 1) * width)
                by_rows.append((ref.at[j * rows : (j + 1) * rows, :], x_s.at[at, to]))
    by_cols = [pltpu.make_async_copy(s, d, sem.at[i]) for i, (s, d) in enumerate(by_cols)]
    by_rows = [pltpu.make_async_copy(s, d, sem.at[2 * n + i]) for i, (s, d) in enumerate(by_rows)]

    @pl.when(first)
    def _():
        for copy in by_rows:
            copy.start()

    @pl.when(jnp.logical_not(first))
    def _():
        for copy in by_cols:
            copy.start()

    w_copies = start_all([(w_ref.at[g], w_s.at[g]) for g in range(3)], sem, 2 * n + n * n)

    @pl.when(first)
    def _():
        wait_all(by_rows)

    @pl.when(jnp.logical_not(first))
    def _():
        wait_all(by_cols)

    for r in range(n):
        at = slice(r * rows, (r + 1) * rows)
        mod_s[at, :] = norm_rows(x_s[at, :].astype(F32), vectors[0:1, :], vectors[1:2, :])
    cols_ref[...] = x_s[:, pl.ds(pl.multiple_of(u * width, 128), width)]
    project(mod_s, w_s, w_copies, q_ref, kv_ref)


def shaped(shape, dtype=BF16):
    return jax.ShapeDtypeStruct(shape, dtype)


def qkv_scratch(tokens, weight, sems):
    width = weight.shape[1]
    return [
        pltpu.VMEM((tokens, width), BF16),
        pltpu.VMEM((tokens, width), BF16),
        pltpu.VMEM(weight.shape, BF16),
        pltpu.SemaphoreType.DMA((sems,)),
    ]


def qkv_first(n, pieces, tiles, weight, hold):
    rows, width = pieces[0].shape
    cols = weight.shape[2]
    tokens = n * rows
    blocks = tiles[0].shape[0]
    scratch = qkv_scratch(tokens, weight, n + 3)
    return pl.pallas_call(
        located(qkv_first_kernel, n, len(hold)),
        in_specs=[ANY_SPEC] * n + [VMEM_SPEC] * n + [ANY_SPEC] * (1 + len(hold)),
        out_specs=[VMEM_SPEC] * 5,
        out_shape=[
            shaped((tokens, cols)),
            shaped((2, tokens, cols)),
            shaped((tokens, width // n)),
            shaped((2, width), F32),
            shaped((1, width), F32),
        ],
        scratch_shapes=scratch[:3] + [pltpu.VMEM((n * blocks, 8, HD), F32)] + scratch[3:],
        compiler_params=params(QKV_MIB),
        cost_estimate=cost(0.1),
        name="qkv_first",
    )(*pieces, *tiles, weight, *hold)


def qkv_next(n, pieces, vectors, weight):
    half, part = pieces[0].shape
    tokens = 2 * half
    cols = weight.shape[2]
    return pl.pallas_call(
        located(qkv_next_kernel, n),
        in_specs=[ANY_SPEC] * (2 * n) + [VMEM_SPEC, ANY_SPEC],
        out_specs=[VMEM_SPEC] * 3,
        out_shape=[shaped((tokens, cols)), shaped((2, tokens, cols)), shaped((tokens, part))],
        scratch_shapes=qkv_scratch(tokens, weight, 2 * n + n * n + 3),
        compiler_params=params(QKV_MIB),
        cost_estimate=cost(6),
        name="qkv_next",
    )(*pieces, vectors, weight)


def cut_into(refs, whole, u, n, by_rows):
    for k, ref in enumerate(refs):
        rows, part = ref.shape
        if by_rows:
            at = pl.ds(pl.multiple_of(lax.rem(u - k + n, n) * rows, rows), rows)
            ref[...] = whole[at, :]
        else:
            at = pl.ds(pl.multiple_of(lax.rem(u + k, n) * part, 128), part)
            ref[...] = whole[:, at]


def cut_kernel(n, count, sc, *refs):
    wholes, outs = refs[:count], refs[-n * count :]
    for c in range(count):
        cut_into(outs[c * n : (c + 1) * n], wholes[c], sc[1], n, False)


def cut_columns(n, wholes, hold):
    outs = []
    for x in wholes:
        outs += [shaped((x.shape[0], x.shape[1] // n))] * n
    return pl.pallas_call(
        located(cut_kernel, n, len(wholes)),
        in_specs=[VMEM_SPEC] * len(wholes) + [ANY_SPEC] * len(hold),
        out_specs=[VMEM_SPEC] * len(outs),
        out_shape=outs,
        compiler_params=params(),
        cost_estimate=cost(1),
        name="cut_columns",
    )(*wholes, *hold)


NT = (((1,), (1,)), ((), ()))
RATE = HD ** (-0.5) * LOG2E


def weigh(q, pieces):
    scores = []
    for keys, _, masked in pieces:
        score = lax.dot_general(q, keys, NT, preferred_element_type=F32)
        scores.append(score if masked is None else jnp.where(masked, -1e30, score))
    peak = functools.reduce(jnp.maximum, [jnp.max(s, axis=-1, keepdims=True) for s in scores])
    total = jnp.zeros(peak.shape, F32)
    numer = jnp.zeros(q.shape, F32)
    for s, (_, values, _) in zip(scores, pieces):
        weights = jnp.exp2((s - peak) * RATE)
        total = total + jnp.sum(weights, axis=-1, keepdims=True)
        numer = numer + jnp.dot(weights.astype(BF16), values, preferred_element_type=F32)
    return peak, total, numer


def store_part(refs, h, peak, total, numer, stats):
    at = slice(h * HD, (h + 1) * HD)
    lane = lax.broadcasted_iota(jnp.int32, stats.shape, 1)
    level = peak * RATE + jnp.log2(total)
    if len(refs) == 2:
        refs[0][:, at] = numer / total
        return jnp.where(lane == h, level, stats)
    refs[0][:, at] = (numer / total).astype(BF16)
    high = level.astype(BF16).astype(F32)
    middle = (level - high).astype(BF16).astype(F32)
    for j, piece in enumerate((high, middle, level - high - middle)):
        stats = jnp.where(lane == 3 * h + j, piece, stats)
    return stats


def attend_kernel(packed, held, sc, patch, q_ref, fo, fm, so, sm, *refs):
    outs = refs[held:]
    b, p = sc[2], patch[sc[3] - 1 - sc[0]]
    heads = q_ref.shape[1] // HD
    stats = jnp.zeros((q_ref.shape[0], HD), F32)
    for h in range(heads):
        at = slice(h * HD, (h + 1) * HD)
        pieces = [(ref[0, :, at], ref[1, :, at], None) for ref in (fo, fm)]
        pieces += [
            (ref[0, :, at], ref[1, :, at], p == jnp.bitwise_xor(b, j))
            for j, ref in enumerate((so, sm))
        ]
        stats = store_part(outs, h, *weigh(q_ref[:, at], pieces), stats)
    if packed:
        outs[0][:, heads * HD :] = stats.astype(BF16)
    else:
        outs[1][...] = stats


def attend(packed, patch, q, fo, fm, so, sm, hold=()):
    rows, cols = q.shape
    if packed:
        out_shape = [shaped((rows, cols + HD))]
    else:
        out_shape = [shaped((rows, cols), F32), shaped((rows, HD), F32)]
    return pl.pallas_call(
        located(attend_kernel, packed, len(hold)),
        in_specs=[SMEM_SPEC] + [VMEM_SPEC] * 5 + [ANY_SPEC] * len(hold),
        out_specs=[VMEM_SPEC] * len(out_shape),
        out_shape=out_shape,
        compiler_params=params(ATTEND_MIB),
        cost_estimate=cost(5),
        name="attend_other" if packed else "attend_own",
    )(patch, q, fo, fm, so, sm, *hold)


def attend_stale_kernel(sc, patch, q_ref, fo, fm, stale, o_ref, level_ref, stale_s, sem):
    count = stale.shape[0]
    live = [lax.rem(patch[sc[3] - sc[0]] + 1 + i, count) for i in range(count - 1)]
    copies = start_all([(stale.at[j], stale_s.at[i]) for i, j in enumerate(live)], sem)
    wait_all(copies)
    stats = jnp.zeros(level_ref.shape, F32)
    for h in range(q_ref.shape[1] // HD):
        at = slice(h * HD, (h + 1) * HD)
        pieces = [(ref[0, :, at], ref[1, :, at], None) for ref in (fo, fm)]
        pieces += [(stale_s[i, 0, :, at], stale_s[i, 1, :, at], None) for i in range(count - 1)]
        stats = store_part((o_ref, level_ref), h, *weigh(q_ref[:, at], pieces), stats)
    level_ref[...] = stats


def attend_stale(patch, q, fo, fm, stale):
    rows, cols = q.shape
    return pl.pallas_call(
        located(attend_stale_kernel),
        in_specs=[SMEM_SPEC] + [VMEM_SPEC] * 3 + [ANY_SPEC],
        out_specs=[VMEM_SPEC] * 2,
        out_shape=[shaped((rows, cols), F32), shaped((rows, HD), F32)],
        scratch_shapes=[
            pltpu.VMEM((stale.shape[0] - 1,) + stale.shape[1:], BF16),
            pltpu.SemaphoreType.DMA((stale.shape[0] - 1,)),
        ],
        compiler_params=params(ATTEND_MIB),
        cost_estimate=cost(8),
        name="attend_stale",
    )(patch, q, fo, fm, stale)


def attend_rest_kernel(q_ref, fo, fm, o_ref, level_ref, out_ref):
    for h in range(q_ref.shape[1] // HD):
        at = slice(h * HD, (h + 1) * HD)
        pieces = [(ref[0, :, at], ref[1, :, at], None) for ref in (fo, fm)]
        peak, total, numer = weigh(q_ref[:, at], pieces)
        peak = peak * RATE
        level = level_ref[:, h : h + 1]
        top = jnp.maximum(level, peak)
        a, b = jnp.exp2(level - top), jnp.exp2(peak - top)
        out_ref[:, at] = ((a * o_ref[:, at] + b * numer) / (a + b * total)).astype(BF16)


def attend_rest(q, fo, fm, o, level):
    return pl.pallas_call(
        attend_rest_kernel,
        in_specs=[VMEM_SPEC] * 5,
        out_specs=VMEM_SPEC,
        out_shape=shaped(q.shape),
        compiler_params=params(ATTEND_MIB),
        cost_estimate=cost(3),
        name="attend_rest",
    )(q, fo, fm, o, level)


def merge_kernel(o_ref, level_ref, other_ref, *refs):
    out_ref = refs[-1]
    cols = o_ref.shape[1]
    for h in range(cols // HD):
        at = slice(h * HD, (h + 1) * HD)
        mine = level_ref[:, h : h + 1]
        parts = [
            other_ref[:, cols + 3 * h + j : cols + 3 * h + j + 1].astype(F32) for j in range(3)
        ]
        theirs = parts[0] + parts[1] + parts[2]
        peak = jnp.maximum(mine, theirs)
        a, b = jnp.exp2(mine - peak), jnp.exp2(theirs - peak)
        mixed = (a * o_ref[:, at] + b * other_ref[:, at].astype(F32)) / (a + b)
        out_ref[:, at] = mixed.astype(BF16)


def merge(o, level, other, hold=()):
    return pl.pallas_call(
        merge_kernel,
        in_specs=[VMEM_SPEC] * 3 + [ANY_SPEC] * len(hold),
        out_specs=VMEM_SPEC,
        out_shape=jax.ShapeDtypeStruct(o.shape, BF16),
        compiler_params=params(),
        cost_estimate=cost(12),
        name="merge",
    )(o, level, other, *hold)


def place_kernel(n, sc, *refs):
    u, core = sc[1], lax.rem(sc[2], 2)
    mine, mate, out_ref = refs[:n], refs[n : 2 * n], refs[2 * n]
    rows = mine[0].shape[0] // 2
    for k in range(n):
        for ref, flip in ((mine[k], 0), (mate[k], 1)):
            for z in range(2):
                at = lax.rem(u - k + n, n) * 4 + 2 * z + jnp.bitwise_xor(core, flip)
                at = pl.multiple_of(at * rows, rows)
                out_ref[pl.ds(at, rows), :] = ref[z * rows : (z + 1) * rows, :]


def place(n, mine, mate):
    rows, cols = mine[0].shape
    return pl.pallas_call(
        located(place_kernel, n),
        in_specs=[VMEM_SPEC] * (2 * n),
        out_specs=VMEM_SPEC,
        out_shape=shaped((2 * n * rows, cols)),
        compiler_params=params(),
        cost_estimate=cost(0.1),
        name="place",
    )(*mine, *mate)


def pass_on(x, hold):
    return pl.pallas_call(
        lambda *refs: None,
        in_specs=[ANY_SPEC] * (1 + len(hold)),
        out_specs=ANY_SPEC,
        out_shape=shaped(x.shape, x.dtype),
        input_output_aliases={0: 0},
        compiler_params=params(),
        cost_estimate=cost(0.1),
        name="pass_on",
    )(x, *hold)


def out_cols_kernel(n, last, sc, a0, a1, a2, a3, w_ref, x_ref, gate_ref, *refs):
    u = sc[1]
    depth = a0.shape[1]
    tokens, width = x_ref.shape
    rows = tokens // n
    total = None
    for k, ref in enumerate((a0, a1, a2, a3)):
        at = pl.multiple_of(lax.rem(u - k + n, n) * depth, 128)
        part = jnp.dot(ref[...], w_ref[pl.ds(at, depth), :], preferred_element_type=F32)
        total = part if total is None else total + part
    gate = gate_ref[:, pl.ds(pl.multiple_of(u * width, 128), width)]
    y = (x_ref[...].astype(F32) + gate * total).astype(BF16)
    y_s = refs[-1]
    y_s[...] = y
    cut_into(refs[-n - 1 : -1], y_s, u, n, True)
    if not last:
        enter, next_refs = refs[0], refs[1:3]
        half = tokens // 2
        end = sc[0] == sc[3] - 1

        @pl.when(end)
        def _():
            for j in range(n):
                to = next_refs[j * rows // half]
                at = j * rows % half
                to[at : at + rows, :] = enter[:, j * width : (j + 1) * width]

        @pl.when(jnp.logical_not(end))
        def _():
            for h in range(2):
                next_refs[h][...] = y[h * half : (h + 1) * half]


def out_cols(n, pieces, weight, x, gate, enter=None):
    tokens, width = x.shape
    last = enter is None
    outs = [shaped((tokens // n, width))] * n
    return pl.pallas_call(
        located(out_cols_kernel, n, last),
        in_specs=[VMEM_SPEC] * (n + 3 + (not last)),
        out_specs=[VMEM_SPEC] * (n + 2 * (not last)),
        out_shape=outs if last else [shaped((tokens // 2, width))] * 2 + outs,
        scratch_shapes=[pltpu.VMEM(x.shape, BF16)],
        compiler_params=params(),
        cost_estimate=cost(2),
        name="out_cols",
    )(*pieces, weight, x, gate, *([] if last else [enter]))


def finish_kernel(n, sc, *refs):
    out_ref = refs[-1]
    width = refs[0].shape[1]
    for t in range(2):
        for k in range(n):
            at = pl.multiple_of(lax.rem(sc[1] + k, n) * width, 128)
            out_ref[0, t, :, pl.ds(at, width)] = refs[t * n + k][...]


def finish(n, parts):
    rows, width = parts[0].shape
    return pl.pallas_call(
        located(finish_kernel, n),
        in_specs=[VMEM_SPEC] * len(parts),
        out_specs=VMEM_SPEC,
        out_shape=shaped((1, 2, rows, n * width)),
        compiler_params=params(),
        cost_estimate=cost(1.5),
        name="finish",
    )(*parts)


def per_device(
    in_flight,
    entering,
    patch_ids,
    timestep,
    time_table,
    mod_weight,
    qkv_weight,
    out_weight,
    stale_cache,
):
    n = lax.axis_size("uly")

    x_pieces = [in_flight[0]] + [shift(in_flight[0], uly=k) for k in range(1, n)]
    stale_own = jnp.transpose(stale_cache[0], (1, 0, 2))
    stale_mate = shift(stale_own, blk=1)
    tile = modulate(timestep, time_table, jnp.transpose(mod_weight[0], (1, 2, 0)), [])
    tiles = jnp.stack([tile, shift(tile, blk=1)])
    tiles = join(tiles, shift(tiles, blk=2), [stale_mate])
    tiles = [tiles] + [shift(tiles, uly=k) for k in range(1, n)]

    weight = jnp.transpose(qkv_weight[0], (1, 0, 2))
    pair = lax.all_gather(
        out_weight[0], "blk", axis=0, tiled=True, axis_index_groups=[[0, 2], [1, 3]]
    )

    q, fresh, cols, vectors, gate = qkv_first(n, x_pieces, tiles, weight, [])

    q_other = shift(q, blk=2)
    rest = (fresh, shift(fresh, blk=1), stale_own, stale_mate)
    cut = cut_columns(n, [pair], [rest[1]])
    mine = [cut[0]] + [shift(cut[k], uly=k) for k in range(1, n)]
    mates = [shift(x, blk=1) for x in mine]
    (for_other,) = attend(True, patch_ids, q_other, *rest)
    stale_own = pass_on(stale_own, [for_other] + mine[1:])
    stale_all = lax.all_gather(stale_own, "blk", axis=0)
    o, level = attend(False, patch_ids, q, *rest[:2], stale_own, stale_mate)
    other = shift(for_other, blk=2)
    w_cols = place(n, mine, mates)
    attended = merge(o, level, other)
    a_pieces = [attended] + [shift(attended, uly=k) for k in range(1, n)]
    half_a, half_b, *parts = out_cols(n, a_pieces, w_cols, cols, gate, entering[0])
    half_a, half_b = shift(half_a, section=1), shift(half_b, section=1)
    parts = [parts[0]] + [shift(parts[k], uly=-k) for k in range(1, n)]
    half_b = pass_on(half_b, parts[1:])
    left_a, right_a = shift(half_a, uly=1), shift(half_a, uly=-1)
    left_b, right_b = shift(half_b, uly=1), shift(half_b, uly=-1)
    across_a, across_b = shift(left_a, uly=1), shift(right_b, uly=-1)
    y_pieces = [half_a, left_a, across_a, right_a, half_b, left_b, across_b, right_b]
    q, fresh, cols = qkv_next(n, y_pieces, vectors, weight)

    mate, far = shift(fresh, blk=1), shift(fresh, blk=2)
    o, level = attend_stale(patch_ids, q, fresh, mate, stale_all)
    far = pass_on(far, [level])
    far_mate = shift(far, blk=1)
    attended = attend_rest(q, far, far_mate, o, level)
    a_pieces = [attended] + [shift(attended, uly=k) for k in range(1, n)]
    last = out_cols(n, a_pieces, w_cols, cols, gate)
    last = [last[0]] + [shift(last[k], uly=-k) for k in range(1, n)]
    return finish(n, parts + last)


def solution(mesh):
    return jax.shard_map(
        per_device,
        mesh=mesh,
        in_specs=(
            P("section", ("uly", "blk"), None),
            P(None, ("uly", "blk"), None),
            P(),
            P(),
            P(),
            P("section", None, None, ("uly", "blk")),
            P("section", None, None, "uly"),
            P("section", ("uly", "blk"), None),
            P("section", "blk", None, "uly"),
        ),
        out_specs=P("section", None, ("uly", "blk"), None),
        check_vma=False,
    )
```

```python
import functools

import jax
import jax.numpy as jnp
from jax import lax
from jax.experimental import pallas as pl
from jax.experimental.pallas import tpu as pltpu
from jax.sharding import PartitionSpec as P

HD = 128
F32 = jnp.float32
BF16 = jnp.bfloat16
QKV_MIB = 48
ATTEND_MIB = 24
LOG2E = 1.4426950408889634
SMEM_SPEC = pl.BlockSpec(memory_space=pltpu.SMEM)
VMEM_SPEC = pl.BlockSpec(memory_space=pltpu.VMEM)
ANY_SPEC = pl.BlockSpec(memory_space=pl.ANY)


def shift(x, section=0, uly=0, blk=0):
    names = ("section", "uly", "blk")
    moves = (section, uly, blk)
    used = tuple(n for n, m in zip(names, moves) if m)
    sizes = [lax.axis_size(n) for n in used]
    total = 1
    for size in sizes:
        total *= size
    pairs = []
    for source in range(total):
        rest, place = source, []
        for size in reversed(sizes):
            place.insert(0, rest % size)
            rest //= size
        target = 0
        for name, size, at in zip(used, sizes, place):
            move = moves[names.index(name)]
            target = target * size + ((at ^ move) if name == "blk" else (at + move) % size)
        pairs.append((source, target))
    return lax.ppermute(x, used if len(used) > 1 else used[0], pairs)


def params(mib=24):
    return pltpu.CompilerParams(vmem_limit_bytes=mib * 1024 * 1024)


def cost(us):
    return pl.CostEstimate(flops=int(us * 1.1e9), transcendentals=0, bytes_accessed=1024)


def located(kernel, *static):
    def body(*refs):
        place = [lax.axis_index(name) for name in ("section", "uly", "blk")]
        return kernel(*static, place + [lax.axis_size("section")], *refs)

    return body


def start_all(pairs, sem, first=0):
    copies = [pltpu.make_async_copy(s, d, sem.at[first + i]) for i, (s, d) in enumerate(pairs)]
    for copy in copies:
        copy.start()
    return copies


def wait_all(copies):
    for copy in copies:
        copy.wait()


def modulate_kernel(held, step, table_ref, w_ref, *refs):
    out_ref, table, w, sem = refs[held:]
    copies = start_all([(table_ref, table), (w_ref, w)], sem)
    copies[0].wait()
    at = lax.broadcasted_iota(jnp.int32, table.shape, 0)
    v = jnp.sum(jnp.where(at == step[0], table[...], 0.0), axis=0, keepdims=True)
    activated = (v / (1.0 + jnp.exp(-v))).astype(BF16)
    wide = jnp.broadcast_to(activated, (8, v.shape[1]))
    count, cols = w.shape[:2]
    parts = []
    copies[1].wait()
    for i in range(count):
        part = lax.dot_general(
            wide, w[i], (((1,), (1,)), ((), ())), preferred_element_type=F32
        )[0:1]
        parts += [part[:, :HD], jnp.concatenate([part[:, HD:], part[:, : 2 * HD - cols]], axis=1)]
    parts += [jnp.zeros((8 - len(parts), HD), F32)]
    out_ref[...] = jnp.concatenate(parts, axis=0)


def modulate(timestep, time_table, mod_weight, hold):
    return pl.pallas_call(
        functools.partial(modulate_kernel, len(hold)),
        in_specs=[SMEM_SPEC] + [ANY_SPEC] * (2 + len(hold)),
        out_specs=VMEM_SPEC,
        out_shape=shaped((8, HD), F32),
        scratch_shapes=[
            pltpu.VMEM(time_table.shape, F32),
            pltpu.VMEM(mod_weight.shape, BF16),
            pltpu.SemaphoreType.DMA((2,)),
        ],
        compiler_params=params(QKV_MIB),
        cost_estimate=cost(0.1),
        name="modulate",
    )(timestep, time_table, mod_weight, *hold)


def join_kernel(x_ref, y_ref, *refs):
    count = x_ref.shape[0]
    refs[-1][:count] = x_ref[...]
    refs[-1][count:] = y_ref[...]


def join(x, y, hold):
    return pl.pallas_call(
        join_kernel,
        in_specs=[VMEM_SPEC] * 2 + [ANY_SPEC] * len(hold),
        out_specs=VMEM_SPEC,
        out_shape=shaped((2 * x.shape[0],) + x.shape[1:], x.dtype),
        compiler_params=params(),
        cost_estimate=cost(0.1),
        name="join",
    )(x, y, *hold)


def norm_rows(x, shift_vec, scale_vec):
    center = x - jnp.mean(x, axis=-1, keepdims=True)
    normed = center * lax.rsqrt(jnp.mean(center * center, axis=-1, keepdims=True) + 1e-06)
    return (normed * (1.0 + scale_vec) + shift_vec).astype(BF16)


def norm_heads(part, heads):
    out = []
    for h in range(heads):
        v = part[:, h * HD : (h + 1) * HD]
        out.append(v * lax.rsqrt(jnp.mean(v * v, axis=-1, keepdims=True) + 1e-06))
    return jnp.concatenate(out, axis=1).astype(BF16)


def project(mod_s, w_s, w_copies, q_ref, kv_ref):
    for g in range(3):
        w_copies[g].wait()
        part = jnp.dot(mod_s[...], w_s[g], preferred_element_type=F32)
        heads = part.shape[1] // HD
        if g == 0:
            q_ref[...] = norm_heads(part, heads)
        elif g == 1:
            kv_ref[0] = norm_heads(part, heads)
        else:
            kv_ref[1] = part.astype(BF16)


def qkv_first_kernel(
    n, held, sc, x0, x1, x2, x3, m0, m1, m2, m3, w_ref, *refs
):
    q_ref, kv_ref, cols_ref, vectors_ref, gate_ref, *scratch = refs[held:]
    x_s, mod_s, w_s, tiles, sem = scratch
    u, b = sc[1], sc[2]
    rows = x0.shape[0]
    width = cols_ref.shape[1]
    blocks = m0.shape[0]
    inner = x0.shape[1] // (n * blocks) - HD
    at = [lax.rem(u - k + n, n) for k in range(n)]
    spots = [pl.ds(pl.multiple_of(i * rows, rows), rows) for i in at]
    x_copies = start_all([(r, x_s.at[i]) for r, i in zip((x0, x1, x2, x3), spots)], sem)
    w_copies = start_all([(w_ref.at[g], w_s.at[g]) for g in range(3)], sem, n)
    for i, ref in zip(at, (m0, m1, m2, m3)):
        for j in range(blocks):
            tiles[i * blocks + jnp.bitwise_xor(b, j)] = ref[j]
    for i, ref in enumerate((vectors_ref.at[0:1], vectors_ref.at[1:2], gate_ref)):
        pieces = []
        for j in range(n * blocks):
            pieces += [tiles[j, 2 * i : 2 * i + 1, :], tiles[j, 2 * i + 1 : 2 * i + 2, :inner]]
        ref[...] = jnp.concatenate(pieces, axis=1)
    for copy, i in zip(x_copies, spots):
        copy.wait()
        mod_s[i, :] = norm_rows(x_s[i, :].astype(F32), vectors_ref[0:1, :], vectors_ref[1:2, :])
    cols_ref[...] = x_s[:, pl.ds(pl.multiple_of(u * width, 128), width)]
    project(mod_s, w_s, w_copies, q_ref, kv_ref)


def qkv_next_kernel(n, sc, *refs):
    pieces, refs = refs[: 2 * n], refs[2 * n :]
    vectors, w_ref, q_ref, kv_ref, cols_ref, x_s, mod_s, w_s, sem = refs
    u = sc[1]
    first = sc[0] == 0
    half, width = pieces[0].shape
    rows = x_s.shape[0] // n
    per = half // rows
    by_cols, by_rows = [], []
    for h in range(2):
        for k in range(n):
            ref = pieces[h * n + k]
            i = lax.rem(u - k + n, n)
            at = pl.ds(pl.multiple_of(i * width, 128), width)
            by_cols.append((ref, x_s.at[h * half : (h + 1) * half, at]))
            at = pl.ds(pl.multiple_of(i * rows, rows), rows)
            for j in range(per):
                to = slice((h * per + j) * width, (h * per + j + 1) * width)
                by_rows.append((ref.at[j * rows : (j + 1) * rows, :], x_s.at[at, to]))
    by_cols = [pltpu.make_async_copy(s, d, sem.at[i]) for i, (s, d) in enumerate(by_cols)]
    by_rows = [pltpu.make_async_copy(s, d, sem.at[2 * n + i]) for i, (s, d) in enumerate(by_rows)]

    @pl.when(first)
    def _():
        for copy in by_rows:
            copy.start()

    @pl.when(jnp.logical_not(first))
    def _():
        for copy in by_cols:
            copy.start()

    w_copies = start_all([(w_ref.at[g], w_s.at[g]) for g in range(3)], sem, 2 * n + n * n)

    @pl.when(first)
    def _():
        wait_all(by_rows)

    @pl.when(jnp.logical_not(first))
    def _():
        wait_all(by_cols)

    for r in range(n):
        at = slice(r * rows, (r + 1) * rows)
        mod_s[at, :] = norm_rows(x_s[at, :].astype(F32), vectors[0:1, :], vectors[1:2, :])
    cols_ref[...] = x_s[:, pl.ds(pl.multiple_of(u * width, 128), width)]
    project(mod_s, w_s, w_copies, q_ref, kv_ref)


def shaped(shape, dtype=BF16):
    return jax.ShapeDtypeStruct(shape, dtype)


def qkv_scratch(tokens, weight, sems):
    width = weight.shape[1]
    return [
        pltpu.VMEM((tokens, width), BF16),
        pltpu.VMEM((tokens, width), BF16),
        pltpu.VMEM(weight.shape, BF16),
        pltpu.SemaphoreType.DMA((sems,)),
    ]


def qkv_first(n, pieces, tiles, weight, hold):
    rows, width = pieces[0].shape
    cols = weight.shape[2]
    tokens = n * rows
    blocks = tiles[0].shape[0]
    scratch = qkv_scratch(tokens, weight, n + 3)
    return pl.pallas_call(
        located(qkv_first_kernel, n, len(hold)),
        in_specs=[ANY_SPEC] * n + [VMEM_SPEC] * n + [ANY_SPEC] * (1 + len(hold)),
        out_specs=[VMEM_SPEC] * 5,
        out_shape=[
            shaped((tokens, cols)),
            shaped((2, tokens, cols)),
            shaped((tokens, width // n)),
            shaped((2, width), F32),
            shaped((1, width), F32),
        ],
        scratch_shapes=scratch[:3] + [pltpu.VMEM((n * blocks, 8, HD), F32)] + scratch[3:],
        compiler_params=params(QKV_MIB),
        cost_estimate=cost(0.1),
        name="qkv_first",
    )(*pieces, *tiles, weight, *hold)


def qkv_next(n, pieces, vectors, weight):
    half, part = pieces[0].shape
    tokens = 2 * half
    cols = weight.shape[2]
    return pl.pallas_call(
        located(qkv_next_kernel, n),
        in_specs=[ANY_SPEC] * (2 * n) + [VMEM_SPEC, ANY_SPEC],
        out_specs=[VMEM_SPEC] * 3,
        out_shape=[shaped((tokens, cols)), shaped((2, tokens, cols)), shaped((tokens, part))],
        scratch_shapes=qkv_scratch(tokens, weight, 2 * n + n * n + 3),
        compiler_params=params(QKV_MIB),
        cost_estimate=cost(6),
        name="qkv_next",
    )(*pieces, vectors, weight)


def cut_into(refs, whole, u, n, by_rows):
    for k, ref in enumerate(refs):
        rows, part = ref.shape
        if by_rows:
            at = pl.ds(pl.multiple_of(lax.rem(u - k + n, n) * rows, rows), rows)
            ref[...] = whole[at, :]
        else:
            at = pl.ds(pl.multiple_of(lax.rem(u + k, n) * part, 128), part)
            ref[...] = whole[:, at]


def cut_kernel(n, count, sc, *refs):
    wholes, outs = refs[:count], refs[-n * count :]
    for c in range(count):
        cut_into(outs[c * n : (c + 1) * n], wholes[c], sc[1], n, False)


def cut_columns(n, wholes, hold):
    outs = []
    for x in wholes:
        outs += [shaped((x.shape[0], x.shape[1] // n))] * n
    return pl.pallas_call(
        located(cut_kernel, n, len(wholes)),
        in_specs=[VMEM_SPEC] * len(wholes) + [ANY_SPEC] * len(hold),
        out_specs=[VMEM_SPEC] * len(outs),
        out_shape=outs,
        compiler_params=params(),
        cost_estimate=cost(1),
        name="cut_columns",
    )(*wholes, *hold)


NT = (((1,), (1,)), ((), ()))
RATE = HD ** (-0.5) * LOG2E


def weigh(q, pieces):
    scores = []
    for keys, _, masked in pieces:
        score = lax.dot_general(q, keys, NT, preferred_element_type=F32)
        scores.append(score if masked is None else jnp.where(masked, -1e30, score))
    peak = functools.reduce(jnp.maximum, [jnp.max(s, axis=-1, keepdims=True) for s in scores])
    total = jnp.zeros(peak.shape, F32)
    numer = jnp.zeros(q.shape, F32)
    for s, (_, values, _) in zip(scores, pieces):
        weights = jnp.exp2((s - peak) * RATE)
        total = total + jnp.sum(weights, axis=-1, keepdims=True)
        numer = numer + jnp.dot(weights.astype(BF16), values, preferred_element_type=F32)
    return peak, total, numer


def store_part(refs, h, peak, total, numer, stats):
    at = slice(h * HD, (h + 1) * HD)
    lane = lax.broadcasted_iota(jnp.int32, stats.shape, 1)
    level = peak * RATE + jnp.log2(total)
    if len(refs) == 2:
        refs[0][:, at] = numer / total
        return jnp.where(lane == h, level, stats)
    refs[0][:, at] = (numer / total).astype(BF16)
    high = level.astype(BF16).astype(F32)
    middle = (level - high).astype(BF16).astype(F32)
    for j, piece in enumerate((high, middle, level - high - middle)):
        stats = jnp.where(lane == 3 * h + j, piece, stats)
    return stats


def attend_kernel(packed, held, sc, patch, q_ref, fo, fm, so, sm, *refs):
    outs = refs[held:]
    b, p = sc[2], patch[sc[3] - 1 - sc[0]]
    heads = q_ref.shape[1] // HD
    stats = jnp.zeros((q_ref.shape[0], HD), F32)
    for h in range(heads):
        at = slice(h * HD, (h + 1) * HD)
        pieces = [(ref[0, :, at], ref[1, :, at], None) for ref in (fo, fm)]
        pieces += [
            (ref[0, :, at], ref[1, :, at], p == jnp.bitwise_xor(b, j))
            for j, ref in enumerate((so, sm))
        ]
        stats = store_part(outs, h, *weigh(q_ref[:, at], pieces), stats)
    if packed:
        outs[0][:, heads * HD :] = stats.astype(BF16)
    else:
        outs[1][...] = stats


def attend(packed, patch, q, fo, fm, so, sm, hold=()):
    rows, cols = q.shape
    if packed:
        out_shape = [shaped((rows, cols + HD))]
    else:
        out_shape = [shaped((rows, cols), F32), shaped((rows, HD), F32)]
    return pl.pallas_call(
        located(attend_kernel, packed, len(hold)),
        in_specs=[SMEM_SPEC] + [VMEM_SPEC] * 5 + [ANY_SPEC] * len(hold),
        out_specs=[VMEM_SPEC] * len(out_shape),
        out_shape=out_shape,
        compiler_params=params(ATTEND_MIB),
        cost_estimate=cost(5),
        name="attend_other" if packed else "attend_own",
    )(patch, q, fo, fm, so, sm, *hold)


def attend_stale_kernel(sc, patch, q_ref, fo, fm, stale, o_ref, level_ref, stale_s, sem):
    count = stale.shape[0]
    live = [lax.rem(patch[sc[3] - sc[0]] + 1 + i, count) for i in range(count - 1)]
    copies = start_all([(stale.at[j], stale_s.at[i]) for i, j in enumerate(live)], sem)
    wait_all(copies)
    stats = jnp.zeros(level_ref.shape, F32)
    for h in range(q_ref.shape[1] // HD):
        at = slice(h * HD, (h + 1) * HD)
        pieces = [(ref[0, :, at], ref[1, :, at], None) for ref in (fo, fm)]
        pieces += [(stale_s[i, 0, :, at], stale_s[i, 1, :, at], None) for i in range(count - 1)]
        stats = store_part((o_ref, level_ref), h, *weigh(q_ref[:, at], pieces), stats)
    level_ref[...] = stats


def attend_stale(patch, q, fo, fm, stale):
    rows, cols = q.shape
    return pl.pallas_call(
        located(attend_stale_kernel),
        in_specs=[SMEM_SPEC] + [VMEM_SPEC] * 3 + [ANY_SPEC],
        out_specs=[VMEM_SPEC] * 2,
        out_shape=[shaped((rows, cols), F32), shaped((rows, HD), F32)],
        scratch_shapes=[
            pltpu.VMEM((stale.shape[0] - 1,) + stale.shape[1:], BF16),
            pltpu.SemaphoreType.DMA((stale.shape[0] - 1,)),
        ],
        compiler_params=params(ATTEND_MIB),
        cost_estimate=cost(8),
        name="attend_stale",
    )(patch, q, fo, fm, stale)


def attend_rest_kernel(q_ref, fo, fm, o_ref, level_ref, out_ref):
    for h in range(q_ref.shape[1] // HD):
        at = slice(h * HD, (h + 1) * HD)
        pieces = [(ref[0, :, at], ref[1, :, at], None) for ref in (fo, fm)]
        peak, total, numer = weigh(q_ref[:, at], pieces)
        peak = peak * RATE
        level = level_ref[:, h : h + 1]
        top = jnp.maximum(level, peak)
        a, b = jnp.exp2(level - top), jnp.exp2(peak - top)
        out_ref[:, at] = ((a * o_ref[:, at] + b * numer) / (a + b * total)).astype(BF16)


def attend_rest(q, fo, fm, o, level):
    return pl.pallas_call(
        attend_rest_kernel,
        in_specs=[VMEM_SPEC] * 5,
        out_specs=VMEM_SPEC,
        out_shape=shaped(q.shape),
        compiler_params=params(ATTEND_MIB),
        cost_estimate=cost(3),
        name="attend_rest",
    )(q, fo, fm, o, level)


def merge_kernel(o_ref, level_ref, other_ref, *refs):
    out_ref = refs[-1]
    cols = o_ref.shape[1]
    for h in range(cols // HD):
        at = slice(h * HD, (h + 1) * HD)
        mine = level_ref[:, h : h + 1]
        parts = [
            other_ref[:, cols + 3 * h + j : cols + 3 * h + j + 1].astype(F32) for j in range(3)
        ]
        theirs = parts[0] + parts[1] + parts[2]
        peak = jnp.maximum(mine, theirs)
        a, b = jnp.exp2(mine - peak), jnp.exp2(theirs - peak)
        mixed = (a * o_ref[:, at] + b * other_ref[:, at].astype(F32)) / (a + b)
        out_ref[:, at] = mixed.astype(BF16)


def merge(o, level, other, hold=()):
    return pl.pallas_call(
        merge_kernel,
        in_specs=[VMEM_SPEC] * 3 + [ANY_SPEC] * len(hold),
        out_specs=VMEM_SPEC,
        out_shape=jax.ShapeDtypeStruct(o.shape, BF16),
        compiler_params=params(),
        cost_estimate=cost(12),
        name="merge",
    )(o, level, other, *hold)


def place_kernel(n, sc, *refs):
    u, core = sc[1], lax.rem(sc[2], 2)
    mine, mate, out_ref = refs[:n], refs[n : 2 * n], refs[2 * n]
    rows = mine[0].shape[0] // 2
    for k in range(n):
        for ref, flip in ((mine[k], 0), (mate[k], 1)):
            for z in range(2):
                at = lax.rem(u - k + n, n) * 4 + 2 * z + jnp.bitwise_xor(core, flip)
                at = pl.multiple_of(at * rows, rows)
                out_ref[pl.ds(at, rows), :] = ref[z * rows : (z + 1) * rows, :]


def place(n, mine, mate):
    rows, cols = mine[0].shape
    return pl.pallas_call(
        located(place_kernel, n),
        in_specs=[VMEM_SPEC] * (2 * n),
        out_specs=VMEM_SPEC,
        out_shape=shaped((2 * n * rows, cols)),
        compiler_params=params(),
        cost_estimate=cost(0.1),
        name="place",
    )(*mine, *mate)


def pass_on(x, hold):
    return pl.pallas_call(
        lambda *refs: None,
        in_specs=[ANY_SPEC] * (1 + len(hold)),
        out_specs=ANY_SPEC,
        out_shape=shaped(x.shape, x.dtype),
        input_output_aliases={0: 0},
        compiler_params=params(),
        cost_estimate=cost(0.1),
        name="pass_on",
    )(x, *hold)


def out_cols_kernel(n, last, sc, a0, a1, a2, a3, w_ref, x_ref, gate_ref, *refs):
    u = sc[1]
    depth = a0.shape[1]
    tokens, width = x_ref.shape
    rows = tokens // n
    total = None
    for k, ref in enumerate((a0, a1, a2, a3)):
        at = pl.multiple_of(lax.rem(u - k + n, n) * depth, 128)
        part = jnp.dot(ref[...], w_ref[pl.ds(at, depth), :], preferred_element_type=F32)
        total = part if total is None else total + part
    gate = gate_ref[:, pl.ds(pl.multiple_of(u * width, 128), width)]
    y = (x_ref[...].astype(F32) + gate * total).astype(BF16)
    y_s = refs[-1]
    y_s[...] = y
    cut_into(refs[-n - 1 : -1], y_s, u, n, True)
    if not last:
        enter, next_refs = refs[0], refs[1:3]
        half = tokens // 2
        end = sc[0] == sc[3] - 1

        @pl.when(end)
        def _():
            for j in range(n):
                to = next_refs[j * rows // half]
                at = j * rows % half
                to[at : at + rows, :] = enter[:, j * width : (j + 1) * width]

        @pl.when(jnp.logical_not(end))
        def _():
            for h in range(2):
                next_refs[h][...] = y[h * half : (h + 1) * half]


def out_cols(n, pieces, weight, x, gate, enter=None):
    tokens, width = x.shape
    last = enter is None
    outs = [shaped((tokens // n, width))] * n
    return pl.pallas_call(
        located(out_cols_kernel, n, last),
        in_specs=[VMEM_SPEC] * (n + 3 + (not last)),
        out_specs=[VMEM_SPEC] * (n + 2 * (not last)),
        out_shape=outs if last else [shaped((tokens // 2, width))] * 2 + outs,
        scratch_shapes=[pltpu.VMEM(x.shape, BF16)],
        compiler_params=params(),
        cost_estimate=cost(2),
        name="out_cols",
    )(*pieces, weight, x, gate, *([] if last else [enter]))


def finish_kernel(n, sc, *refs):
    out_ref = refs[-1]
    width = refs[0].shape[1]
    for t in range(2):
        for k in range(n):
            at = pl.multiple_of(lax.rem(sc[1] + k, n) * width, 128)
            out_ref[0, t, :, pl.ds(at, width)] = refs[t * n + k][...]


def finish(n, parts):
    rows, width = parts[0].shape
    return pl.pallas_call(
        located(finish_kernel, n),
        in_specs=[VMEM_SPEC] * len(parts),
        out_specs=VMEM_SPEC,
        out_shape=shaped((1, 2, rows, n * width)),
        compiler_params=params(),
        cost_estimate=cost(1.5),
        name="finish",
    )(*parts)


def per_device(
    in_flight,
    entering,
    patch_ids,
    timestep,
    time_table,
    mod_weight,
    qkv_weight,
    out_weight,
    stale_cache,
):
    n = lax.axis_size("uly")

    x_pieces = [in_flight[0]] + [shift(in_flight[0], uly=k) for k in range(1, n)]
    stale_own = jnp.transpose(stale_cache[0], (1, 0, 2))
    stale_mate = shift(stale_own, blk=1)
    tile = modulate(timestep, time_table, jnp.transpose(mod_weight[0], (1, 2, 0)), [])
    tiles = jnp.stack([tile, shift(tile, blk=1)])
    tiles = join(tiles, shift(tiles, blk=2), [stale_mate])
    tiles = [tiles] + [shift(tiles, uly=k) for k in range(1, n)]

    weight = jnp.transpose(qkv_weight[0], (1, 0, 2))
    pair = lax.all_gather(
        out_weight[0], "blk", axis=0, tiled=True, axis_index_groups=[[0, 2], [1, 3]]
    )

    q, fresh, cols, vectors, gate = qkv_first(n, x_pieces, tiles, weight, [])

    q_other = shift(q, blk=2)
    rest = (fresh, shift(fresh, blk=1), stale_own, stale_mate)
    cut = cut_columns(n, [pair], [rest[1]])
    mine = [cut[0]] + [shift(cut[k], uly=k) for k in range(1, n)]
    mates = [shift(x, blk=1) for x in mine]
    (for_other,) = attend(True, patch_ids, q_other, *rest)
    stale_own = pass_on(stale_own, [for_other, mine[1], mine[3]])
    stale_all = lax.all_gather(stale_own, "blk", axis=0)
    o, level = attend(False, patch_ids, q, *rest[:2], stale_own, stale_mate)
    other = shift(for_other, blk=2)
    w_cols = place(n, mine, mates)
    attended = merge(o, level, other)
    a_pieces = [attended] + [shift(attended, uly=k) for k in range(1, n)]
    half_a, half_b, *parts = out_cols(n, a_pieces, w_cols, cols, gate, entering[0])
    half_a, half_b = shift(half_a, section=1), shift(half_b, section=1)
    parts = [parts[0]] + [shift(parts[k], uly=-k) for k in range(1, n)]
    half_b = pass_on(half_b, parts[1:])
    left_a, right_a = shift(half_a, uly=1), shift(half_a, uly=-1)
    left_b, right_b = shift(half_b, uly=1), shift(half_b, uly=-1)
    across_a, across_b = shift(left_a, uly=1), shift(right_b, uly=-1)
    y_pieces = [half_a, left_a, across_a, right_a, half_b, left_b, across_b, right_b]
    q, fresh, cols = qkv_next(n, y_pieces, vectors, weight)

    mate, far = shift(fresh, blk=1), shift(fresh, blk=2)
    o, level = attend_stale(patch_ids, q, fresh, mate, stale_all)
    far = pass_on(far, [level])
    far_mate = shift(far, blk=1)
    attended = attend_rest(q, far, far_mate, o, level)
    a_pieces = [attended] + [shift(attended, uly=k) for k in range(1, n)]
    last = out_cols(n, a_pieces, w_cols, cols, gate)
    last = [last[0]] + [shift(last[k], uly=-k) for k in range(1, n)]
    return finish(n, parts + last)


def solution(mesh):
    return jax.shard_map(
        per_device,
        mesh=mesh,
        in_specs=(
            P("section", ("uly", "blk"), None),
            P(None, ("uly", "blk"), None),
            P(),
            P(),
            P(),
            P("section", None, None, ("uly", "blk")),
            P("section", None, None, "uly"),
            P("section", ("uly", "blk"), None),
            P("section", "blk", None, "uly"),
        ),
        out_specs=P("section", None, ("uly", "blk"), None),
        check_vma=False,
    )
```
